32 devices in a mesh: row: 4 (over y, x), lat: 8 (over z, core).
Axes of the slice: x: 2, y: 2, z: 4, core: 2. Of those that a mesh axis runs over, the one named last changes fastest.
Arguments:
- tokens: bfloat16 [4, 2048, 512], P('row', 'lat'), may hold values from -6 to 6
- latents: bfloat16 [4, 8192, 512], P('row', 'lat'), may hold values from -6 to 6
- segment_ids: int32 [4, 2048], P('row', 'lat'), may hold values from 0 to 3, as said below
- pad_mask: int32 [4, 2048], P('row', 'lat'), may hold values from 0 to 1, as said below
- block_scene: int32 [4, 4], P('row'), may hold values from 0 to 3, each once within a row
- out_grad: bfloat16 [4, 8192, 512], P('row', 'lat'), may hold values from -6 to 6
- gain_cross_q: bfloat16 [512], P('lat'), may hold values from 0.099609375 to 1.8984375
- gain_cross_kv: bfloat16 [512], P('lat'), may hold values from 0.099609375 to 1.8984375
- w_cross_q: bfloat16 [512, 512], P('lat'), may hold values from -0.5 to 0.5
- w_cross_kv: bfloat16 [512, 1024], P('lat'), may hold values from -0.25 to 0.25
- w_cross_out: bfloat16 [512, 512], P('lat'), may hold values from -1.5 to 1.5
- gain_mlp1: bfloat16 [512], P('lat'), may hold values from 0.099609375 to 1.8984375
- w_up1: bfloat16 [512, 2048], P('lat'), may hold values from -0.25 to 0.25
- w_down1: bfloat16 [2048, 512], P('lat'), may hold values from -0.1875 to 0.1875
- gain_self: bfloat16 [512], P('lat'), may hold values from 0.099609375 to 1.8984375
- w_self_qkv: bfloat16 [512, 1536], P('lat'), may hold values from -0.375 to 0.375
- w_self_out: bfloat16 [512, 512], P('lat'), may hold values from -1 to 1
- gain_mlp2: bfloat16 [512], P('lat'), may hold values from 0.099609375 to 1.8984375
- w_up2: bfloat16 [512, 2048], P('lat'), may hold values from -0.25 to 0.25
- w_down2: bfloat16 [2048, 512], P('lat'), may hold values from -0.1875 to 0.1875
Outputs:
- out: float32 [4, 8192, 512], P('row', 'lat')
- latent_grad: float32 [4, 8192, 512], P('row', 'lat')
- token_grad: float32 [4, 2048, 512], P('row', 'lat')
- grad_gain_cross_q: float32 [512], P('lat')
- grad_gain_cross_kv: float32 [512], P('lat')
- grad_w_cross_q: float32 [512, 512], P('lat')
- grad_w_cross_kv: float32 [512, 1024], P('lat')
- grad_w_cross_out: float32 [512, 512], P('lat')
- grad_gain_mlp1: float32 [512], P('lat')
- grad_w_up1: float32 [512, 2048], P('lat')
- grad_w_down1: float32 [2048, 512], P('lat')
- grad_gain_self: float32 [512], P('lat')
- grad_w_self_qkv: float32 [512, 1536], P('lat')
- grad_w_self_out: float32 [512, 512], P('lat')
- grad_gain_mlp2: float32 [512], P('lat')
- grad_w_up2: float32 [512, 2048], P('lat')
- grad_w_down2: float32 [2048, 512], P('lat')
The draws below stay inside these ranges and needn't reach their ends.
Inputs may be any that keep to these rules, and one draw needn't show every extreme that they name: `segment_ids`: each row packs scenes 0 to 3 in order, each in consecutive slots; a scene holds between 256 and 480 slots, and scene 0 exactly the latter; slots after the last scene are padding and carry any scene number. `pad_mask`: 1 exactly on the slots of the scenes, 0 on the padding after them. In each row a permutation of the scenes: latent block b belongs to scene block_scene[row, b].
All inputs are finite; a program needn't handle non-finite values.
Results may differ from the reference program's by a relative error of at most 0.028.
Values may be sent and summed in bfloat16 or wider, within the bound.
A program may use at most 384 MiB of HBM per device.

```python
import jax
import jax.numpy as jnp
from jax import lax

D = 512
FF = 2048
HEADS = 8
LAT_SCENE = 2048
SCENES = 4
ROWS = 4
SLOTS = 2048
LATENTS = 8192
SPAN = 512


def scene_layout(key):
    lengths = jax.random.randint(jax.random.fold_in(key, 11), (ROWS, SCENES), SPAN // 2, SPAN - SPAN // 16 + 1)
    first = jnp.arange(SCENES) == 0
    lengths = jnp.where(first[None, :], SPAN - SPAN // 16, lengths).astype(jnp.int32)
    ends = jnp.cumsum(lengths, axis=1)
    position = jnp.arange(SLOTS, dtype=jnp.int32)
    scene = jnp.sum((position[None, None, :] >= ends[:, :, None]).astype(jnp.int32), axis=1)
    filled = position[None, :] < ends[:, -1:]
    return (scene, filled)


def draw_segment_ids(key, part):
    scene, filled = scene_layout(key)
    key = jax.random.fold_in(key, 3)
    filler = jax.random.randint(key, (ROWS, SLOTS), 0, SCENES)
    return jnp.where(filled, scene, filler).astype(jnp.int32)


def draw_pad_mask(key, part):
    scene, filled = scene_layout(key)
    return filled.astype(jnp.int32)


def shard_levels(own_key, extent, shards, smallest, top_value):
    level = 1.0
    for dim, blocks in shards:
        heights = jax.random.uniform(jax.random.fold_in(jax.random.fold_in(own_key, 6), dim), (blocks,), jnp.float32, smallest / len(shards), top_value / len(shards))
        level = level * jnp.repeat(jnp.exp(heights), extent[dim] // blocks).reshape((-1,) + (1,) * (len(extent) - 1 - dim))
    return level


def centred(rng, shape, width, most, cuts=(), held_as=jnp.bfloat16):
    loudness = shard_levels(rng, shape, cuts, -0.22, 0.18) if cuts else 1.0
    array = jax.random.normal(rng, shape, jnp.float32) * width * loudness
    return jnp.minimum(jnp.maximum(array, -most), most).astype(held_as)


def setup_inputs(seed: int = 0) -> dict:
    seeds = jax.random.split(jax.random.key(seed), 21)
    return {
        "tokens": centred(seeds[0], (ROWS, SLOTS, D), 1.0, 6.0, ((0, 4), (1, 8))),
        "latents": centred(seeds[1], (ROWS, LATENTS, D), 1.0, 6.0, ((0, 4), (1, 8))),
        "segment_ids": draw_segment_ids(jax.random.fold_in(seeds[20], 71), 0),
        "pad_mask": draw_pad_mask(jax.random.fold_in(seeds[20], 71), 0),
        "block_scene": jax.vmap(lambda own: jax.random.permutation(own, SCENES))(jax.random.split(seeds[4], ROWS)).reshape((ROWS, SCENES)).astype(jnp.int32),
        "out_grad": centred(seeds[5], (ROWS, LATENTS, D), 1.0, 6.0, ((0, 4), (1, 8))),
        "gain_cross_q": jnp.clip(1.0 + 0.18 * jax.random.normal(seeds[6], (D,), jnp.float32), 0.099609375, 1.8984375).astype(jnp.bfloat16),
        "gain_cross_kv": jnp.clip(1.0 + 0.18 * jax.random.normal(seeds[7], (D,), jnp.float32), 0.099609375, 1.8984375).astype(jnp.bfloat16),
        "w_cross_q": centred(seeds[8], (D, D), (D // 4) ** -0.5, 0.5, ((0, 8),)),
        "w_cross_kv": centred(seeds[9], (D, 2 * D), D ** -0.5, 0.25, ((0, 8),)),
        "w_cross_out": centred(seeds[10], (D, D), (D // 32) ** -0.5, 1.5, ((0, 8),)),
        "gain_mlp1": jnp.clip(1.0 + 0.18 * jax.random.normal(seeds[11], (D,), jnp.float32), 0.099609375, 1.8984375).astype(jnp.bfloat16),
        "w_up1": centred(seeds[12], (D, FF), D ** -0.5, 0.25, ((0, 8),)),
        "w_down1": centred(seeds[13], (FF, D), (FF // 2) ** -0.5, 0.1875, ((0, 8),)),
        "gain_self": jnp.clip(1.0 + 0.18 * jax.random.normal(seeds[14], (D,), jnp.float32), 0.099609375, 1.8984375).astype(jnp.bfloat16),
        "w_self_qkv": centred(seeds[15], (D, 3 * D), (D // 2) ** -0.5, 0.375, ((0, 8),)),
        "w_self_out": centred(seeds[16], (D, D), (D // 16) ** -0.5, 1.0, ((0, 8),)),
        "gain_mlp2": jnp.clip(1.0 + 0.18 * jax.random.normal(seeds[17], (D,), jnp.float32), 0.099609375, 1.8984375).astype(jnp.bfloat16),
        "w_up2": centred(seeds[18], (D, FF), D ** -0.5, 0.25, ((0, 8),)),
        "w_down2": centred(seeds[19], (FF, D), (FF // 2) ** -0.5, 0.1875, ((0, 8),)),
    }


EPS = 1e-05
NEG = -1e+30

@jax.custom_vjp
def low(v):
    return lax.optimization_barrier(v.astype(jnp.bfloat16)).astype(jnp.float32)

@jax.custom_vjp
def low_back(v):
    return v

def low_keep(v):
    return (low(v), None)

def low_pass(kept, grad):
    return (grad,)

def back_keep(v):
    return (v, None)

def back_low(kept, grad):
    return (low(grad),)
low.defvjp(low_keep, low_pass)
low_back.defvjp(back_keep, back_low)

def low_both(value):
    return low_back(low(value))

def matmul(left, right):
    return jnp.dot(left, right, precision=lax.Precision.HIGHEST)

def layer_norm(value, gain):
    centered = value - lax.optimization_barrier(jnp.mean(value, axis=-1, keepdims=True))
    return centered * lax.rsqrt(lax.optimization_barrier(jnp.mean(centered * centered, axis=-1, keepdims=True)) + EPS) * gain

def gelu(value):
    return jax.nn.gelu(value, approximate=True)

def feed_forward(state, gain, w_up, w_down):
    upper = low_back(matmul(low(layer_norm(state, gain)), w_up))
    return state + low_back(matmul(low(gelu(upper)), w_down))

def layer_forward(params, latent_rows, token_rows, segment_ids, pad_mask, block_scene):
    g_q, g_kv, w_q, w_kv, w_out, g_m1, w_up1, w_down1, g_s, w_qkv, w_so, g_m2, w_up2, w_down2 = params
    cross_scale = D ** (-0.5)
    head_size = D // HEADS
    self_scale = head_size ** (-0.5)

    def one_row(row):
        state, token_state, seg_row, pad_row, table = row
        tag = jnp.where(pad_row == 1, seg_row, -1)
        query = low_both(matmul(low(layer_norm(state, g_q)), w_q))
        keyval = low_both(matmul(low(layer_norm(token_state, g_kv)), w_kv))
        keys = keyval[:, :D]
        values = keyval[:, D:]

        def cross_block(item):
            block_query, scene = item
            scores = low_back(matmul(block_query, keys.T) * cross_scale)
            scores = jnp.where((tag == scene)[None, :], scores, NEG)
            probs = low(jax.nn.softmax(scores, axis=-1))
            return low_both(matmul(probs, values))
        attended = lax.map(jax.checkpoint(cross_block), (query.reshape(SCENES, LAT_SCENE, D), table))
        attended = attended.reshape(LATENTS, D)
        state1 = state + low_back(matmul(attended, w_out))
        state2 = feed_forward(state1, g_m1, w_up1, w_down1)
        packed = low_both(matmul(low(layer_norm(state2, g_s)), w_qkv))
        packed = packed.reshape(SCENES, LAT_SCENE, 3, HEADS, head_size)

        def self_block(block):
            scores = jnp.einsum('qhd,khd->hqk', block[:, 0], block[:, 1], precision=lax.Precision.HIGHEST)
            scores = low_back(scores * self_scale)
            probs = low(jax.nn.softmax(scores, axis=-1))
            mixed = jnp.einsum('hqk,khd->qhd', probs, block[:, 2], precision=lax.Precision.HIGHEST)
            return low_both(mixed).reshape(LAT_SCENE, D)
        attended2 = lax.map(jax.checkpoint(self_block), packed).reshape(LATENTS, D)
        state3 = state2 + low_back(matmul(attended2, w_so))
        return feed_forward(state3, g_m2, w_up2, w_down2)
    return lax.map(jax.checkpoint(one_row), (latent_rows, token_rows, segment_ids, pad_mask, block_scene))

def reference(tokens, latents, segment_ids, pad_mask, block_scene, out_grad, gain_cross_q, gain_cross_kv, w_cross_q, w_cross_kv, w_cross_out, gain_mlp1, w_up1, w_down1, gain_self, w_self_qkv, w_self_out, gain_mlp2, w_up2, w_down2):
    params = (gain_cross_q.astype(jnp.float32), gain_cross_kv.astype(jnp.float32), w_cross_q.astype(jnp.float32), w_cross_kv.astype(jnp.float32), w_cross_out.astype(jnp.float32), gain_mlp1.astype(jnp.float32), w_up1.astype(jnp.float32), w_down1.astype(jnp.float32), gain_self.astype(jnp.float32), w_self_qkv.astype(jnp.float32), w_self_out.astype(jnp.float32), gain_mlp2.astype(jnp.float32), w_up2.astype(jnp.float32), w_down2.astype(jnp.float32))

    def whole(weights, latent_rows, token_rows):
        return layer_forward(weights, latent_rows, token_rows, segment_ids, pad_mask, block_scene)
    out, pull = jax.vjp(whole, params, latents.astype(jnp.float32), tokens.astype(jnp.float32))
    grads, latent_grad, token_grad = pull(out_grad.astype(jnp.float32))
    return (out, latent_grad, token_grad, grads[0], grads[1], grads[2], grads[3], grads[4], grads[5], grads[6], grads[7], grads[8], grads[9], grads[10], grads[11], grads[12], grads[13])
```

```python
import functools

import jax
import jax.numpy as jnp
from jax import lax
from jax.experimental import pallas as pl
from jax.experimental.pallas import tpu as pltpu
from jax.sharding import PartitionSpec as P

D = 512
FF = 2048
HEADS = 8
LAT_SCENE = 2048
HEAD = D // HEADS
PAIRS = HEADS // 2
LANES = 128
FF_STEP = 512
EPS = 1e-05
NEG = -1e30
CROSS_SCALE = D ** (-0.5)
SELF_SCALE = HEAD ** (-0.5)
GELU_C = 0.7978845608028654
GELU_K = 0.044715
VMEM_LIMIT = 60 * 1024 * 1024
F32 = jnp.float32
BF16 = jnp.bfloat16


def low(value):
    return value.astype(BF16)


def dot(left, right):
    return jnp.dot(left, right, preferred_element_type=F32)


def dot_nt(left, right):
    return lax.dot_general(left, right, (((1,), (1,)), ((), ())), preferred_element_type=F32)


def dot_tn(left, right):
    return lax.dot_general(left, right, (((0,), (0,)), ((), ())), preferred_element_type=F32)


def normed(value):
    centered = value - jnp.mean(value, axis=-1, keepdims=True)
    factor = lax.rsqrt(jnp.mean(centered * centered, axis=-1, keepdims=True) + EPS)
    return centered * factor, factor


def norm_back(grad, unit, factor, gain):
    scaled = grad * gain
    inner = (
        scaled
        - jnp.mean(scaled, axis=-1, keepdims=True)
        - unit * jnp.mean(scaled * unit, axis=-1, keepdims=True)
    )
    return factor * inner, jnp.sum(grad * unit, axis=0, keepdims=True)


def gelu(u):
    return 0.5 * u * (1.0 + jnp.tanh(GELU_C * (u + GELU_K * u * u * u)))


def gelu_both(u):
    square = u * u
    t = jnp.tanh(GELU_C * u * (1.0 + GELU_K * square))
    half = 0.5 * (1.0 + t)
    slope = half + 0.5 * u * (1.0 - t * t) * (GELU_C * (1.0 + 3.0 * GELU_K * square))
    return u * half, slope


def call(kernel, grid, ins, outs, scratch=(), comm=None, collective_id=None):
    in_specs = [pl.BlockSpec(block, index) for _, block, index in ins]
    out_specs = [pl.BlockSpec(block, index) for _, _, block, index in outs]
    out_shape = [jax.ShapeDtypeStruct(shape, kind) for shape, kind, _, _ in outs]
    arrays, scratch = [array for array, _, _ in ins], list(scratch)
    if comm is not None:
        arrays += comm.inputs
        in_specs += [pl.BlockSpec(memory_space=pl.ANY)] * len(comm.inputs)
        out_shape += comm.out_shapes
        out_specs += [
            pl.BlockSpec(made.shape, lambda *_, n=len(made.shape): (0,) * n) for made in comm.out_shapes
        ]
        scratch += comm.scratch
    return pl.pallas_call(
        kernel,
        grid=grid,
        in_specs=in_specs,
        out_specs=out_specs,
        out_shape=out_shape,
        scratch_shapes=scratch,
        compiler_params=pltpu.CompilerParams(
            vmem_limit_bytes=VMEM_LIMIT,
            collective_id=None if comm is None else collective_id,
            has_side_effects=comm is not None,
        ),
    )(*arrays)


def flat(*_):
    return (0, 0)


def column(c):
    return lambda *_: (0, c)


def rows_of(i, *_):
    return (i, 0)


def front_kernel(
    lat_ref, tok_ref, bias_ref, gain_ref, wq_ref, wkv_ref, wout_ref, wup_ref, wdown_ref, wqkv_ref,
    x1_ref, x2_ref, q_ref, p_ref, o_ref, kv_ref, q2_ref, k2_ref, v2_ref,
):
    @pl.when(pl.program_id(0) == 0)
    def _():
        unit, _ = normed(tok_ref[...].astype(F32))
        kv_ref[...] = low(dot(low(unit * gain_ref[1:2, :]), wkv_ref[...]))

    x = lat_ref[...].astype(F32)
    unit, _ = normed(x)
    q = low(dot(low(unit * gain_ref[0:1, :]), wq_ref[...]))
    q_ref[...] = q
    s = dot_nt(q, kv_ref[:, :D]) * CROSS_SCALE + bias_ref[...]
    e = jnp.exp(s - jnp.max(s, axis=1, keepdims=True))
    p = low(e / jnp.sum(e, axis=1, keepdims=True))
    p_ref[...] = p
    o = low(dot(p, kv_ref[:, D:]))
    o_ref[...] = o
    x1 = x + dot(o, wout_ref[...])
    x1_ref[...] = x1
    unit, _ = normed(x1)
    m1 = low(unit * gain_ref[2:3, :])
    total = x1
    for c in range(FF // FF_STEP):
        cols = slice(c * FF_STEP, (c + 1) * FF_STEP)
        h = low(gelu(dot(m1, wup_ref[:, cols])))
        total = total + dot(h, wdown_ref[cols, :])
    x2_ref[...] = total
    unit, _ = normed(total)
    bn = low(unit * gain_ref[3:4, :])
    q2_ref[...] = low(dot(bn, wqkv_ref[:, :D])) * SELF_SCALE
    k2_ref[...] = low(dot(bn, wqkv_ref[:, D : 2 * D]))
    v2_ref[...] = low(dot(bn, wqkv_ref[:, 2 * D :]))


def front(latents, window, bias, gains, wide, tall):
    rows, span = latents.shape[0], window.shape[0]
    block = min(rows, 256)
    r = (block, D)
    return call(
        front_kernel,
        (rows // block,),
        [
            (latents, r, rows_of),
            (window, (span, D), flat),
            (bias, (1, span), flat),
            (gains, (8, D), flat),
            (wide, (D, D), column(2)),
            (wide, (D, 2 * D), column(0)),
            (wide, (D, D), column(3)),
            (wide, (D, FF), column(1)),
            (tall, (FF, D), column(0)),
            (wide, (D, 3 * D), column(3)),
        ],
        [
            ((rows, D), F32, r, rows_of),
            ((rows, D), F32, r, rows_of),
            ((rows, D), BF16, r, rows_of),
            ((rows, span), BF16, (block, span), rows_of),
            ((rows, D), BF16, r, rows_of),
            ((span, 2 * D), BF16, (span, 2 * D), flat),
            ((rows, D), BF16, r, rows_of),
            ((rows, D), BF16, r, rows_of),
            ((rows, D), BF16, r, rows_of),
        ],
    )


def lane_is(shape, head):
    lane = lax.broadcasted_iota(jnp.int32, shape, 1)
    return (lane < HEAD) if head == 0 else (lane >= HEAD)


def only(value, head):
    return jnp.where(lane_is(value.shape, head), value, jnp.zeros_like(value))


def self_forward_kernel(parts, q_ref, *refs):
    k_refs, v_refs = refs[:parts], refs[parts : 2 * parts]
    o_ref, lse_ref = refs[2 * parts : 2 * parts + 2]
    ones_refs = refs[2 * parts + 2 :]

    @pl.when(pl.program_id(1) == 0)
    def _():
        for v_ref, ones_ref in zip(v_refs, ones_refs):
            v = v_ref[...]
            for head in range(2):
                ones_ref[head] = jnp.where(lane_is(v.shape, head), v, jnp.ones_like(v))

    q = q_ref[...]
    outs, logs = [], []
    for head in range(2):
        scores = [dot_nt(only(q, head), k_ref[...]) for k_ref in k_refs]
        top = functools.reduce(jnp.maximum, [jnp.max(s, axis=1, keepdims=True) for s in scores])
        mixed = None
        for s, ones_ref in zip(scores, ones_refs):
            term = dot(low(jnp.exp(s - top)), ones_ref[head])
            mixed = term if mixed is None else mixed + term
        total = pltpu.roll(mixed, HEAD, 1)
        outs.append(mixed / total)
        logs.append(top + jnp.log(total))
    first = lane_is(outs[0].shape, 0)
    o_ref[...] = low(jnp.where(first, outs[0], outs[1]))
    turned = jnp.transpose(jnp.where(first, logs[0], logs[1]))
    lse_ref[0, 0:1, :] = turned[0:1]
    lse_ref[0, 1:2, :] = turned[HEAD : HEAD + 1]


def self_forward(q2, keys, values):
    rows = q2.shape[0]
    block = min(rows, 256)
    parts = len(keys)
    whole = lambda array: (array, (array.shape[0], LANES), lambda p, i: (0, p))
    return call(
        functools.partial(self_forward_kernel, parts),
        (PAIRS, rows // block),
        [(q2, (block, LANES), lambda p, i: (i, p))]
        + [whole(k) for k in keys]
        + [whole(v) for v in values],
        [
            ((rows, D), BF16, (block, LANES), lambda p, i: (i, p)),
            ((PAIRS, 8, rows), F32, (1, 8, block), lambda p, i: (p, 0, i)),
        ],
        [pltpu.VMEM((2, k.shape[0], LANES), BF16) for k in keys],
    )


def run_beside(comm, step, total):
    n = len(comm.chunks)
    plan = {}
    at = lambda when, fn, k: plan.setdefault(min(when, total - 1), []).append((fn, k))
    for k in range(n):
        at(0, comm.start, k)
        at(1 + k, comm.in_chip, k)
        at(total * (4 + 4 * k) // 16 + 1, comm.in_plane, k)
        at(total * (7 + 4 * k) // 16 + 1, comm.in_line, k)
        at(total - 1, comm.end, k)
    for when, steps in sorted(plan.items()):
        def run(when=when, steps=steps):
            if when == 0:
                comm.here.greet()
            for fn, k in steps:
                fn(k)
        pl.when(step == when)(run)


def self_backward_kernel(parts, steps, comm, q_ref, do_ref, lse_ref, delta_ref, *refs):
    if comm is not None:
        n_in, n_out, n_scratch = len(comm.inputs), len(comm.out_shapes), len(comm.scratch)
        outs = 2 * parts + n_in
        comm.bind(
            refs[2 * parts : outs],
            refs[outs + 1 + 2 * parts : outs + 1 + 2 * parts + n_out],
            refs[len(refs) - n_scratch :],
        )
        refs = refs[: 2 * parts] + refs[outs : outs + 1 + 2 * parts] + refs[
            outs + 1 + 2 * parts + n_out : len(refs) - n_scratch
        ]
    k_refs, v_refs = refs[:parts], refs[parts : 2 * parts]
    dq_ref = refs[2 * parts]
    dk_refs = refs[2 * parts + 1 : 3 * parts + 1]
    dv_refs = refs[3 * parts + 1 : 4 * parts + 1]
    dk_sums, dv_sums = refs[4 * parts + 1 : 5 * parts + 1], refs[5 * parts + 1 :]
    pair, step = pl.program_id(0), pl.program_id(1)

    @pl.when(step == 0)
    def _():
        for ref in (*dk_sums, *dv_sums):
            ref[...] = jnp.zeros_like(ref)

    if comm is not None:
        run_beside(comm, pair * steps + step, PAIRS * steps)

    q, do = q_ref[...], do_ref[...]
    dqs = []
    for head in range(2):
        qz, doz = only(q, head), only(do, head)
        lse = lse_ref[0, head : head + 1, :]
        delta = delta_ref[pl.ds(2 * pair + head, 1), :]
        dq = None
        for k_ref, v_ref, dk_sum, dv_sum in zip(k_refs, v_refs, dk_sums, dv_sums):
            k = k_ref[...]
            p = jnp.exp(dot_nt(k, qz) - lse)
            dp = dot_nt(v_ref[...], doz)
            ds = low(p * (dp - delta))
            dv_sum[...] += dot(low(p), doz)
            dk_sum[...] += dot(ds, qz)
            term = dot_tn(ds, k)
            dq = term if dq is None else dq + term
        dqs.append(dq)
    dq_ref[...] = low(jnp.where(lane_is(dqs[0].shape, 0), dqs[0], dqs[1]) * SELF_SCALE)

    @pl.when(step == steps - 1)
    def _():
        for ref, total in zip((*dk_refs, *dv_refs), (*dk_sums, *dv_sums)):
            ref[...] = low(total[...])


def self_backward(q2, do2, lse, delta, keys, values, comm=None):
    rows = q2.shape[0]
    block = min(rows, 256)
    parts = len(keys)
    whole = lambda array: (array, (array.shape[0], LANES), lambda p, i: (0, p))
    made = lambda array: (array.shape, BF16, (array.shape[0], LANES), lambda p, i: (0, p))
    out = call(
        functools.partial(self_backward_kernel, parts, rows // block, comm),
        (PAIRS, rows // block),
        [
            (q2, (block, LANES), lambda p, i: (i, p)),
            (do2, (block, LANES), lambda p, i: (i, p)),
            (lse, (1, 8, block), lambda p, i: (p, 0, i)),
            (delta, (8, block), lambda p, i: (0, i)),
        ]
        + [whole(k) for k in keys]
        + [whole(v) for v in values],
        [((rows, D), BF16, (block, LANES), lambda p, i: (i, p))]
        + [made(k) for k in keys]
        + [made(v) for v in values],
        [pltpu.VMEM((k.shape[0], LANES), F32) for k in (*keys, *values)],
        comm=comm,
        collective_id=1,
    )
    return out[0], out[1 : 1 + parts], out[1 + parts : 1 + 2 * parts], out[1 + 2 * parts :]


def second_kernel(
    steps, x2_ref, o2_ref, og_ref, gain_ref, wso_ref, wup_ref, wdown_ref,
    out_ref, g3_ref, do_ref, delta_ref, dwup_ref, dwdown_ref, dwso_ref, dgain_ref,
    m_ref, f_ref, dm_ref,
):
    c = pl.program_id(0)

    @pl.when(c == 0)
    def _():
        x3 = x2_ref[...] + dot(o2_ref[...], wso_ref[...])
        unit, _ = normed(x3)
        m_ref[...] = low(unit * gain_ref[4:5, :])
        out_ref[...] = x3
        f_ref[...] = jnp.zeros_like(f_ref)
        dm_ref[...] = jnp.zeros_like(dm_ref)

    m, og = m_ref[...], og_ref[...]
    h, slope = gelu_both(dot(m, wup_ref[...]))
    h = low(h)
    f_ref[...] += dot(h, wdown_ref[...])
    dwdown_ref[...] = low(dot_tn(h, og))
    du = low(slope * dot_nt(og, wdown_ref[...]))
    dwup_ref[...] = low(dot_tn(m, du))
    dm_ref[...] += dot_nt(du, wup_ref[...])

    @pl.when(c == steps - 1)
    def _():
        x3 = out_ref[...]
        unit, factor = normed(x3)
        out_ref[...] = x3 + f_ref[...]
        back, dgain = norm_back(dm_ref[...], unit, factor, gain_ref[4:5, :])
        g3 = og_ref[...].astype(F32) + back
        g3_ref[...] = g3
        dgain_ref[...] = jnp.broadcast_to(dgain, dgain_ref.shape)
        b3 = low(g3)
        o2 = o2_ref[...]
        dwso_ref[...] = low(dot_tn(o2, b3))
        do = low(dot_nt(b3, wso_ref[...]))
        do_ref[...] = do
        head = lax.broadcasted_iota(jnp.int32, (HEADS, D), 1) // HEAD
        pick = jnp.where(head == lax.broadcasted_iota(jnp.int32, (HEADS, D), 0), 1.0, 0.0)
        product = do.astype(F32) * o2.astype(F32)
        high = low(product)
        rest = low(product - high.astype(F32))
        delta_ref[...] = dot_nt(low(pick), high) + dot_nt(low(pick), rest)


def second(x2, o2, og, gains, wide, tall):
    rows = x2.shape[0]
    steps = FF // FF_STEP
    r = (rows, D)
    return call(
        functools.partial(second_kernel, steps),
        (steps,),
        [
            (x2, r, flat),
            (o2, r, flat),
            (og, r, flat),
            (gains, (8, D), flat),
            (wide, (D, D), column(8)),
            (wide, (D, FF_STEP), lambda c: (0, 3 * FF // FF_STEP + c)),
            (tall, (FF_STEP, D), lambda c: (c, 1)),
        ],
        [
            (r, F32, r, flat),
            (r, F32, r, flat),
            (r, BF16, r, flat),
            ((HEADS, rows), F32, (HEADS, rows), flat),
            ((D, FF), BF16, (D, FF_STEP), lambda c: (0, c)),
            ((FF, D), BF16, (FF_STEP, D), lambda c: (c, 0)),
            ((D, D), BF16, (D, D), flat),
            ((8, D), F32, (8, D), flat),
        ],
        [pltpu.VMEM(r, BF16), pltpu.VMEM(r, F32), pltpu.VMEM(r, F32)],
    )


def qkv_back_kernel(
    x2_ref, g3_ref, dq_ref, dk_ref, dk_more_ref, dv_ref, dv_more_ref, gain_ref, w_ref,
    g2_ref, dw_ref, dgain_ref,
):
    unit, factor = normed(x2_ref[...])
    gain = gain_ref[3:4, :]
    bn = low(unit * gain)
    dq = dq_ref[...]
    dk = low(dk_ref[...].astype(F32) + dk_more_ref[...].astype(F32))
    dv = low(dv_ref[...].astype(F32) + dv_more_ref[...].astype(F32))
    dbn = None
    for i, part in enumerate((dq, dk, dv)):
        cols = slice(i * D, (i + 1) * D)
        dw_ref[:, cols] = low(dot_tn(bn, part))
        term = dot_nt(part, w_ref[:, cols])
        dbn = term if dbn is None else dbn + term
    back, dgain = norm_back(dbn, unit, factor, gain)
    g2_ref[...] = g3_ref[...] + back
    dgain_ref[...] = jnp.broadcast_to(dgain, dgain_ref.shape)


def qkv_back(x2, g3, dq, dk, dk_more, dv, dv_more, gains, wide):
    rows = x2.shape[0]
    r = (rows, D)
    return call(
        qkv_back_kernel,
        (1,),
        [(a, r, flat) for a in (x2, g3, dq, dk, dk_more, dv, dv_more)]
        + [(gains, (8, D), flat), (wide, (D, 3 * D), column(3))],
        [
            (r, F32, r, flat),
            ((D, 3 * D), BF16, (D, 3 * D), flat),
            ((8, D), F32, (8, D), flat),
        ],
    )


def first_back_kernel(
    steps, x1_ref, g2_ref, o_ref, gain_ref, wout_ref, wup_ref, wdown_ref,
    g1_ref, do_ref, dwup_ref, dwdown_ref, dwout_ref, dgain_ref,
    m_ref, b_ref, dm_ref,
):
    c = pl.program_id(0)

    @pl.when(c == 0)
    def _():
        unit, _ = normed(x1_ref[...])
        m_ref[...] = low(unit * gain_ref[2:3, :])
        b_ref[...] = low(g2_ref[...])
        dm_ref[...] = jnp.zeros_like(dm_ref)

    m, b = m_ref[...], b_ref[...]
    h, slope = gelu_both(dot(m, wup_ref[...]))
    dwdown_ref[...] = low(dot_tn(low(h), b))
    du = low(slope * dot_nt(b, wdown_ref[...]))
    dwup_ref[...] = low(dot_tn(m, du))
    dm_ref[...] += dot_nt(du, wup_ref[...])

    @pl.when(c == steps - 1)
    def _():
        unit, factor = normed(x1_ref[...])
        back, dgain = norm_back(dm_ref[...], unit, factor, gain_ref[2:3, :])
        g1 = g2_ref[...] + back
        g1_ref[...] = g1
        dgain_ref[...] = jnp.broadcast_to(dgain, dgain_ref.shape)
        b1 = low(g1)
        dwout_ref[...] = low(dot_tn(o_ref[...], b1))
        do_ref[...] = low(dot_nt(b1, wout_ref[...]))


def first_back(x1, g2, o, gains, wide, tall):
    rows = x1.shape[0]
    steps = FF // FF_STEP
    r = (rows, D)
    return call(
        functools.partial(first_back_kernel, steps),
        (steps,),
        [
            (x1, r, flat),
            (g2, r, flat),
            (o, r, flat),
            (gains, (8, D), flat),
            (wide, (D, D), column(3)),
            (wide, (D, FF_STEP), lambda c: (0, FF // FF_STEP + c)),
            (tall, (FF_STEP, D), lambda c: (c, 0)),
        ],
        [
            (r, F32, r, flat),
            (r, BF16, r, flat),
            ((D, FF), BF16, (D, FF_STEP), lambda c: (0, c)),
            ((FF, D), BF16, (FF_STEP, D), lambda c: (c, 0)),
            ((D, D), BF16, (D, D), flat),
            ((8, D), F32, (8, D), flat),
        ],
        [pltpu.VMEM(r, BF16), pltpu.VMEM(r, BF16), pltpu.VMEM(r, F32)],
    )


def cross_back_kernel(
    steps, lat_ref, g1_ref, do_ref, p_ref, q_ref, kv_ref, gain_ref, wq_ref,
    lg_ref, dwq_ref, dkv_ref, dgain_ref, dk_sum, dv_sum, dwq_sum,
):
    i = pl.program_id(0)

    @pl.when(i == 0)
    def _():
        for ref in (dk_sum, dv_sum, dwq_sum, dgain_ref):
            ref[...] = jnp.zeros_like(ref)

    p, do, q = p_ref[...], do_ref[...], q_ref[...]
    dp = dot_nt(do, kv_ref[:, D:])
    wide_p = p.astype(F32)
    ds = low(wide_p * (dp - jnp.sum(wide_p * dp, axis=1, keepdims=True)))
    dq = low(dot(ds, kv_ref[:, :D]) * CROSS_SCALE)
    dk_sum[...] += dot_tn(ds, q)
    dv_sum[...] += dot_tn(p, do)
    unit, factor = normed(lat_ref[...].astype(F32))
    gain = gain_ref[0:1, :]
    dwq_sum[...] += dot_tn(low(unit * gain), dq)
    back, dgain = norm_back(dot_nt(dq, wq_ref[...]), unit, factor, gain)
    lg_ref[...] = g1_ref[...] + back
    dgain_ref[...] += jnp.broadcast_to(dgain, dgain_ref.shape)

    @pl.when(i == steps - 1)
    def _():
        dwq_ref[...] = low(dwq_sum[...])
        dkv_ref[:, :D] = low(dk_sum[...] * CROSS_SCALE)
        dkv_ref[:, D:] = low(dv_sum[...])


def cross_back(latents, g1, do, p, q, kv, gains, wide):
    rows, span = p.shape
    block = min(rows, 512)
    r = (block, D)
    return call(
        functools.partial(cross_back_kernel, rows // block),
        (rows // block,),
        [
            (latents, r, rows_of),
            (g1, r, rows_of),
            (do, r, rows_of),
            (p, (block, span), rows_of),
            (q, r, rows_of),
            (kv, (span, 2 * D), flat),
            (gains, (8, D), flat),
            (wide, (D, D), column(2)),
        ],
        [
            ((rows, D), F32, r, rows_of),
            ((D, D), BF16, (D, D), flat),
            ((span, 2 * D), BF16, (span, 2 * D), flat),
            ((8, D), F32, (8, D), flat),
        ],
        [pltpu.VMEM((span, D), F32), pltpu.VMEM((span, D), F32), pltpu.VMEM((D, D), F32)],
    )


def token_back_kernel(tok_ref, dkv_ref, more_ref, gain_ref, w_ref, tg_ref, dw_ref, dgain_ref):
    unit, factor = normed(tok_ref[...].astype(F32))
    gain = gain_ref[1:2, :]
    dkv = low(dkv_ref[...].astype(F32) + more_ref[...].astype(F32))
    dw_ref[...] = low(dot_tn(low(unit * gain), dkv))
    back, dgain = norm_back(dot_nt(dkv, w_ref[...]), unit, factor, gain)
    tg_ref[...] = low(back)
    dgain_ref[...] = jnp.broadcast_to(dgain, dgain_ref.shape)


def token_back(tokens, dkv, more, gains, wide):
    rows = tokens.shape[0]
    return call(
        token_back_kernel,
        (1,),
        [
            (tokens, (rows, D), flat),
            (dkv, (rows, 2 * D), flat),
            (more, (rows, 2 * D), flat),
            (gains, (8, D), flat),
            (wide, (D, 2 * D), column(0)),
        ],
        [
            ((rows, D), BF16, (rows, D), flat),
            ((D, 2 * D), BF16, (D, 2 * D), flat),
            ((8, D), F32, (8, D), flat),
        ],
    )


MESH = pl.DeviceIdType.MESH
UP, DOWN = 0, 1


class Place:
    def __init__(self):
        row, lat = lax.axis_index("row"), lax.axis_index("lat")
        self.x, self.y, self.z, self.c = row % 2, row // 2, lat // 2, lat % 2
        self.r = row
        self.rx = self.y * 2 + 1 - self.x
        self.ry = (1 - self.y) * 2 + self.x
        self.rd = (1 - self.y) * 2 + 1 - self.x
        self.to_x, self.to_y = (self.rx, lat), (self.ry, lat)
        self.to_core = (row, self.z * 2 + 1 - self.c)
        self.to_z = ((row, lat + 2), (row, lat - 2))
        self.more = (self.z < 3, self.z > 0)

    def greet(self):
        barrier = pltpu.get_barrier_semaphore()
        for device in (self.to_x, self.to_y, self.to_core):
            pl.semaphore_signal(barrier, inc=1, device_id=device, device_id_type=MESH)
        for way in (UP, DOWN):
            @pl.when(self.more[way])
            def _():
                pl.semaphore_signal(barrier, inc=1, device_id=self.to_z[way], device_id_type=MESH)
        pl.semaphore_wait(barrier, 3 + jnp.minimum(self.z, 1) + jnp.minimum(3 - self.z, 1))

    def source(self, way, hop):
        return (self.z - hop, self.z >= hop) if way == UP else (self.z + hop, self.z + hop <= 3)


def send(src, dst, sems, index, device):
    return pltpu.make_async_remote_copy(
        src_ref=src, dst_ref=dst, send_sem=sems[0].at[index], recv_sem=sems[1].at[index],
        device_id=device, device_id_type=MESH,
    )


def sem_pair(*shape):
    return [pltpu.SemaphoreType.DMA(shape), pltpu.SemaphoreType.DMA(shape)]


WIDE_STEP = 2048
NARROW_STEP = 512
TOKEN_PARTS = 4
AHEAD = 2
GAP = 2
CHUNKS = (
    (3, 0, 16),
    (0, 0, WIDE_STEP),
    (0, WIDE_STEP, WIDE_STEP),
    (1, 0, NARROW_STEP),
    (0, 2 * WIDE_STEP, WIDE_STEP),
    (0, 3 * WIDE_STEP, WIDE_STEP),
    (1, NARROW_STEP, NARROW_STEP),
) + tuple((2, part, TOKEN_PARTS) for part in range(TOKEN_PARTS))


def gather_kernel(counts, *refs):
    n_wide, n_tall = counts
    n_in = 2 + n_wide + n_tall
    tok_ref, meta_ref = refs[:2]
    shards = (refs[2 : 2 + n_wide], refs[2 + n_wide : n_in])
    tok_all, meta_all, wide_all, tall_all = refs[n_in : n_in + 4]
    sems = refs[n_in + 4 :]
    local_sem, z_sems, p_sems, q_sems, c_sems = sems[0], sems[1:3], sems[3:5], sems[5:7], sems[7:9]
    here = Place()
    z, c, r = here.z, here.c, here.r
    full = (wide_all, tall_all, tok_all, meta_all)
    total = len(CHUNKS)

    def block(k, source, core=None):
        which, first, width = CHUNKS[k]
        core = c if core is None else core
        if which == 3:
            return meta_all.at[source, core]
        if which == 2:
            rows = tok_all.shape[2] // width
            return tok_all.at[source, core, pl.ds(first * rows, rows)]
        return full[which].at[source, core, :, :, pl.ds(first, width)]

    def piece(k, source, quarter, half=None):
        which, first, width = CHUNKS[k]
        if which >= 2:
            return block(k, source)
        if half is not None:
            first, width = first + half * (width // 2), width // 2
        return full[which].at[source, c, quarter, :, pl.ds(first, width)]

    def shared(k):
        return CHUNKS[k][0] < 2

    here.greet()
    copies = [pltpu.make_async_copy(tok_ref, tok_all.at[z, c], local_sem.at[0]),
              pltpu.make_async_copy(meta_ref, meta_all.at[z, c], local_sem.at[1])]
    for which in (0, 1):
        first = 0
        for shard in shards[which]:
            width = shard.shape[-1]
            copies.append(pltpu.make_async_copy(
                shard, full[which].at[z, c, :, :, pl.ds(first, width)], local_sem.at[len(copies)]))
            first += width
    for copy in copies:
        copy.start()
    for copy in copies:
        copy.wait()

    def z_send(k, way, hop):
        source, _ = here.source(way, hop - 1)
        ref = piece(k, source, r)
        return send(ref, ref, z_sems, (k, way, hop - 1), here.to_z[way])

    def z_recv(k, way, hop):
        source, _ = here.source(way, hop)
        ref = piece(k, source, r)
        return send(ref, ref, z_sems, (k, way, hop - 1), here.to_z[way])

    def p_send(k, way, hop, axis):
        source, _ = here.source(way, hop)
        ref = piece(k, source, r)
        return send(ref, ref, p_sems, (k, way, hop - 1, axis), (here.to_x, here.to_y)[axis])

    def p_recv(k, way, hop, axis):
        source, _ = here.source(way, hop)
        ref = piece(k, source, (here.rx, here.ry)[axis])
        return send(ref, ref, p_sems, (k, way, hop - 1, axis), (here.to_x, here.to_y)[axis])

    def q_send(k, way, hop, half):
        source, _ = here.source(way, hop)
        ref = piece(k, source, (here.rx, here.ry)[half], half)
        return send(ref, ref, q_sems, (k, way, hop - 1, half), (here.to_y, here.to_x)[half])

    def q_recv(k, way, hop, half):
        source, _ = here.source(way, hop)
        ref = piece(k, source, here.rd, half)
        return send(ref, ref, q_sems, (k, way, hop - 1, half), (here.to_y, here.to_x)[half])

    def c_copy(k, source, index, mine):
        ref = block(k, source, c if mine else 1 - c)
        return send(ref, ref, c_sems, (k, index), here.to_core)

    def ways(hop, fn):
        for way in (UP, DOWN):
            source, valid = here.source(way, hop)
            pl.when(valid)(functools.partial(fn, way, hop, source))

    def index_of(way, hop):
        return 1 + way * 3 + hop - 1

    def first_sends(k):
        for way in (UP, DOWN):
            pl.when(here.more[way])(lambda way=way: z_send(k, way, 1).start())
        c_copy(k, z, 0, True).start()

    def stage_z(k, hop):
        def arrive(way, hop, source):
            z_recv(k, way, hop).wait_recv()
            if hop < 3:
                pl.when(here.more[way])(lambda: z_send(k, way, hop + 1).start())
            if shared(k):
                p_send(k, way, hop, 0).start()
                p_send(k, way, hop, 1).start()
            else:
                c_copy(k, source, index_of(way, hop), True).start()
        ways(hop, arrive)

    def stage_p(k, hop):
        def arrive(way, hop, source):
            for axis in (0, 1):
                p_recv(k, way, hop, axis).wait_recv()
                q_send(k, way, hop, axis).start()
        ways(hop, arrive)

    def stage_q(k, hop):
        def arrive(way, hop, source):
            q_recv(k, way, hop, 0).wait_recv()
            q_recv(k, way, hop, 1).wait_recv()
            c_copy(k, source, index_of(way, hop), True).start()
        ways(hop, arrive)

    for k in range(AHEAD):
        first_sends(k)
    for step in range(total + 4 * GAP + 1):
        if step + AHEAD < total:
            first_sends(step + AHEAD)
        for lag, stage in ((0, stage_z), (GAP, stage_p), (2 * GAP, stage_q)):
            for hop in (1, 2, 3):
                k = step - lag - GAP * (hop - 1)
                if 0 <= k < total and (lag == 0 or shared(k)):
                    stage(k, hop)
    for k in range(total):
        for way in (UP, DOWN):
            for hop in (1, 2, 3):
                source, valid = here.source(way, hop - 1)
                pl.when(valid & here.more[way])(lambda k=k, way=way, hop=hop: z_send(k, way, hop).wait_send())
        c_copy(k, z, 0, True).wait_send()
        c_copy(k, z, 0, False).wait_recv()

        def finish(way, hop, source):
            c_copy(k, source, index_of(way, hop), True).wait_send()
            c_copy(k, source, index_of(way, hop), False).wait_recv()
            if shared(k):
                for axis in (0, 1):
                    p_send(k, way, hop, axis).wait_send()
                    q_send(k, way, hop, axis).wait_send()
        for hop in (1, 2, 3):
            ways(hop, finish)


def gather_all(tokens, meta, wide_shards, tall_shards):
    anywhere = pl.BlockSpec(memory_space=pl.ANY)
    slots = tokens.shape[0]
    wide_shards = [w.reshape(4, w.shape[0] // 4, w.shape[1]) for w in wide_shards]
    tall_shards = [w.reshape(4, w.shape[0] // 4, w.shape[1]) for w in tall_shards]
    wide_cols = sum(w.shape[-1] for w in wide_shards)
    tall_cols = sum(w.shape[-1] for w in tall_shards)
    total = len(CHUNKS)
    inputs = [tokens, meta, *wide_shards, *tall_shards]
    tok_all, meta_all, wide, tall = pl.pallas_call(
        functools.partial(gather_kernel, (len(wide_shards), len(tall_shards))),
        in_specs=[pl.BlockSpec(memory_space=pltpu.VMEM)] * len(inputs),
        out_specs=[anywhere] * 4,
        out_shape=[
            jax.ShapeDtypeStruct((4, 2) + tokens.shape, BF16),
            jax.ShapeDtypeStruct((4, 2) + meta.shape, BF16),
            jax.ShapeDtypeStruct((4, 2) + wide_shards[0].shape[:2] + (wide_cols,), BF16),
            jax.ShapeDtypeStruct((4, 2) + tall_shards[0].shape[:2] + (tall_cols,), BF16),
        ],
        scratch_shapes=[pltpu.SemaphoreType.DMA((len(inputs),))]
        + sem_pair(total, 2, 3)
        + sem_pair(total, 2, 3, 2)
        + sem_pair(total, 2, 3, 2)
        + sem_pair(total, 7),
        compiler_params=pltpu.CompilerParams(collective_id=0, has_side_effects=True),
    )(*inputs)
    return (
        tok_all.reshape(8 * slots, D),
        meta_all.reshape(8, meta.shape[0], meta.shape[1]),
        wide.reshape(-1, wide_cols),
        tall.reshape(-1, tall_cols),
    )


class Peers(Place):
    def __init__(self):
        super().__init__()
        lat = lax.axis_index("lat")
        self.plane = (self.to_x, self.to_y, (self.rd, lat))
        self.quarters = (self.rx, self.ry, self.rd)
        self.above = [lax.rem(self.z + 1 + i, 4) for i in range(3)]
        self.line = [(self.r, z * 2 + self.c) for z in self.above]

    def greet(self):
        barrier = pltpu.get_barrier_semaphore()
        others = (self.to_core, *self.plane, *self.line)
        for device in others:
            pl.semaphore_signal(barrier, inc=1, device_id=device, device_id_type=MESH)
        pl.semaphore_wait(barrier, len(others))


class WeightSum:
    def __init__(self, chunks, gains=None, tokens=None):
        self.chunks = []
        self.inputs = []
        for chunk in chunks:
            self.chunks.append([])
            for array in chunk:
                shape = (4, 2, 4, array.shape[0] // 32, array.shape[1])
                self.chunks[-1].append((len(self.inputs), shape[-1]))
                self.inputs.append(array.reshape(shape))
        self.sizes = [
            (self.inputs[parts[0][0]].shape[3], sum(width for _, width in parts))
            for parts in self.chunks
        ]
        self.out_shapes = [jax.ShapeDtypeStruct((4,) + size, BF16) for size in self.sizes]
        self.scratch = []
        for size in self.sizes:
            self.scratch += [pltpu.VMEM(shape + size, BF16) for shape in ((4, 4), (4, 4), (3, 4), (3,), (4,))]
        n = len(self.chunks)
        self.scratch += [pltpu.SemaphoreType.DMA((len(self.inputs),))]
        self.scratch += sem_pair(len(self.inputs)) + sem_pair(n, 3) + sem_pair(n, 3) + sem_pair(n, 3)
        self.gains = gains
        self.tokens = tokens
        if gains is not None:
            self.inputs.append(gains)
            self.out_shapes.append(jax.ShapeDtypeStruct(gains.shape, F32))
            self.scratch += [pltpu.VMEM(shape + gains.shape, F32) for shape in ((), (), (4,), (3,))]
            self.scratch += [pltpu.SemaphoreType.DMA((1,))]
            self.scratch += sem_pair(1) + sem_pair(3) + sem_pair(3)
        if tokens is not None:
            rows = tokens.shape[0] // 8
            self.inputs.append(tokens.reshape(4, 2, rows, D))
            self.out_shapes.append(jax.ShapeDtypeStruct((rows, D), F32))
            self.scratch += [pltpu.VMEM((n, rows, D), BF16) for n in (4, 4, 3)]
            self.scratch += [pltpu.SemaphoreType.DMA((1,))] + sem_pair(1) + sem_pair(3)

    def bind(self, ins, outs, scratch):
        self.here = Peers()
        self.ins, self.outs = ins, outs
        scratch = list(scratch)
        take = lambda n: [scratch.pop(0) for _ in range(n)]
        self.buffers = [take(5) for _ in self.chunks]
        self.local = take(1)[0]
        self.c_sems, self.p_sems, self.z_sems, self.g_sems = (take(2) for _ in range(4))
        if self.gains is not None:
            self.gain_buffers, self.gain_local = take(4), take(1)[0]
            self.gain_sems = [take(2) for _ in range(3)]
        if self.tokens is not None:
            self.token_buffers, self.token_local = take(3), take(1)[0]
            self.token_sems = [take(2) for _ in range(2)]


    def own(self, k):
        first = 0
        for index, width in self.chunks[k]:
            yield pltpu.make_async_copy(
                self.ins[index].at[:, self.here.c],
                self.buffers[k][0].at[:, :, :, pl.ds(first, width)],
                self.local.at[index],
            )
            first += width

    def to_core(self, k):
        first = 0
        for index, width in self.chunks[k]:
            yield send(
                self.ins[index].at[:, 1 - self.here.c],
                self.buffers[k][1].at[:, :, :, pl.ds(first, width)],
                self.c_sems, index, self.here.to_core,
            )
            first += width

    def to_plane(self, k):
        for i in range(3):
            yield send(
                self.buffers[k][0].at[:, self.here.quarters[i]], self.buffers[k][2].at[i],
                self.p_sems, (k, i), self.here.plane[i],
            )

    def to_line(self, k):
        for i in range(3):
            yield send(
                self.buffers[k][0].at[self.here.above[i], self.here.r], self.buffers[k][3].at[i],
                self.z_sems, (k, i), self.here.line[i],
            )

    def finished(self, k):
        for i in range(3):
            mine = self.buffers[k][4].at[self.here.r]
            yield send(mine, mine, self.g_sems, (k, i), self.here.plane[i])

    def arriving(self, k):
        for i in range(3):
            theirs = self.buffers[k][4].at[self.here.quarters[i]]
            yield send(theirs, theirs, self.g_sems, (k, i), self.here.plane[i])


    def start(self, k):
        for copy in (*self.own(k), *self.to_core(k)):
            copy.start()

    def in_chip(self, k):
        for copy in self.own(k):
            copy.wait()
        for copy in self.to_core(k):
            copy.wait_recv()
        mine, theirs = self.buffers[k][:2]
        for z in range(4):
            for quarter in range(4):
                mine[z, quarter] = mine[z, quarter] + theirs[z, quarter]
        for copy in self.to_plane(k):
            copy.start()

    def in_plane(self, k):
        for copy in self.to_plane(k):
            copy.wait_recv()
        mine, _, theirs = self.buffers[k][:3]
        for z in range(4):
            total = mine[z, self.here.r].astype(F32) + theirs[0, z].astype(F32)
            mine[z, self.here.r] = low(total + theirs[1, z].astype(F32) + theirs[2, z].astype(F32))
        for copy in self.to_line(k):
            copy.start()

    def in_line(self, k):
        for copy in self.to_line(k):
            copy.wait_recv()
        mine, theirs, done = self.buffers[k][0], self.buffers[k][3], self.buffers[k][4]
        total = mine[self.here.z, self.here.r].astype(F32) + theirs[0].astype(F32)
        done[self.here.r] = low(total + theirs[1].astype(F32) + theirs[2].astype(F32))
        for copy in self.finished(k):
            copy.start()

    def end(self, k):
        for copy in self.arriving(k):
            copy.wait_recv()
        for copy in (*self.to_core(k), *self.to_plane(k), *self.to_line(k), *self.finished(k)):
            copy.wait_send()
        self.outs[k][...] = self.buffers[k][4][...]


    def gain_copy(self, stage, i):
        mine, core, plane, line = self.gain_buffers
        if stage == 0:
            return send(mine, core, self.gain_sems[0], 0, self.here.to_core)
        if stage == 1:
            return send(mine, plane.at[self.here.r], self.gain_sems[1], i, self.here.plane[i])
        return send(mine, line.at[i], self.gain_sems[2], i, self.here.line[i])

    def gain_plane_recv(self, i):
        mine, _, plane, _ = self.gain_buffers
        return send(mine, plane.at[self.here.quarters[i]], self.gain_sems[1], i, self.here.plane[i])

    def gain_step(self, stage):
        mine, core, plane, line = self.gain_buffers
        if stage == 0:
            copy = pltpu.make_async_copy(self.ins[sum(map(len, self.chunks))], mine, self.gain_local.at[0])
            copy.start()
            copy.wait()
            self.gain_copy(0, 0).start()
        elif stage == 1:
            self.gain_copy(0, 0).wait()
            mine[...] += core[...]
            plane[self.here.r] = mine[...]
            for i in range(3):
                self.gain_copy(1, i).start()
        elif stage == 2:
            for i in range(3):
                self.gain_copy(1, i).wait_send()
                self.gain_plane_recv(i).wait_recv()
            mine[...] = (plane[0] + plane[1]) + (plane[2] + plane[3])
            for i in range(3):
                self.gain_copy(2, i).start()
        else:
            for i in range(3):
                self.gain_copy(2, i).wait()
            self.outs[len(self.chunks)][...] = (mine[...] + line[0]) + (line[1] + line[2])


    def token_own(self):
        return pltpu.make_async_copy(
            self.ins[-1].at[:, self.here.c], self.token_buffers[0], self.token_local.at[0])

    def token_core(self):
        return send(self.ins[-1].at[:, 1 - self.here.c], self.token_buffers[1],
                    self.token_sems[0], 0, self.here.to_core)

    def token_line(self, i):
        return send(self.token_buffers[0].at[self.here.above[i]], self.token_buffers[2].at[i],
                    self.token_sems[1], i, self.here.line[i])

    def token_step(self, stage):
        mine, core, line = self.token_buffers
        if stage == 0:
            self.token_own().start()
            self.token_core().start()
        elif stage == 1:
            self.token_own().wait()
            self.token_core().wait()
            for z in range(4):
                mine[z] = mine[z] + core[z]
            for i in range(3):
                self.token_line(i).start()
        else:
            for i in range(3):
                self.token_line(i).wait()
            total = mine[self.here.z].astype(F32) + line[0].astype(F32)
            self.outs[-1][...] = total + line[1].astype(F32) + line[2].astype(F32)


def tail_kernel(comm, *refs):
    n_in, n_out = len(comm.inputs), len(comm.out_shapes)
    comm.bind(refs[:n_in], refs[n_in : n_in + n_out], refs[n_in + n_out :])
    order = range(len(comm.chunks))
    comm.here.greet()
    comm.token_step(0)
    comm.gain_step(0)
    for k in order:
        comm.start(k)
    comm.token_step(1)
    comm.gain_step(1)
    for k in order:
        comm.in_chip(k)
    comm.gain_step(2)
    for k in order:
        comm.in_plane(k)
    comm.gain_step(3)
    for k in order:
        comm.in_line(k)
    comm.token_step(2)
    for k in order:
        comm.end(k)


def sum_tail(comm, collective_id):
    anywhere = pl.BlockSpec(memory_space=pl.ANY)
    inside = pl.BlockSpec(memory_space=pltpu.VMEM)
    return pl.pallas_call(
        functools.partial(tail_kernel, comm),
        in_specs=[anywhere] * len(comm.inputs),
        out_specs=[inside] * len(comm.out_shapes),
        out_shape=comm.out_shapes,
        scratch_shapes=comm.scratch,
        compiler_params=pltpu.CompilerParams(
            collective_id=collective_id, has_side_effects=True, vmem_limit_bytes=VMEM_LIMIT
        ),
    )(*comm.inputs)


def widen_kernel(*refs):
    half = len(refs) // 2
    for source, target in zip(refs[:half], refs[half:]):
        target[...] = source[...].astype(F32)


def widen(arrays):
    return pl.pallas_call(
        widen_kernel,
        out_shape=[jax.ShapeDtypeStruct(a.shape, F32) for a in arrays],
        compiler_params=pltpu.CompilerParams(vmem_limit_bytes=VMEM_LIMIT),
    )(*arrays)


def from_partner(shard, bit):
    return lax.ppermute(shard, "lat", [(i, i ^ 1 << bit) for i in range(lax.axis_size("lat"))])


def gather_lat(shard):
    return lax.all_gather(shard, "lat", axis=0, tiled=True)


def halve(value, place, bits):
    kept, more = value, jnp.zeros_like(value)
    for bit in reversed(range(bits)):
        value = low(kept.astype(F32) + more.astype(F32))
        half = value.shape[0] // 2
        upper = place // 2**bit % 2
        kept = lax.dynamic_slice_in_dim(value, upper * half, half)
        more = from_partner(lax.dynamic_slice_in_dim(value, (1 - upper) * half, half), bit)
    return kept, more


def reduce_weights(grad):
    share = lax.psum_scatter(grad, "lat", scatter_dimension=0, tiled=True)
    return lax.psum(share, "row").astype(F32)


def local(
    tokens, latents, segment_ids, pad_mask, block_scene, out_grad,
    gain_cross_q, gain_cross_kv, w_cross_q, w_cross_kv, w_cross_out,
    gain_mlp1, w_up1, w_down1, gain_self, w_self_qkv, w_self_out, gain_mlp2, w_up2, w_down2,
):
    tokens, latents, og = tokens[0], latents[0], out_grad[0]
    rows, slots = latents.shape[0], tokens.shape[0] * lax.axis_size("lat")
    scenes = block_scene.shape[1]
    span = slots // scenes
    place = lax.axis_index("lat")
    group = LAT_SCENE // rows
    bits = group.bit_length() - 1

    tag = jnp.where(pad_mask == 1, segment_ids, -1)
    gains = jnp.stack([gain_cross_q, gain_cross_kv, gain_mlp1, gain_self, gain_mlp2], axis=0)
    wides = [w_cross_kv, w_cross_q, w_cross_out, w_up1, w_self_out, w_self_qkv, w_up2]
    talls = [w_down1, w_down2]
    planes = lax.axis_size("row") == 4 and lax.axis_size("lat") == 8
    if planes:
        meta = jnp.concatenate([low(tag), gains.reshape(1, -1)], axis=1)
        meta = jnp.pad(meta, ((0, 15), (0, -meta.shape[1] % LANES)))
        all_tokens, meta, wide, tall = gather_all(tokens, meta, wides, talls)
        all_tags = meta[:, 0, : tag.shape[1]].reshape(1, slots).astype(jnp.int32)
        gains = meta[:, 0, tag.shape[1] : tag.shape[1] + gains.size]
        gains = gains.reshape(8, 5, -1).transpose(1, 0, 2).reshape(5, D)
    else:
        all_tags = lax.all_gather(low(tag), "lat", axis=1, tiled=True).astype(jnp.int32)
        all_tokens = gather_lat(tokens)
        gains = lax.all_gather(gains, "lat", axis=1, tiled=True)
        wide = gather_lat(jnp.concatenate(wides, axis=1))
        tall = gather_lat(jnp.concatenate(talls, axis=1))
    gains = jnp.pad(gains.astype(F32), ((0, 3), (0, 0)))

    block = place * rows // LAT_SCENE
    scene = jnp.sum(jnp.where(jnp.arange(scenes) == block, block_scene[0], 0))
    before = jnp.sum(((all_tags >= 0) & (all_tags < scene)).astype(jnp.int32))
    start = jnp.minimum(before // 16 * 16, slots - span)
    window = lax.dynamic_slice_in_dim(all_tokens, start, span)
    bias = jnp.where(lax.dynamic_slice_in_dim(all_tags, start, span, axis=1) == scene, 0.0, NEG)

    x1, x2, q, p, o, kv, q2, k2, v2 = front(latents, window, bias.astype(F32), gains, wide, tall)
    if group == 2:
        k2_more, v2_more = from_partner((k2, v2), 0)
        keys, values = (k2, k2_more), (v2, v2_more)
    else:
        for bit in range(bits):
            upper = place // 2**bit % 2 == 1
            more = from_partner((k2, v2), bit)
            k2, v2 = (
                jnp.where(upper, jnp.concatenate([b, a]), jnp.concatenate([a, b]))
                for a, b in zip((k2, v2), more)
            )
        keys, values = (k2,), (v2,)
    o2, lse = self_forward(q2, keys, values)
    out, g3, do2, delta, dwup2, dwdown2, dwso, dgain_m2 = second(x2, o2, og, gains, wide, tall)
    comm = WeightSum([[dwup2], [dwdown2], [dwso]]) if planes else None
    dq2, dk2, dv2, early = self_backward(q2, do2, lse, delta, keys, values, comm)
    if group == 2:
        dk_more, dv_more = from_partner((dk2[1], dv2[1]), 0)
        dk, dv = dk2[0], dv2[0]
    else:
        dk, dk_more = halve(dk2[0], place, bits)
        dv, dv_more = halve(dv2[0], place, bits)
    g2, dwqkv, dgain_s = qkv_back(x2, g3, dq2, dk, dk_more, dv, dv_more, gains, wide)
    g1, do, dwup1, dwdown1, dwout, dgain_m1 = first_back(x1, g2, o, gains, wide, tall)
    latent_grad, dwq, dkv, dgain_q = cross_back(latents, g1, do, p, q, kv, gains, wide)
    mine, more = halve(dkv, place, bits)
    first = place % group * (span // group)
    token_rows = lax.dynamic_slice_in_dim(window, first, span // group)
    token_part, dwkv, dgain_kv = token_back(token_rows, mine, more, gains, wide)
    token_part = lax.dynamic_update_slice_in_dim(
        jnp.zeros((slots, D), BF16), token_part, start + first, 0
    )
    dgains = (dgain_q, dgain_kv, dgain_m1, dgain_s, dgain_m2)
    if planes:
        dgains = jnp.concatenate([g[:1] for g in dgains] + [jnp.zeros((3, D), F32)])
        comm = WeightSum(
            [[dwqkv], [dwup1], [dwdown1], [dwkv, dwq, dwout]], gains=dgains, tokens=token_part
        )
        *late, dgains, token_grad = sum_tail(comm, 2)
        dgains = lax.dynamic_slice_in_dim(dgains, place * (D // 8), D // 8, axis=1)
        qkv, up1, down1, mixed, up2, down2, so = (
            a.reshape(-1, a.shape[2]) for a in (*late, *early)
        )
        dwkv, dwq, dwout = mixed[:, : 2 * D], mixed[:, 2 * D : 3 * D], mixed[:, 3 * D :]
        sums = widen([dwq, dwkv, dwout, up1, down1, qkv, so, up2, down2])
    else:
        token_grad = lax.psum_scatter(token_part, "lat", scatter_dimension=0, tiled=True).astype(F32)
        dgains = jnp.stack([g[0] for g in dgains])
        dgains = lax.psum_scatter(low(dgains), "lat", scatter_dimension=1, tiled=True)
        dgains = lax.psum(dgains, "row").astype(F32)
        sums = [
            reduce_weights(g) for g in (dwq, dwkv, dwout, dwup1, dwdown1, dwqkv, dwso, dwup2, dwdown2)
        ]
    dwq, dwkv, dwout, dwup1, dwdown1, dwqkv, dwso, dwup2, dwdown2 = sums
    return (
        out[None],
        latent_grad[None],
        token_grad[None],
        dgains[0],
        dgains[1],
        dwq,
        dwkv,
        dwout,
        dgains[2],
        dwup1,
        dwdown1,
        dgains[3],
        dwqkv,
        dwso,
        dgains[4],
        dwup2,
        dwdown2,
    )


def solution(mesh):
    by_row = P("row", "lat", None)
    weight = P("lat", None)
    gain = P("lat")
    parameters = (
        gain, gain, weight, weight, weight, gain, weight, weight, gain, weight, weight, gain,
        weight, weight,
    )
    return jax.shard_map(
        local,
        mesh=mesh,
        in_specs=(by_row, by_row, P("row", "lat"), P("row", "lat"), P("row", None), by_row)
        + parameters,
        out_specs=(by_row, by_row, by_row) + parameters,
        check_vma=False,
    )
```

```python
import functools

import jax
import jax.numpy as jnp
from jax import lax
from jax.experimental import pallas as pl
from jax.experimental.pallas import tpu as pltpu
from jax.sharding import PartitionSpec as P

D = 512
FF = 2048
HEADS = 8
LAT_SCENE = 2048
HEAD = D // HEADS
PAIRS = HEADS // 2
LANES = 128
FF_STEP = 512
EPS = 1e-05
NEG = -1e30
CROSS_SCALE = D ** (-0.5)
SELF_SCALE = HEAD ** (-0.5)
GELU_C = 0.7978845608028654
GELU_K = 0.044715
VMEM_LIMIT = 60 * 1024 * 1024
F32 = jnp.float32
BF16 = jnp.bfloat16


def low(value):
    return value.astype(BF16)


def dot(left, right):
    return jnp.dot(left, right, preferred_element_type=F32)


def dot_nt(left, right):
    return lax.dot_general(left, right, (((1,), (1,)), ((), ())), preferred_element_type=F32)


def dot_tn(left, right):
    return lax.dot_general(left, right, (((0,), (0,)), ((), ())), preferred_element_type=F32)


def normed(value):
    centered = value - jnp.mean(value, axis=-1, keepdims=True)
    factor = lax.rsqrt(jnp.mean(centered * centered, axis=-1, keepdims=True) + EPS)
    return centered * factor, factor


def norm_back(grad, unit, factor, gain):
    scaled = grad * gain
    inner = (
        scaled
        - jnp.mean(scaled, axis=-1, keepdims=True)
        - unit * jnp.mean(scaled * unit, axis=-1, keepdims=True)
    )
    return factor * inner, jnp.sum(grad * unit, axis=0, keepdims=True)


def gelu(u):
    return 0.5 * u * (1.0 + jnp.tanh(GELU_C * (u + GELU_K * u * u * u)))


def gelu_both(u):
    square = u * u
    t = jnp.tanh(GELU_C * u * (1.0 + GELU_K * square))
    half = 0.5 * (1.0 + t)
    slope = half + 0.5 * u * (1.0 - t * t) * (GELU_C * (1.0 + 3.0 * GELU_K * square))
    return u * half, slope


def call(kernel, grid, ins, outs, scratch=(), comm=None, collective_id=None):
    in_specs = [pl.BlockSpec(block, index) for _, block, index in ins]
    out_specs = [pl.BlockSpec(block, index) for _, _, block, index in outs]
    out_shape = [jax.ShapeDtypeStruct(shape, kind) for shape, kind, _, _ in outs]
    arrays, scratch = [array for array, _, _ in ins], list(scratch)
    if comm is not None:
        arrays += comm.inputs
        in_specs += [pl.BlockSpec(memory_space=pl.ANY)] * len(comm.inputs)
        out_shape += comm.out_shapes
        out_specs += [
            pl.BlockSpec(made.shape, lambda *_, n=len(made.shape): (0,) * n) for made in comm.out_shapes
        ]
        scratch += comm.scratch
    return pl.pallas_call(
        kernel,
        grid=grid,
        in_specs=in_specs,
        out_specs=out_specs,
        out_shape=out_shape,
        scratch_shapes=scratch,
        compiler_params=pltpu.CompilerParams(
            vmem_limit_bytes=VMEM_LIMIT,
            collective_id=None if comm is None else collective_id,
            has_side_effects=comm is not None,
        ),
    )(*arrays)


def flat(*_):
    return (0, 0)


def column(c):
    return lambda *_: (0, c)


def rows_of(i, *_):
    return (i, 0)


def front_kernel(
    lat_ref, tok_ref, bias_ref, gain_ref, wq_ref, wkv_ref, wout_ref, wup_ref, wdown_ref, wqkv_ref,
    x1_ref, x2_ref, q_ref, p_ref, o_ref, kv_ref, q2_ref, k2_ref, v2_ref,
):
    @pl.when(pl.program_id(0) == 0)
    def _():
        unit, _ = normed(tok_ref[...].astype(F32))
        kv_ref[...] = low(dot(low(unit * gain_ref[1:2, :]), wkv_ref[...]))

    x = lat_ref[...].astype(F32)
    unit, _ = normed(x)
    q = low(dot(low(unit * gain_ref[0:1, :]), wq_ref[...]))
    q_ref[...] = q
    s = dot_nt(q, kv_ref[:, :D]) * CROSS_SCALE + bias_ref[...]
    e = jnp.exp(s - jnp.max(s, axis=1, keepdims=True))
    p = low(e / jnp.sum(e, axis=1, keepdims=True))
    p_ref[...] = p
    o = low(dot(p, kv_ref[:, D:]))
    o_ref[...] = o
    x1 = x + dot(o, wout_ref[...])
    x1_ref[...] = x1
    unit, _ = normed(x1)
    m1 = low(unit * gain_ref[2:3, :])
    total = x1
    for c in range(FF // FF_STEP):
        cols = slice(c * FF_STEP, (c + 1) * FF_STEP)
        h = low(gelu(dot(m1, wup_ref[:, cols])))
        total = total + dot(h, wdown_ref[cols, :])
    x2_ref[...] = total
    unit, _ = normed(total)
    bn = low(unit * gain_ref[3:4, :])
    q2_ref[...] = low(dot(bn, wqkv_ref[:, :D])) * SELF_SCALE
    k2_ref[...] = low(dot(bn, wqkv_ref[:, D : 2 * D]))
    v2_ref[...] = low(dot(bn, wqkv_ref[:, 2 * D :]))


def front(latents, window, bias, gains, wide, tall):
    rows, span = latents.shape[0], window.shape[0]
    block = min(rows, 512)
    r = (block, D)
    return call(
        front_kernel,
        (rows // block,),
        [
            (latents, r, rows_of),
            (window, (span, D), flat),
            (bias, (1, span), flat),
            (gains, (8, D), flat),
            (wide, (D, D), column(2)),
            (wide, (D, 2 * D), column(0)),
            (wide, (D, D), column(3)),
            (wide, (D, FF), column(1)),
            (tall, (FF, D), column(0)),
            (wide, (D, 3 * D), column(3)),
        ],
        [
            ((rows, D), F32, r, rows_of),
            ((rows, D), F32, r, rows_of),
            ((rows, D), BF16, r, rows_of),
            ((rows, span), BF16, (block, span), rows_of),
            ((rows, D), BF16, r, rows_of),
            ((span, 2 * D), BF16, (span, 2 * D), flat),
            ((rows, D), BF16, r, rows_of),
            ((rows, D), BF16, r, rows_of),
            ((rows, D), BF16, r, rows_of),
        ],
    )


def lane_is(shape, head):
    lane = lax.broadcasted_iota(jnp.int32, shape, 1)
    return (lane < HEAD) if head == 0 else (lane >= HEAD)


def only(value, head):
    return jnp.where(lane_is(value.shape, head), value, jnp.zeros_like(value))


def self_forward_kernel(parts, q_ref, *refs):
    k_refs, v_refs = refs[:parts], refs[parts : 2 * parts]
    o_ref, p_ref, scale_ref = refs[2 * parts : 2 * parts + 3]
    ones_refs = refs[2 * parts + 3 :]

    @pl.when(pl.program_id(1) == 0)
    def _():
        for v_ref, ones_ref in zip(v_refs, ones_refs):
            v = v_ref[...]
            for head in range(2):
                ones_ref[head] = jnp.where(lane_is(v.shape, head), v, jnp.ones_like(v))

    q = q_ref[...]
    outs, scales = [], []
    for head in range(2):
        scores = [dot_nt(only(q, head), k_ref[...]) for k_ref in k_refs]
        top = functools.reduce(jnp.maximum, [jnp.max(s, axis=1, keepdims=True) for s in scores])
        mixed, first = None, 0
        for s, ones_ref in zip(scores, ones_refs):
            p = low(jnp.exp(s - top))
            p_ref[head, :, first : first + p.shape[1]] = p
            first += p.shape[1]
            term = dot(p, ones_ref[head])
            mixed = term if mixed is None else mixed + term
        scales.append(1.0 / pltpu.roll(mixed, HEAD, 1))
        outs.append(mixed * scales[-1])
    left = lane_is(outs[0].shape, 0)
    o_ref[...] = low(jnp.where(left, outs[0], outs[1]))
    scale_ref[...] = jnp.where(left, scales[0], scales[1])


def self_forward(q2, keys, values):
    rows = q2.shape[0]
    block = min(rows, 256)
    parts = len(keys)
    total = sum(k.shape[0] for k in keys)
    whole = lambda array: (array, (array.shape[0], LANES), lambda p, i: (0, p))
    return call(
        functools.partial(self_forward_kernel, parts),
        (PAIRS, rows // block),
        [(q2, (block, LANES), lambda p, i: (i, p))]
        + [whole(k) for k in keys]
        + [whole(v) for v in values],
        [
            ((rows, D), BF16, (block, LANES), lambda p, i: (i, p)),
            ((HEADS, rows, total), BF16, (2, block, total), lambda p, i: (p, i, 0)),
            ((rows, D), F32, (block, LANES), lambda p, i: (i, p)),
        ],
        [pltpu.VMEM((2, k.shape[0], LANES), BF16) for k in keys],
    )


def run_beside(comm, point, plan, odd):
    for when, work in plan.items():
        if when % 2 != odd:
            continue
        def run(when=when, work=work):
            if when == 0:
                comm.here.greet()
            for name, k in work:
                getattr(comm, name)(k)
        pl.when(point == when)(run)


SELF_PLAN = {
    0: (("start", 0), ("start", 1), ("start", 2)),
    4: (("in_chip", 0),),
    6: (("in_chip", 1),),
    7: (("in_chip", 2),),
    10: (("in_pairs", 0),),
    15: (("in_pairs", 1),),
    16: (("in_pairs", 2),),
    18: (("in_plane", 0),),
    20: (("in_plane", 1), ("turn0", 0)),
    21: (("in_plane", 2),),
    22: (("turn1", 0), ("turn0", 1)),
    24: (("turn2", 0), ("turn1", 1), ("turn0", 2)),
    26: (("in_line", 0), ("turn2", 1), ("turn1", 2)),
    28: (("in_line", 1), ("turn2", 2)),
    30: (("in_line", 2),),
    31: (("end", 0), ("end", 1), ("end", 2)),
}
FIRST_PLAN = {
    0: (("start", 0),),
    2: (("in_chip", 0),),
    4: (("in_pairs", 0),),
    5: (("in_plane", 0),),
    6: (("turn0", 0), ("turn1", 0)),
    7: (("turn2", 0), ("in_line", 0), ("end", 0)),
}


def self_backward_kernel(parts, steps, comm, q_ref, do_ref, o_ref, scale_ref, p_ref, *refs):
    if comm is not None:
        n_in, n_out, n_scratch = len(comm.inputs), len(comm.out_shapes), len(comm.scratch)
        outs = 2 * parts + n_in
        comm.bind(
            refs[2 * parts : outs],
            refs[outs + 1 + 2 * parts : outs + 1 + 2 * parts + n_out],
            refs[len(refs) - n_scratch :],
        )
        refs = refs[: 2 * parts] + refs[outs : outs + 1 + 2 * parts] + refs[
            outs + 1 + 2 * parts + n_out : len(refs) - n_scratch
        ]
    k_refs, v_refs = refs[:parts], refs[parts : 2 * parts]
    dq_ref = refs[2 * parts]
    dk_refs = refs[2 * parts + 1 : 3 * parts + 1]
    dv_refs = refs[3 * parts + 1 : 4 * parts + 1]
    dk_sums, dv_sums = refs[4 * parts + 1 : 5 * parts + 1], refs[5 * parts + 1 :]
    pair, step = pl.program_id(0), pl.program_id(1)

    @pl.when(step == 0)
    def _():
        for ref in (*dk_sums, *dv_sums):
            ref[...] = jnp.zeros_like(ref)

    if comm is not None:
        run_beside(comm, 2 * (pair * steps + step), SELF_PLAN, 0)

    q = q_ref[...]
    do = low(do_ref[...].astype(F32) * scale_ref[...])
    product = do.astype(F32) * o_ref[...].astype(F32)
    q_turned, do_turned = jnp.transpose(q), jnp.transpose(do)
    dqs = []
    for head in range(2):
        rows = slice(head * HEAD, (head + 1) * HEAD)
        doz = only(do, head)
        delta = jnp.sum(only(product, head), axis=1, keepdims=True)
        dq, first = None, 0
        for k_ref, v_ref, dk_sum, dv_sum in zip(k_refs, v_refs, dk_sums, dv_sums):
            count = k_ref.shape[0]
            p = p_ref[head, :, first : first + count]
            first += count
            ds = low(p.astype(F32) * (dot_nt(doz, v_ref[...]) - delta))
            dv_sum[rows, :] += dot(do_turned[rows], p)
            dk_sum[rows, :] += dot(q_turned[rows], ds)
            term = dot(ds, k_ref[...])
            dq = term if dq is None else dq + term
        dqs.append(dq)
    dq_ref[...] = low(jnp.where(lane_is(dqs[0].shape, 0), dqs[0], dqs[1]) * SELF_SCALE)

    @pl.when(step == steps - 1)
    def _():
        for ref, total in zip((*dk_refs, *dv_refs), (*dk_sums, *dv_sums)):
            ref[...] = jnp.transpose(low(total[...]))

    if comm is not None:
        run_beside(comm, 2 * (pair * steps + step) + 1, SELF_PLAN, 1)


def self_backward(q2, do2, o2, scale2, p2, keys, values, comm=None):
    rows = q2.shape[0]
    block = min(rows, 256)
    parts = len(keys)
    whole = lambda array: (array, (array.shape[0], LANES), lambda p, i: (0, p))
    made = lambda array: (array.shape, BF16, (array.shape[0], LANES), lambda p, i: (0, p))
    out = call(
        functools.partial(self_backward_kernel, parts, rows // block, comm),
        (PAIRS, rows // block),
        [
            (q2, (block, LANES), lambda p, i: (i, p)),
            (do2, (block, LANES), lambda p, i: (i, p)),
            (o2, (block, LANES), lambda p, i: (i, p)),
            (scale2, (block, LANES), lambda p, i: (i, p)),
            (p2, (2, block, p2.shape[2]), lambda p, i: (p, i, 0)),
        ]
        + [whole(k) for k in keys]
        + [whole(v) for v in values],
        [((rows, D), BF16, (block, LANES), lambda p, i: (i, p))]
        + [made(k) for k in keys]
        + [made(v) for v in values],
        [pltpu.VMEM((LANES, k.shape[0]), F32) for k in (*keys, *values)],
        comm=comm,
        collective_id=1,
    )
    return out[0], out[1 : 1 + parts], out[1 + parts : 1 + 2 * parts], out[1 + 2 * parts :]


def second_kernel(
    steps, x2_ref, o2_ref, og_ref, gain_ref, wso_ref, wup_ref, wdown_ref,
    out_ref, g3_ref, do_ref, dwup_ref, dwdown_ref, dwso_ref, dgain_ref,
    m_ref, f_ref, dm_ref,
):
    c = pl.program_id(0)

    @pl.when(c == 0)
    def _():
        x3 = x2_ref[...] + dot(o2_ref[...], wso_ref[...])
        unit, _ = normed(x3)
        m_ref[...] = low(unit * gain_ref[4:5, :])
        out_ref[...] = x3
        f_ref[...] = jnp.zeros_like(f_ref)
        dm_ref[...] = jnp.zeros_like(dm_ref)

    m, og = m_ref[...], og_ref[...]
    h, slope = gelu_both(dot(m, wup_ref[...]))
    h = low(h)
    f_ref[...] += dot(h, wdown_ref[...])
    dwdown_ref[...] = low(dot_tn(h, og))
    du = low(slope * dot_nt(og, wdown_ref[...]))
    dwup_ref[...] = low(dot_tn(m, du))
    dm_ref[...] += dot_nt(du, wup_ref[...])

    @pl.when(c == steps - 1)
    def _():
        x3 = out_ref[...]
        unit, factor = normed(x3)
        out_ref[...] = x3 + f_ref[...]
        back, dgain = norm_back(dm_ref[...], unit, factor, gain_ref[4:5, :])
        g3 = og_ref[...].astype(F32) + back
        g3_ref[...] = g3
        dgain_ref[...] = jnp.broadcast_to(dgain, dgain_ref.shape)
        b3 = low(g3)
        o2 = o2_ref[...]
        dwso_ref[...] = low(dot_tn(o2, b3))
        do_ref[...] = low(dot_nt(b3, wso_ref[...]))


def second(x2, o2, og, gains, wide, tall):
    rows = x2.shape[0]
    steps = FF // FF_STEP
    r = (rows, D)
    return call(
        functools.partial(second_kernel, steps),
        (steps,),
        [
            (x2, r, flat),
            (o2, r, flat),
            (og, r, flat),
            (gains, (8, D), flat),
            (wide, (D, D), column(8)),
            (wide, (D, FF_STEP), lambda c: (0, 3 * FF // FF_STEP + c)),
            (tall, (FF_STEP, D), lambda c: (c, 1)),
        ],
        [
            (r, F32, r, flat),
            (r, F32, r, flat),
            (r, BF16, r, flat),
            ((D, FF), BF16, (D, FF_STEP), lambda c: (0, c)),
            ((FF, D), BF16, (FF_STEP, D), lambda c: (c, 0)),
            ((D, D), BF16, (D, D), flat),
            ((8, D), F32, (8, D), flat),
        ],
        [pltpu.VMEM(r, BF16), pltpu.VMEM(r, F32), pltpu.VMEM(r, F32)],
    )


def qkv_back_kernel(
    x2_ref, g3_ref, dq_ref, dk_ref, dk_more_ref, dv_ref, dv_more_ref, gain_ref, w_ref,
    g2_ref, dw_ref, dgain_ref,
):
    unit, factor = normed(x2_ref[...])
    gain = gain_ref[3:4, :]
    bn = low(unit * gain)
    dq = dq_ref[...]
    dk = low(dk_ref[...].astype(F32) + dk_more_ref[...].astype(F32))
    dv = low(dv_ref[...].astype(F32) + dv_more_ref[...].astype(F32))
    dbn = None
    for i, part in enumerate((dq, dk, dv)):
        cols = slice(i * D, (i + 1) * D)
        dw_ref[:, cols] = low(dot_tn(bn, part))
        term = dot_nt(part, w_ref[:, cols])
        dbn = term if dbn is None else dbn + term
    back, dgain = norm_back(dbn, unit, factor, gain)
    g2_ref[...] = g3_ref[...] + back
    dgain_ref[...] = jnp.broadcast_to(dgain, dgain_ref.shape)


def qkv_back(x2, g3, dq, dk, dk_more, dv, dv_more, gains, wide):
    rows = x2.shape[0]
    r = (rows, D)
    return call(
        qkv_back_kernel,
        (1,),
        [(a, r, flat) for a in (x2, g3, dq, dk, dk_more, dv, dv_more)]
        + [(gains, (8, D), flat), (wide, (D, 3 * D), column(3))],
        [
            (r, F32, r, flat),
            ((D, 3 * D), BF16, (D, 3 * D), flat),
            ((8, D), F32, (8, D), flat),
        ],
    )


def first_back_kernel(steps, comm, x1_ref, g2_ref, o_ref, gain_ref, wout_ref, wup_ref, wdown_ref, *refs):
    c = pl.program_id(0)
    if comm is not None:
        n_in, n_out = len(comm.inputs), len(comm.out_shapes)
        comm.bind(refs[:n_in], refs[n_in + 6 : n_in + 6 + n_out], refs[n_in + 9 + n_out :])
        refs = refs[n_in : n_in + 6] + refs[n_in + 6 + n_out : n_in + 9 + n_out]
        run_beside(comm, 2 * c, FIRST_PLAN, 0)
    g1_ref, do_ref, dwup_ref, dwdown_ref, dwout_ref, dgain_ref, m_ref, b_ref, dm_ref = refs

    @pl.when(c == 0)
    def _():
        unit, _ = normed(x1_ref[...])
        m_ref[...] = low(unit * gain_ref[2:3, :])
        b_ref[...] = low(g2_ref[...])
        dm_ref[...] = jnp.zeros_like(dm_ref)

    m, b = m_ref[...], b_ref[...]
    h, slope = gelu_both(dot(m, wup_ref[...]))
    dwdown_ref[...] = low(dot_tn(low(h), b))
    du = low(slope * dot_nt(b, wdown_ref[...]))
    dwup_ref[...] = low(dot_tn(m, du))
    dm_ref[...] += dot_nt(du, wup_ref[...])

    @pl.when(c == steps - 1)
    def _():
        unit, factor = normed(x1_ref[...])
        back, dgain = norm_back(dm_ref[...], unit, factor, gain_ref[2:3, :])
        g1 = g2_ref[...] + back
        g1_ref[...] = g1
        dgain_ref[...] = jnp.broadcast_to(dgain, dgain_ref.shape)
        b1 = low(g1)
        dwout_ref[...] = low(dot_tn(o_ref[...], b1))
        do_ref[...] = low(dot_nt(b1, wout_ref[...]))

    if comm is not None:
        run_beside(comm, 2 * c + 1, FIRST_PLAN, 1)


def first_back(x1, g2, o, gains, wide, tall, comm=None):
    rows = x1.shape[0]
    steps = FF // FF_STEP
    r = (rows, D)
    return call(
        functools.partial(first_back_kernel, steps, comm),
        (steps,),
        [
            (x1, r, flat),
            (g2, r, flat),
            (o, r, flat),
            (gains, (8, D), flat),
            (wide, (D, D), column(3)),
            (wide, (D, FF_STEP), lambda c: (0, FF // FF_STEP + c)),
            (tall, (FF_STEP, D), lambda c: (c, 0)),
        ],
        [
            (r, F32, r, flat),
            (r, BF16, r, flat),
            ((D, FF), BF16, (D, FF_STEP), lambda c: (0, c)),
            ((FF, D), BF16, (FF_STEP, D), lambda c: (c, 0)),
            ((D, D), BF16, (D, D), flat),
            ((8, D), F32, (8, D), flat),
        ],
        [pltpu.VMEM(r, BF16), pltpu.VMEM(r, BF16), pltpu.VMEM(r, F32)],
        comm=comm,
        collective_id=3,
    )


def cross_back_kernel(
    steps, lat_ref, g1_ref, do_ref, p_ref, q_ref, kv_ref, gain_ref, wq_ref,
    lg_ref, dwq_ref, dkv_ref, dgain_ref, dk_sum, dv_sum, dwq_sum,
):
    i = pl.program_id(0)

    @pl.when(i == 0)
    def _():
        for ref in (dk_sum, dv_sum, dwq_sum, dgain_ref):
            ref[...] = jnp.zeros_like(ref)

    p, do, q = p_ref[...], do_ref[...], q_ref[...]
    dp = dot_nt(do, kv_ref[:, D:])
    wide_p = p.astype(F32)
    ds = low(wide_p * (dp - jnp.sum(wide_p * dp, axis=1, keepdims=True)))
    dq = low(dot(ds, kv_ref[:, :D]) * CROSS_SCALE)
    dk_sum[...] += dot_tn(ds, q)
    dv_sum[...] += dot_tn(p, do)
    unit, factor = normed(lat_ref[...].astype(F32))
    gain = gain_ref[0:1, :]
    dwq_sum[...] += dot_tn(low(unit * gain), dq)
    back, dgain = norm_back(dot_nt(dq, wq_ref[...]), unit, factor, gain)
    lg_ref[...] = g1_ref[...] + back
    dgain_ref[...] += jnp.broadcast_to(dgain, dgain_ref.shape)

    @pl.when(i == steps - 1)
    def _():
        dwq_ref[...] = low(dwq_sum[...])
        dkv_ref[:, :D] = low(dk_sum[...] * CROSS_SCALE)
        dkv_ref[:, D:] = low(dv_sum[...])


def cross_back(latents, g1, do, p, q, kv, gains, wide):
    rows, span = p.shape
    block = min(rows, 512)
    r = (block, D)
    return call(
        functools.partial(cross_back_kernel, rows // block),
        (rows // block,),
        [
            (latents, r, rows_of),
            (g1, r, rows_of),
            (do, r, rows_of),
            (p, (block, span), rows_of),
            (q, r, rows_of),
            (kv, (span, 2 * D), flat),
            (gains, (8, D), flat),
            (wide, (D, D), column(2)),
        ],
        [
            ((rows, D), F32, r, rows_of),
            ((D, D), BF16, (D, D), flat),
            ((span, 2 * D), BF16, (span, 2 * D), flat),
            ((8, D), F32, (8, D), flat),
        ],
        [pltpu.VMEM((span, D), F32), pltpu.VMEM((span, D), F32), pltpu.VMEM((D, D), F32)],
    )


def token_back_kernel(tok_ref, dkv_ref, more_ref, gain_ref, w_ref, tg_ref, dw_ref, dgain_ref):
    unit, factor = normed(tok_ref[...].astype(F32))
    gain = gain_ref[1:2, :]
    dkv = low(dkv_ref[...].astype(F32) + more_ref[...].astype(F32))
    dw_ref[...] = low(dot_tn(low(unit * gain), dkv))
    back, dgain = norm_back(dot_nt(dkv, w_ref[...]), unit, factor, gain)
    tg_ref[...] = low(back)
    dgain_ref[...] = jnp.broadcast_to(dgain, dgain_ref.shape)


def token_back(tokens, dkv, more, gains, wide):
    rows = tokens.shape[0]
    return call(
        token_back_kernel,
        (1,),
        [
            (tokens, (rows, D), flat),
            (dkv, (rows, 2 * D), flat),
            (more, (rows, 2 * D), flat),
            (gains, (8, D), flat),
            (wide, (D, 2 * D), column(0)),
        ],
        [
            ((rows, D), BF16, (rows, D), flat),
            ((D, 2 * D), BF16, (D, 2 * D), flat),
            ((8, D), F32, (8, D), flat),
        ],
    )


MESH = pl.DeviceIdType.MESH
UP, DOWN = 0, 1


class Place:
    def __init__(self):
        row, lat = lax.axis_index("row"), lax.axis_index("lat")
        self.x, self.y, self.z, self.c = row % 2, row // 2, lat // 2, lat % 2
        self.r = row
        self.rx = self.y * 2 + 1 - self.x
        self.ry = (1 - self.y) * 2 + self.x
        self.rd = (1 - self.y) * 2 + 1 - self.x
        self.to_x, self.to_y = (self.rx, lat), (self.ry, lat)
        self.to_core = (row, self.z * 2 + 1 - self.c)
        self.to_z = ((row, lat + 2), (row, lat - 2))
        self.more = (self.z < 3, self.z > 0)

    def greet(self):
        barrier = pltpu.get_barrier_semaphore()
        for device in (self.to_x, self.to_y, self.to_core):
            pl.semaphore_signal(barrier, inc=1, device_id=device, device_id_type=MESH)
        for way in (UP, DOWN):
            @pl.when(self.more[way])
            def _():
                pl.semaphore_signal(barrier, inc=1, device_id=self.to_z[way], device_id_type=MESH)
        pl.semaphore_wait(barrier, 3 + jnp.minimum(self.z, 1) + jnp.minimum(3 - self.z, 1))

    def source(self, way, hop):
        return (self.z - hop, self.z >= hop) if way == UP else (self.z + hop, self.z + hop <= 3)


def send(src, dst, sems, index, device):
    return pltpu.make_async_remote_copy(
        src_ref=src, dst_ref=dst, send_sem=sems[0].at[index], recv_sem=sems[1].at[index],
        device_id=device, device_id_type=MESH,
    )


def sem_pair(*shape):
    return [pltpu.SemaphoreType.DMA(shape), pltpu.SemaphoreType.DMA(shape)]


WIDE_STEP = 2048
NARROW_STEP = 512
TOKEN_PARTS = 4
AHEAD = 2
GAP = 2
CHUNKS = (
    (3, 0, 16),
    (0, 0, WIDE_STEP),
    (0, WIDE_STEP, WIDE_STEP),
    (1, 0, NARROW_STEP),
    (0, 2 * WIDE_STEP, WIDE_STEP),
    (0, 3 * WIDE_STEP, WIDE_STEP),
    (1, NARROW_STEP, NARROW_STEP),
) + tuple((2, part, TOKEN_PARTS) for part in range(TOKEN_PARTS))


def gather_kernel(counts, *refs):
    n_wide, n_tall = counts
    n_in = 2 + n_wide + n_tall
    tok_ref, meta_ref = refs[:2]
    shards = (refs[2 : 2 + n_wide], refs[2 + n_wide : n_in])
    tok_all, meta_all, wide_all, tall_all = refs[n_in : n_in + 4]
    sems = refs[n_in + 4 :]
    local_sem, z_sems, p_sems, q_sems, c_sems = sems[0], sems[1:3], sems[3:5], sems[5:7], sems[7:9]
    here = Place()
    z, c, r = here.z, here.c, here.r
    full = (wide_all, tall_all, tok_all, meta_all)
    total = len(CHUNKS)

    def block(k, source, core=None):
        which, first, width = CHUNKS[k]
        core = c if core is None else core
        if which == 3:
            return meta_all.at[source, core]
        if which == 2:
            rows = tok_all.shape[2] // width
            return tok_all.at[source, core, pl.ds(first * rows, rows)]
        return full[which].at[source, core, :, :, pl.ds(first, width)]

    def piece(k, source, quarter, half=None):
        which, first, width = CHUNKS[k]
        if which >= 2:
            return block(k, source)
        if half is not None:
            first, width = first + half * (width // 2), width // 2
        return full[which].at[source, c, quarter, :, pl.ds(first, width)]

    def shared(k):
        return CHUNKS[k][0] < 2

    here.greet()
    copies = [pltpu.make_async_copy(tok_ref, tok_all.at[z, c], local_sem.at[0]),
              pltpu.make_async_copy(meta_ref, meta_all.at[z, c], local_sem.at[1])]
    for which in (0, 1):
        first = 0
        for shard in shards[which]:
            width = shard.shape[-1]
            copies.append(pltpu.make_async_copy(
                shard, full[which].at[z, c, :, :, pl.ds(first, width)], local_sem.at[len(copies)]))
            first += width
    for copy in copies:
        copy.start()
    for copy in copies:
        copy.wait()

    def z_send(k, way, hop):
        source, _ = here.source(way, hop - 1)
        ref = piece(k, source, r)
        return send(ref, ref, z_sems, (k, way, hop - 1), here.to_z[way])

    def z_recv(k, way, hop):
        source, _ = here.source(way, hop)
        ref = piece(k, source, r)
        return send(ref, ref, z_sems, (k, way, hop - 1), here.to_z[way])

    def p_send(k, way, hop, axis):
        source, _ = here.source(way, hop)
        ref = piece(k, source, r)
        return send(ref, ref, p_sems, (k, way, hop - 1, axis), (here.to_x, here.to_y)[axis])

    def p_recv(k, way, hop, axis):
        source, _ = here.source(way, hop)
        ref = piece(k, source, (here.rx, here.ry)[axis])
        return send(ref, ref, p_sems, (k, way, hop - 1, axis), (here.to_x, here.to_y)[axis])

    def q_send(k, way, hop, half):
        source, _ = here.source(way, hop)
        ref = piece(k, source, (here.rx, here.ry)[half], half)
        return send(ref, ref, q_sems, (k, way, hop - 1, half), (here.to_y, here.to_x)[half])

    def q_recv(k, way, hop, half):
        source, _ = here.source(way, hop)
        ref = piece(k, source, here.rd, half)
        return send(ref, ref, q_sems, (k, way, hop - 1, half), (here.to_y, here.to_x)[half])

    def c_copy(k, source, index, mine):
        ref = block(k, source, c if mine else 1 - c)
        return send(ref, ref, c_sems, (k, index), here.to_core)

    def ways(hop, fn):
        for way in (UP, DOWN):
            source, valid = here.source(way, hop)
            pl.when(valid)(functools.partial(fn, way, hop, source))

    def index_of(way, hop):
        return 1 + way * 3 + hop - 1

    def first_sends(k):
        for way in (UP, DOWN):
            pl.when(here.more[way])(lambda way=way: z_send(k, way, 1).start())
        c_copy(k, z, 0, True).start()

    def stage_z(k, hop):
        def arrive(way, hop, source):
            z_recv(k, way, hop).wait_recv()
            if hop < 3:
                pl.when(here.more[way])(lambda: z_send(k, way, hop + 1).start())
            if shared(k):
                p_send(k, way, hop, 0).start()
                p_send(k, way, hop, 1).start()
            else:
                c_copy(k, source, index_of(way, hop), True).start()
        ways(hop, arrive)

    def stage_p(k, hop):
        def arrive(way, hop, source):
            for axis in (0, 1):
                p_recv(k, way, hop, axis).wait_recv()
                q_send(k, way, hop, axis).start()
        ways(hop, arrive)

    def stage_q(k, hop):
        def arrive(way, hop, source):
            q_recv(k, way, hop, 0).wait_recv()
            q_recv(k, way, hop, 1).wait_recv()
            c_copy(k, source, index_of(way, hop), True).start()
        ways(hop, arrive)

    for k in range(AHEAD):
        first_sends(k)
    for step in range(total + 4 * GAP + 1):
        if step + AHEAD < total:
            first_sends(step + AHEAD)
        for lag, stage in ((0, stage_z), (GAP, stage_p), (2 * GAP, stage_q)):
            for hop in (1, 2, 3):
                k = step - lag - GAP * (hop - 1)
                if 0 <= k < total and (lag == 0 or shared(k)):
                    stage(k, hop)
    for k in range(total):
        for way in (UP, DOWN):
            for hop in (1, 2, 3):
                source, valid = here.source(way, hop - 1)
                pl.when(valid & here.more[way])(lambda k=k, way=way, hop=hop: z_send(k, way, hop).wait_send())
        c_copy(k, z, 0, True).wait_send()
        c_copy(k, z, 0, False).wait_recv()

        def finish(way, hop, source):
            c_copy(k, source, index_of(way, hop), True).wait_send()
            c_copy(k, source, index_of(way, hop), False).wait_recv()
            if shared(k):
                for axis in (0, 1):
                    p_send(k, way, hop, axis).wait_send()
                    q_send(k, way, hop, axis).wait_send()
        for hop in (1, 2, 3):
            ways(hop, finish)


def gather_all(tokens, meta, wide_shards, tall_shards):
    anywhere = pl.BlockSpec(memory_space=pl.ANY)
    slots = tokens.shape[0]
    wide_shards = [w.reshape(4, w.shape[0] // 4, w.shape[1]) for w in wide_shards]
    tall_shards = [w.reshape(4, w.shape[0] // 4, w.shape[1]) for w in tall_shards]
    wide_cols = sum(w.shape[-1] for w in wide_shards)
    tall_cols = sum(w.shape[-1] for w in tall_shards)
    total = len(CHUNKS)
    inputs = [tokens, meta, *wide_shards, *tall_shards]
    tok_all, meta_all, wide, tall = pl.pallas_call(
        functools.partial(gather_kernel, (len(wide_shards), len(tall_shards))),
        in_specs=[pl.BlockSpec(memory_space=pltpu.VMEM)] * len(inputs),
        out_specs=[anywhere] * 4,
        out_shape=[
            jax.ShapeDtypeStruct((4, 2) + tokens.shape, BF16),
            jax.ShapeDtypeStruct((4, 2) + meta.shape, BF16),
            jax.ShapeDtypeStruct((4, 2) + wide_shards[0].shape[:2] + (wide_cols,), BF16),
            jax.ShapeDtypeStruct((4, 2) + tall_shards[0].shape[:2] + (tall_cols,), BF16),
        ],
        scratch_shapes=[pltpu.SemaphoreType.DMA((len(inputs),))]
        + sem_pair(total, 2, 3)
        + sem_pair(total, 2, 3, 2)
        + sem_pair(total, 2, 3, 2)
        + sem_pair(total, 7),
        compiler_params=pltpu.CompilerParams(collective_id=0, has_side_effects=True),
    )(*inputs)
    return (
        tok_all.reshape(8 * slots, D),
        meta_all.reshape(8, meta.shape[0], meta.shape[1]),
        wide.reshape(-1, wide_cols),
        tall.reshape(-1, tall_cols),
    )


class Peers(Place):
    def __init__(self):
        super().__init__()
        lat = lax.axis_index("lat")
        self.plane = (self.to_x, self.to_y, (self.rd, lat))
        self.quarters = (self.rx, self.ry, self.rd)
        self.above = [lax.rem(self.z + 1 + i, 4) for i in range(3)]
        self.line = [(self.r, z * 2 + self.c) for z in self.above]

    def greet(self):
        barrier = pltpu.get_barrier_semaphore()
        others = (self.to_core, *self.plane, *self.line)
        for device in others:
            pl.semaphore_signal(barrier, inc=1, device_id=device, device_id_type=MESH)
        pl.semaphore_wait(barrier, len(others))


LINE = (
    ((1, UP, 3), (2, DOWN, 0)),
    ((1, UP, 2), (2, DOWN, 1), (2, UP, 3), (1, DOWN, 0)),
    ((1, UP, 1), (2, DOWN, 2), (2, UP, 2), (1, DOWN, 1)),
    ((3, UP, 3), (0, DOWN, 0)),
)


class LineSum:
    def __init__(self, here, block, arrived, sems):
        self.here, self.block, self.arrived, self.sems = here, block, arrived, sems

    def copy(self, way, dest):
        index = (way, dest - 1 if way == UP else dest)
        return send(self.block(dest), self.arrived.at[index], [s for s in self.sems], index, self.here.to_z[way])

    def start(self):
        @pl.when(self.here.z == 0)
        def _():
            for dest in (3, 2, 1):
                self.copy(UP, dest).start()

        @pl.when(self.here.z == 3)
        def _():
            for dest in (0, 1, 2):
                self.copy(DOWN, dest).start()

    def turn(self, group):
        for device, way, dest in LINE[group]:
            @pl.when(self.here.z == device)
            def _(device=device, way=way, dest=dest):
                self.copy(way, dest).wait_recv()
                ref = self.block(dest)
                ref[...] = ref[...] + self.arrived[way, dest - 1 if way == UP else dest]
                if dest != device:
                    self.copy(way, dest).start()

    def finish(self):
        for dest in (1, 2, 3):
            pl.when(self.here.z < dest)(lambda dest=dest: self.copy(UP, dest).wait_send())
        for dest in (0, 1, 2):
            pl.when(self.here.z > dest)(lambda dest=dest: self.copy(DOWN, dest).wait_send())


class Staged:
    def __init__(self, rows, cols):
        self.shape = (rows, cols)


class WeightSum:
    def __init__(self, chunks, gains=None, tokens=None):
        self.chunks, self.inputs, self.scratch, self.staged = [], [], [], []
        self.sources = 0
        for chunk in chunks:
            parts = []
            for array in chunk:
                shape = (4, 2, 4, array.shape[0] // 32, array.shape[1])
                if isinstance(array, Staged):
                    parts.append((self.sources, None, len(self.staged), shape[-1]))
                    self.staged.append(pltpu.VMEM(shape, BF16))
                else:
                    parts.append((self.sources, len(self.inputs), None, shape[-1]))
                    self.inputs.append(array.reshape(shape))
                self.sources += 1
            self.chunks.append((parts, shape[3], sum(part[3] for part in parts)))
        self.out_shapes = [
            jax.ShapeDtypeStruct((4, rows, cols), BF16) for _, rows, cols in self.chunks
        ]
        for _, rows, cols in self.chunks:
            half = cols // 2
            self.scratch += [
                pltpu.VMEM((4, 2, 2, rows, cols), BF16),
                pltpu.VMEM((4, 2, 2, rows, cols), BF16),
                pltpu.VMEM((2, 4, 2, rows, half), BF16),
                pltpu.VMEM((2, 4, rows, half), BF16),
                pltpu.VMEM((2, 3, rows, cols), BF16),
                pltpu.VMEM((4, rows, cols), BF16),
            ]
        n = len(self.chunks)
        self.scratch += self.staged
        self.scratch += [pltpu.SemaphoreType.DMA((self.sources, 2))]
        for shape in ((self.sources, 2), (n, 2), (n, 2), (n, 2, 3), (n, 3)):
            self.scratch += sem_pair(*shape)
        self.gains, self.tokens = gains, tokens
        if gains is not None:
            self.out_shapes.append(jax.ShapeDtypeStruct(gains, F32))
            self.scratch += [pltpu.VMEM(shape + gains, F32) for shape in ((), (), (4,), (3,))]
            self.scratch += sem_pair(1) + sem_pair(3) + sem_pair(3)
        if tokens is not None:
            self.out_shapes.append(jax.ShapeDtypeStruct((tokens // 8, D), F32))
            self.scratch += [pltpu.VMEM((4, tokens // 8, D), BF16)]
            self.scratch += [pltpu.VMEM((2, tokens // 8, D), BF16)]
            self.scratch += [pltpu.VMEM((2, 3, tokens // 8, D), BF16)]
            self.scratch += sem_pair(1) + sem_pair(2, 3)

    def bind(self, ins, outs, scratch):
        self.here = Peers()
        self.ins, self.outs = ins, outs
        scratch = list(scratch)
        take = lambda n: [scratch.pop(0) for _ in range(n)]
        self.buffers = [take(6) for _ in self.chunks]
        self.stages = take(len(self.staged))
        self.local = take(1)[0]
        self.c_sems, self.x_sems, self.y_sems, self.z_sems, self.g_sems = (take(2) for _ in range(5))
        if self.gains is not None:
            self.gain_buffers = take(4)
            self.gain_sems = [take(2) for _ in range(3)]
        if self.tokens is not None:
            self.token_mine, self.token_window, arrived = take(3)
            self.token_sems = take(2)
            self.token_line = LineSum(self.here, lambda z: self.token_mine.at[z], arrived, take(2))


    def parts(self, k):
        first = 0
        for source, given, staged, width in self.chunks[k][0]:
            ref = self.stages[staged] if given is None else self.ins[given]
            yield source, ref, pl.ds(first, width)
            first += width

    def halves(self, k):
        half = self.chunks[k][2] // 2
        return pl.ds(0, half), pl.ds(half, half)

    def own(self, k):
        for source, ref, cols in self.parts(k):
            for y in range(2):
                yield pltpu.make_async_copy(
                    ref.at[:, self.here.c, pl.ds(2 * y, 2)],
                    self.buffers[k][0].at[:, y, :, :, cols],
                    self.local.at[source, y],
                )

    def to_core(self, k):
        for source, ref, cols in self.parts(k):
            for y in range(2):
                yield send(
                    ref.at[:, 1 - self.here.c, pl.ds(2 * y, 2)],
                    self.buffers[k][1].at[:, y, :, :, cols],
                    self.c_sems, (source, y), self.here.to_core,
                )

    def first_turn(self, k):
        mine, theirs, here = self.buffers[k][0], self.buffers[k][2], self.here
        left, right = self.halves(k)
        yield send(mine.at[:, :, 1 - here.x, :, left], theirs.at[0], self.x_sems, (k, 0), here.to_x)
        yield send(mine.at[:, 1 - here.y, :, :, right], theirs.at[1], self.x_sems, (k, 1), here.to_y)

    def second_turn(self, k):
        mine, theirs, here = self.buffers[k][0], self.buffers[k][3], self.here
        left, right = self.halves(k)
        yield send(mine.at[:, 1 - here.y, here.x, :, left], theirs.at[0], self.y_sems, (k, 0), here.to_y)
        yield send(mine.at[:, here.y, 1 - here.x, :, right], theirs.at[1], self.y_sems, (k, 1), here.to_x)

    def line(self, k):
        here, buffers = self.here, self.buffers[k]
        sems = [sem.at[k] for sem in self.z_sems]
        return LineSum(here, lambda z: buffers[0].at[z, here.y, here.x], buffers[4], sems)

    def finished(self, k):
        for i in range(3):
            mine = self.buffers[k][5].at[self.here.r]
            yield send(mine, mine, self.g_sems, (k, i), self.here.plane[i])

    def arriving(self, k):
        for i in range(3):
            theirs = self.buffers[k][5].at[self.here.quarters[i]]
            yield send(theirs, theirs, self.g_sems, (k, i), self.here.plane[i])


    def start(self, k):
        for copy in (*self.own(k), *self.to_core(k)):
            copy.start()

    def in_chip(self, k):
        for copy in self.own(k):
            copy.wait()
        for copy in self.to_core(k):
            copy.wait_recv()
        mine, theirs = self.buffers[k][:2]
        for z in range(4):
            for y in range(2):
                for x in range(2):
                    mine[z, y, x] = mine[z, y, x] + theirs[z, y, x]
        for copy in self.first_turn(k):
            copy.start()

    def in_pairs(self, k):
        for copy in self.first_turn(k):
            copy.wait()
        mine, theirs, here = self.buffers[k][0], self.buffers[k][2], self.here
        left, right = self.halves(k)
        for z in range(4):
            for i in range(2):
                mine[z, i, here.x, :, left] = mine[z, i, here.x, :, left] + theirs[0, z, i]
                mine[z, here.y, i, :, right] = mine[z, here.y, i, :, right] + theirs[1, z, i]
        for copy in self.second_turn(k):
            copy.start()

    def in_plane(self, k):
        for copy in self.second_turn(k):
            copy.wait()
        mine, theirs, here = self.buffers[k][0], self.buffers[k][3], self.here
        for z in range(4):
            for i, cols in enumerate(self.halves(k)):
                mine[z, here.y, here.x, :, cols] = mine[z, here.y, here.x, :, cols] + theirs[i, z]
        self.line(k).start()

    def turn0(self, k):
        self.line(k).turn(0)

    def turn1(self, k):
        self.line(k).turn(1)

    def turn2(self, k):
        self.line(k).turn(2)

    def in_line(self, k):
        self.line(k).turn(3)
        mine, done, here = self.buffers[k][0], self.buffers[k][5], self.here
        done[here.r] = mine[here.z, here.y, here.x]
        for copy in self.finished(k):
            copy.start()

    def end(self, k):
        for copy in self.arriving(k):
            copy.wait_recv()
        for copy in (*self.to_core(k), *self.finished(k)):
            copy.wait_send()
        self.line(k).finish()
        self.outs[k][...] = self.buffers[k][5][...]


    def gain_copy(self, stage, i):
        mine, core, plane, line = self.gain_buffers
        if stage == 0:
            return send(mine, core, self.gain_sems[0], 0, self.here.to_core)
        if stage == 1:
            return send(mine, plane.at[self.here.r], self.gain_sems[1], i, self.here.plane[i])
        return send(mine, line.at[i], self.gain_sems[2], i, self.here.line[i])

    def gain_plane_recv(self, i):
        mine, _, plane, _ = self.gain_buffers
        return send(mine, plane.at[self.here.quarters[i]], self.gain_sems[1], i, self.here.plane[i])

    def gain_step(self, stage):
        mine, core, plane, line = self.gain_buffers
        if stage == 0:
            self.gain_copy(0, 0).start()
        elif stage == 1:
            self.gain_copy(0, 0).wait()
            mine[...] += core[...]
            plane[self.here.r] = mine[...]
            for i in range(3):
                self.gain_copy(1, i).start()
        elif stage == 2:
            for i in range(3):
                self.gain_copy(1, i).wait_send()
                self.gain_plane_recv(i).wait_recv()
            mine[...] = (plane[0] + plane[1]) + (plane[2] + plane[3])
            for i in range(3):
                self.gain_copy(2, i).start()
        else:
            for i in range(3):
                self.gain_copy(2, i).wait()
            self.outs[len(self.chunks)][...] = (mine[...] + line[0]) + (line[1] + line[2])


    def token_core(self):
        mine = self.token_window.at[self.here.c]
        return send(mine, mine, self.token_sems, 0, self.here.to_core)

    def token_core_recv(self):
        theirs = self.token_window.at[1 - self.here.c]
        return send(theirs, theirs, self.token_sems, 0, self.here.to_core)

    def token_place(self, start):
        self.token_core().wait_send()
        self.token_core_recv().wait_recv()
        count, rows = 2 * self.token_window.shape[1], self.token_mine.shape[1]
        window = self.token_window[...].reshape(count, D)
        for z in range(4):
            slot = lax.broadcasted_iota(jnp.int32, (rows, count), 0) + (2 * z + self.here.c) * rows
            row = lax.broadcasted_iota(jnp.int32, (rows, count), 1) + start
            self.token_mine[z] = low(dot(low(jnp.where(slot == row, 1.0, 0.0)), window))
        self.token_line.start()

    def token_end(self):
        self.token_line.turn(3)
        self.outs[-1][...] = self.token_mine[self.here.z].astype(F32)
        self.token_line.finish()


def tail_kernel(
    comm, lat_ref, g1_ref, do_ref, p_ref, q_ref, kv_ref, gain_ref, wq_ref, wkv_ref, win_ref, start_ref,
    dm1_ref, ds_ref, dm2_ref, *refs,
):
    n_in, n_out = len(comm.inputs), len(comm.out_shapes)
    ins, lg_ref = refs[:n_in], refs[n_in]
    outs, scratch = refs[n_in + 1 : n_in + 1 + n_out], refs[n_in + 1 + n_out :]
    kv_sum, dkv_ref, more_ref, kv_sems = scratch[0], scratch[1], scratch[2], scratch[3:5]
    comm.bind(ins, outs, scratch[5:])
    here = comm.here
    mixed = len(comm.chunks) - 1
    early = range(mixed)
    rows, span = p_ref.shape
    gains = comm.gain_buffers[0]

    here.greet()
    for k in early:
        comm.start(k)
    block = rows // 2
    dwq = None
    gains[...] = jnp.zeros_like(gains)
    for i in range(2):
        at = slice(i * block, (i + 1) * block)
        p, do, q = p_ref[at], do_ref[at], q_ref[at]
        dp = dot_nt(do, kv_ref[:, D:])
        wide_p = p.astype(F32)
        ds = low(wide_p * (dp - jnp.sum(wide_p * dp, axis=1, keepdims=True)))
        dq = low(dot(ds, kv_ref[:, :D]) * CROSS_SCALE)
        dk, dv = dot_tn(ds, q), dot_tn(p, do)
        if i == 0:
            kv_sum[:, :D], kv_sum[:, D:] = dk, dv
        else:
            dkv_ref[:, :D] = low((kv_sum[:, :D] + dk) * CROSS_SCALE)
            dkv_ref[:, D:] = low(kv_sum[:, D:] + dv)
        unit, factor = normed(lat_ref[at].astype(F32))
        gain = gain_ref[0:1, :]
        term = dot_tn(low(unit * gain), dq)
        dwq = term if dwq is None else dwq + term
        back, dgain = norm_back(dot_nt(dq, wq_ref[...]), unit, factor, gain)
        lg_ref[at] = g1_ref[at] + back
        gains[0:1] += dgain
        if i < mixed:
            comm.in_chip(i)
    for k in range(2, mixed):
        comm.in_chip(k)
    half = span // 2
    to_core = send(
        dkv_ref.at[pl.ds(half * (1 - here.c), half)], more_ref, kv_sems, 0, here.to_core)
    to_core.start()
    comm.stages[1][...] = low(dwq).reshape(comm.stages[1].shape)
    gains[2:3], gains[3:4], gains[4:5] = dm1_ref[0:1], ds_ref[0:1], dm2_ref[0:1]
    unit, factor = normed(win_ref[pl.ds(half * here.c, half)].astype(F32))
    gain = gain_ref[1:2, :]
    to_core.wait()
    dkv = low(dkv_ref[pl.ds(half * here.c, half)].astype(F32) + more_ref[...].astype(F32))
    back, dgain = norm_back(dot_nt(dkv, wkv_ref[...]), unit, factor, gain)
    comm.token_window[here.c] = low(back)
    comm.token_core().start()
    gains[1:2] = dgain
    comm.gain_step(0)
    comm.stages[0][...] = low(dot_tn(low(unit * gain), dkv)).reshape(comm.stages[0].shape)
    comm.start(mixed)
    comm.token_place(start_ref[0:1, 0:1])
    for k in early:
        comm.in_pairs(k)
    comm.in_chip(mixed)
    comm.gain_step(1)
    comm.token_line.turn(0)
    for k in early:
        comm.in_plane(k)
    comm.in_pairs(mixed)
    for k in early:
        comm.turn0(k)
    comm.token_line.turn(1)
    for k in early:
        comm.turn1(k)
    comm.in_plane(mixed)
    comm.gain_step(2)
    for k in early:
        comm.turn2(k)
    comm.turn0(mixed)
    comm.token_line.turn(2)
    for k in early:
        comm.in_line(k)
    comm.turn1(mixed)
    comm.gain_step(3)
    comm.turn2(mixed)
    comm.token_end()
    comm.in_line(mixed)
    for k in range(mixed + 1):
        comm.end(k)


def tail(comm, latents, g1, do, p, q, kv, gains, wide, window, start, dgains):
    rows, span = p.shape
    r = (rows, D)
    return call(
        functools.partial(tail_kernel, comm),
        (1,),
        [
            (latents, r, flat),
            (g1, r, flat),
            (do, r, flat),
            (p, p.shape, flat),
            (q, r, flat),
            (kv, kv.shape, flat),
            (gains, (8, D), flat),
            (wide, (D, D), column(2)),
            (wide, (D, 2 * D), column(0)),
            (window, (span, D), flat),
            (start, start.shape, flat),
        ]
        + [(g, (8, D), flat) for g in dgains],
        [(r, F32, r, flat)],
        [
            pltpu.VMEM((span, 2 * D), F32),
            pltpu.VMEM((span, 2 * D), BF16),
            pltpu.VMEM((span // 2, 2 * D), BF16),
        ]
        + sem_pair(1),
        comm=comm,
        collective_id=2,
    )


def widen_kernel(cuts, *refs):
    half = len(cuts)
    targets = list(refs[half:])
    for source, widths in zip(refs[:half], cuts):
        first = 0
        for width in widths:
            targets.pop(0)[...] = source[:, first : first + width].astype(F32)
            first += width


def widen(arrays, cuts):
    return pl.pallas_call(
        functools.partial(widen_kernel, cuts),
        out_shape=[
            jax.ShapeDtypeStruct((a.shape[0], width), F32)
            for a, widths in zip(arrays, cuts)
            for width in widths
        ],
        compiler_params=pltpu.CompilerParams(vmem_limit_bytes=VMEM_LIMIT),
    )(*arrays)


def from_partner(shard, bit):
    return lax.ppermute(shard, "lat", [(i, i ^ 1 << bit) for i in range(lax.axis_size("lat"))])


def gather_lat(shard):
    return lax.all_gather(shard, "lat", axis=0, tiled=True)


def halve(value, place, bits):
    kept, more = value, jnp.zeros_like(value)
    for bit in reversed(range(bits)):
        value = low(kept.astype(F32) + more.astype(F32))
        half = value.shape[0] // 2
        upper = place // 2**bit % 2
        kept = lax.dynamic_slice_in_dim(value, upper * half, half)
        more = from_partner(lax.dynamic_slice_in_dim(value, (1 - upper) * half, half), bit)
    return kept, more


def reduce_weights(grad):
    share = lax.psum_scatter(grad, "lat", scatter_dimension=0, tiled=True)
    return lax.psum(share, "row").astype(F32)


def local(
    tokens, latents, segment_ids, pad_mask, block_scene, out_grad,
    gain_cross_q, gain_cross_kv, w_cross_q, w_cross_kv, w_cross_out,
    gain_mlp1, w_up1, w_down1, gain_self, w_self_qkv, w_self_out, gain_mlp2, w_up2, w_down2,
):
    tokens, latents, og = tokens[0], latents[0], out_grad[0]
    rows, slots = latents.shape[0], tokens.shape[0] * lax.axis_size("lat")
    scenes = block_scene.shape[1]
    span = slots // scenes
    place = lax.axis_index("lat")
    group = LAT_SCENE // rows
    bits = group.bit_length() - 1

    tag = jnp.where(pad_mask == 1, segment_ids, -1)
    gains = jnp.stack([gain_cross_q, gain_cross_kv, gain_mlp1, gain_self, gain_mlp2], axis=0)
    wides = [w_cross_kv, w_cross_q, w_cross_out, w_up1, w_self_out, w_self_qkv, w_up2]
    talls = [w_down1, w_down2]
    planes = lax.axis_size("row") == 4 and lax.axis_size("lat") == 8
    if planes:
        meta = jnp.concatenate([low(tag), gains.reshape(1, -1)], axis=1)
        meta = jnp.pad(meta, ((0, 15), (0, -meta.shape[1] % LANES)))
        all_tokens, meta, wide, tall = gather_all(tokens, meta, wides, talls)
        all_tags = meta[:, 0, : tag.shape[1]].reshape(1, slots).astype(jnp.int32)
        gains = meta[:, 0, tag.shape[1] : tag.shape[1] + gains.size]
        gains = gains.reshape(8, 5, -1).transpose(1, 0, 2).reshape(5, D)
    else:
        all_tags = lax.all_gather(low(tag), "lat", axis=1, tiled=True).astype(jnp.int32)
        all_tokens = gather_lat(tokens)
        gains = lax.all_gather(gains, "lat", axis=1, tiled=True)
        wide = gather_lat(jnp.concatenate(wides, axis=1))
        tall = gather_lat(jnp.concatenate(talls, axis=1))
    gains = jnp.pad(gains.astype(F32), ((0, 3), (0, 0)))

    block = place * rows // LAT_SCENE
    scene = jnp.sum(jnp.where(jnp.arange(scenes) == block, block_scene[0], 0))
    before = jnp.sum(((all_tags >= 0) & (all_tags < scene)).astype(jnp.int32))
    start = jnp.minimum(before // 16 * 16, slots - span)
    window = lax.dynamic_slice_in_dim(all_tokens, start, span)
    bias = jnp.where(lax.dynamic_slice_in_dim(all_tags, start, span, axis=1) == scene, 0.0, NEG)

    x1, x2, q, p, o, kv, q2, k2, v2 = front(latents, window, bias.astype(F32), gains, wide, tall)
    if group == 2:
        k2_more, v2_more = from_partner((k2, v2), 0)
        keys, values = (k2, k2_more), (v2, v2_more)
    else:
        for bit in range(bits):
            upper = place // 2**bit % 2 == 1
            more = from_partner((k2, v2), bit)
            k2, v2 = (
                jnp.where(upper, jnp.concatenate([b, a]), jnp.concatenate([a, b]))
                for a, b in zip((k2, v2), more)
            )
        keys, values = (k2,), (v2,)
    o2, p2, scale2 = self_forward(q2, keys, values)
    out, g3, do2, dwup2, dwdown2, dwso, dgain_m2 = second(x2, o2, og, gains, wide, tall)
    comm = WeightSum([[dwup2], [dwdown2], [dwso]]) if planes else None
    dq2, dk2, dv2, early = self_backward(q2, do2, o2, scale2, p2, keys, values, comm)
    if group == 2:
        dk_more, dv_more = from_partner((dk2[1], dv2[1]), 0)
        dk, dv = dk2[0], dv2[0]
    else:
        dk, dk_more = halve(dk2[0], place, bits)
        dv, dv_more = halve(dv2[0], place, bits)
    g2, dwqkv, dgain_s = qkv_back(x2, g3, dq2, dk, dk_more, dv, dv_more, gains, wide)
    g1, do, dwup1, dwdown1, dwout, dgain_m1 = first_back(x1, g2, o, gains, wide, tall)
    if planes:
        comm = WeightSum(
            [[dwqkv], [dwup1], [dwdown1], [Staged(D, 2 * D), Staged(D, D), dwout]], gains=(8, D), tokens=slots
        )
        latent_grad, *late, dgains, token_grad = tail(
            comm, latents, g1, do, p, q, kv, gains, wide, window,
            jnp.broadcast_to(start, (8, LANES)), (dgain_m1, dgain_s, dgain_m2),
        )
        dgains = lax.dynamic_slice_in_dim(dgains, place * (D // 8), D // 8, axis=1)
        up2, down2, so, qkv, up1, down1, mixed = (
            a.reshape(-1, a.shape[2]) for a in (*early, *late)
        )
        dwkv, dwq, dwout, *others = widen(
            [mixed, up1, down1, qkv, so, up2, down2],
            ((2 * D, D, D), (FF,), (D,), (3 * D,), (D,), (FF,), (D,)),
        )
        sums = dwq, dwkv, dwout, *others
    else:
        latent_grad, dwq, dkv, dgain_q = cross_back(latents, g1, do, p, q, kv, gains, wide)
        mine, more = halve(dkv, place, bits)
        first = place % group * (span // group)
        token_rows = lax.dynamic_slice_in_dim(window, first, span // group)
        token_part, dwkv, dgain_kv = token_back(token_rows, mine, more, gains, wide)
        token_part = lax.dynamic_update_slice_in_dim(
            jnp.zeros((slots, D), BF16), token_part, start + first, 0
        )
        token_grad = lax.psum_scatter(token_part, "lat", scatter_dimension=0, tiled=True).astype(F32)
        dgains = jnp.stack([g[0] for g in (dgain_q, dgain_kv, dgain_m1, dgain_s, dgain_m2)])
        dgains = lax.psum_scatter(low(dgains), "lat", scatter_dimension=1, tiled=True)
        dgains = lax.psum(dgains, "row").astype(F32)
        sums = [
            reduce_weights(g) for g in (dwq, dwkv, dwout, dwup1, dwdown1, dwqkv, dwso, dwup2, dwdown2)
        ]
    dwq, dwkv, dwout, dwup1, dwdown1, dwqkv, dwso, dwup2, dwdown2 = sums
    return (
        out[None],
        latent_grad[None],
        token_grad[None],
        dgains[0],
        dgains[1],
        dwq,
        dwkv,
        dwout,
        dgains[2],
        dwup1,
        dwdown1,
        dgains[3],
        dwqkv,
        dwso,
        dgains[4],
        dwup2,
        dwdown2,
    )


def solution(mesh):
    by_row = P("row", "lat", None)
    weight = P("lat", None)
    gain = P("lat")
    parameters = (
        gain, gain, weight, weight, weight, gain, weight, weight, gain, weight, weight, gain,
        weight, weight,
    )
    return jax.shard_map(
        local,
        mesh=mesh,
        in_specs=(by_row, by_row, P("row", "lat"), P("row", "lat"), P("row", None), by_row)
        + parameters,
        out_specs=(by_row, by_row, by_row) + parameters,
        check_vma=False,
    )
```

```python
import functools

import jax
import jax.numpy as jnp
from jax import lax
from jax.experimental import pallas as pl
from jax.experimental.pallas import tpu as pltpu
from jax.sharding import PartitionSpec as P

D = 512
FF = 2048
HEADS = 8
LAT_SCENE = 2048
HEAD = D // HEADS
PAIRS = HEADS // 2
LANES = 128
FF_STEP = 512
EPS = 1e-05
NEG = -1e30
CROSS_SCALE = D ** (-0.5)
SELF_SCALE = HEAD ** (-0.5)
GELU_C = 0.7978845608028654
GELU_K = 0.044715
VMEM_LIMIT = 60 * 1024 * 1024
F32 = jnp.float32
BF16 = jnp.bfloat16


def low(value):
    return value.astype(BF16)


def dot(left, right):
    return jnp.dot(left, right, preferred_element_type=F32)


def dot_nt(left, right):
    return lax.dot_general(left, right, (((1,), (1,)), ((), ())), preferred_element_type=F32)


def dot_tn(left, right):
    return lax.dot_general(left, right, (((0,), (0,)), ((), ())), preferred_element_type=F32)


def normed(value):
    centered = value - jnp.mean(value, axis=-1, keepdims=True)
    factor = lax.rsqrt(jnp.mean(centered * centered, axis=-1, keepdims=True) + EPS)
    return centered * factor, factor


def norm_back(grad, unit, factor, gain):
    scaled = grad * gain
    inner = (
        scaled
        - jnp.mean(scaled, axis=-1, keepdims=True)
        - unit * jnp.mean(scaled * unit, axis=-1, keepdims=True)
    )
    return factor * inner, jnp.sum(grad * unit, axis=0, keepdims=True)


def gelu(u):
    return 0.5 * u * (1.0 + jnp.tanh(GELU_C * (u + GELU_K * u * u * u)))


def gelu_both(u):
    square = u * u
    t = jnp.tanh(GELU_C * u * (1.0 + GELU_K * square))
    half = 0.5 * (1.0 + t)
    slope = half + 0.5 * u * (1.0 - t * t) * (GELU_C * (1.0 + 3.0 * GELU_K * square))
    return u * half, slope


def call(kernel, grid, ins, outs, scratch=(), comm=None, collective_id=None):
    in_specs = [ANYWHERE if block is None else pl.BlockSpec(block, index) for _, block, index in ins]
    out_specs = [ANYWHERE if block is None else pl.BlockSpec(block, index) for _, _, block, index in outs]
    out_shape = [jax.ShapeDtypeStruct(shape, kind) for shape, kind, _, _ in outs]
    arrays, scratch = [array for array, _, _ in ins], list(scratch)
    if comm is not None:
        arrays += comm.inputs
        in_specs += comm.in_specs
        out_shape += comm.out_shapes
        out_specs += comm.out_specs
        scratch += comm.scratch
    return pl.pallas_call(
        kernel,
        grid=grid,
        in_specs=in_specs,
        out_specs=out_specs,
        out_shape=out_shape,
        scratch_shapes=scratch,
        compiler_params=pltpu.CompilerParams(
            vmem_limit_bytes=VMEM_LIMIT,
            collective_id=None if comm is None else collective_id,
            has_side_effects=comm is not None,
        ),
    )(*arrays)


def inside(shape):
    return pl.BlockSpec(shape, lambda *_: (0,) * len(shape))


ANYWHERE = pl.BlockSpec(memory_space=pl.ANY)


def flat(*_):
    return (0, 0)


def column(c):
    return lambda *_: (0, c)


def rows_of(i, *_):
    return (i, 0)


def front_kernel(
    lat_ref, tok_ref, tags_ref, scene_ref, gain_ref, wq_ref, wkv_ref, wout_ref, wup_ref, wdown_ref, wqkv_ref,
    x1_ref, x2_ref, q_ref, p_ref, o_ref, kv_ref, q2_ref, k2_ref, v2_ref, win_ref, start_ref,
    bias_ref, sem,
):
    @pl.when(pl.program_id(0) == 0)
    def _():
        span, slots = win_ref.shape[0], tok_ref.shape[0]
        tags, scene = tags_ref[...].astype(F32), scene_ref[0, 0].astype(F32)
        count = lambda chosen: jnp.sum(jnp.where(chosen, 1.0, 0.0)).astype(jnp.int32)
        before = count((tags >= 0.0) & (tags < scene))
        length = count(tags == scene)
        start = pl.multiple_of(jnp.minimum(before // 16 * 16, slots - span), 16)
        copy = pltpu.make_async_copy(tok_ref.at[pl.ds(start, span)], win_ref, sem)
        copy.start()
        start_ref[...] = jnp.full(start_ref.shape, start, jnp.int32)
        slot = lax.broadcasted_iota(jnp.int32, bias_ref.shape, 1) + start
        bias_ref[...] = jnp.where((slot >= before) & (slot < before + length), 0.0, NEG)
        copy.wait()
        unit, _ = normed(win_ref[...].astype(F32))
        kv_ref[...] = low(dot(low(unit * gain_ref[1:2, :]), wkv_ref[...]))

    x = lat_ref[...].astype(F32)
    unit, _ = normed(x)
    q = low(dot(low(unit * gain_ref[0:1, :]), wq_ref[...]))
    q_ref[...] = q
    s = dot_nt(q, kv_ref[:, :D]) * CROSS_SCALE + bias_ref[0:1, :]
    e = jnp.exp(s - jnp.max(s, axis=1, keepdims=True))
    p = low(e / jnp.sum(e, axis=1, keepdims=True))
    p_ref[...] = p
    o = low(dot(p, kv_ref[:, D:]))
    o_ref[...] = o
    x1 = x + dot(o, wout_ref[...])
    x1_ref[...] = x1
    unit, _ = normed(x1)
    m1 = low(unit * gain_ref[2:3, :])
    total = x1
    for c in range(FF // FF_STEP):
        cols = slice(c * FF_STEP, (c + 1) * FF_STEP)
        h = low(gelu(dot(m1, wup_ref[:, cols])))
        total = total + dot(h, wdown_ref[cols, :])
    x2_ref[...] = total
    unit, _ = normed(total)
    bn = low(unit * gain_ref[3:4, :])
    q2_ref[...] = low(dot(bn, wqkv_ref[:, :D])) * SELF_SCALE
    k2_ref[...] = low(dot(bn, wqkv_ref[:, D : 2 * D]))
    v2_ref[...] = low(dot(bn, wqkv_ref[:, 2 * D :]))


def front(latents, tokens, tags, scene, span, gains, mix, up1, down1, qkv):
    rows = latents.shape[0]
    block = min(rows, 512)
    r = (block, D)
    return call(
        front_kernel,
        (rows // block,),
        [
            (latents, r, rows_of),
            (tokens, None, None),
            (tags, tags.shape, flat),
            (scene, scene.shape, flat),
            (gains, (8, D), flat),
            (mix, (D, D), column(2)),
            (mix, (D, 2 * D), column(0)),
            (mix, (D, D), column(3)),
            (up1, (D, FF), flat),
            (down1, (FF, D), flat),
            (qkv, (D, 3 * D), flat),
        ],
        [
            ((rows, D), F32, r, rows_of),
            ((rows, D), F32, r, rows_of),
            ((rows, D), BF16, r, rows_of),
            ((rows, span), BF16, (block, span), rows_of),
            ((rows, D), BF16, r, rows_of),
            ((span, 2 * D), BF16, (span, 2 * D), flat),
            ((rows, D), BF16, r, rows_of),
            ((rows, D), BF16, r, rows_of),
            ((rows, D), BF16, r, rows_of),
            ((span, D), BF16, (span, D), flat),
            ((8, LANES), jnp.int32, (8, LANES), flat),
        ],
        [pltpu.VMEM((8, span), F32), pltpu.SemaphoreType.DMA],
    )


def lane_is(shape, head):
    lane = lax.broadcasted_iota(jnp.int32, shape, 1)
    return (lane < HEAD) if head == 0 else (lane >= HEAD)


def only(value, head):
    return jnp.where(lane_is(value.shape, head), value, jnp.zeros_like(value))


def self_forward_kernel(parts, steps, comm, q_ref, *refs):
    refs = list(refs)
    take = lambda n: [refs.pop(0) for _ in range(n)]
    pair, step = pl.program_id(0), pl.program_id(1)
    point = pair * steps + step
    if comm is None:
        k_refs, v_refs = take(parts), take(parts)
        o_ref, p_ref, scale_ref = take(3)
        ones_refs = refs
    else:
        (k_ref,), (v_ref,) = take(1), take(1)
        both = take(2)
        ins = take(len(comm.inputs))
        o_ref, p_ref, scale_ref, k_more, v_more = take(5)
        outs = take(len(comm.out_shapes))
        ones_refs, (landed,), sems = take(2), take(1), take(2)
        comm.bind(ins, outs, refs)
        k_refs, v_refs = (k_ref, k_more), (v_ref, v_more)

        def to_core(i, p):
            cols = pl.ds(p * LANES, LANES)
            return send(both[i].at[:, cols], landed.at[i, p], sems, (i, p), comm.here.to_core)

        @pl.when(point == 0)
        def _():
            comm.here.greet()
            for p in range(PAIRS):
                for i in range(2):
                    to_core(i, p).start()
            comm.begin()

        pl.when(point == 1)(comm.begin_sends)
        for i in range(comm.steps):
            pl.when(point == SHIFT + i)(functools.partial(comm.step, i))

        @pl.when(step == 0)
        def _():
            for i, ref in enumerate((k_more, v_more)):
                arrived = landed.at[i, pair]
                send(arrived, arrived, sems, (i, pair), comm.here.to_core).wait_recv()
                ref[...] = arrived[...]

    @pl.when(step == 0)
    def _():
        for v_ref, ones_ref in zip(v_refs, ones_refs):
            v = v_ref[...]
            for head in range(2):
                ones_ref[head] = jnp.where(lane_is(v.shape, head), v, jnp.ones_like(v))

    q = q_ref[...]
    outs, scales = [], []
    for head in range(2):
        scores = [dot_nt(only(q, head), k_ref[...]) for k_ref in k_refs]
        top = functools.reduce(jnp.maximum, [jnp.max(s, axis=1, keepdims=True) for s in scores])
        mixed, first = None, 0
        for s, ones_ref in zip(scores, ones_refs):
            p = low(jnp.exp(s - top))
            p_ref[head, :, first : first + p.shape[1]] = p
            first += p.shape[1]
            term = dot(p, ones_ref[head])
            mixed = term if mixed is None else mixed + term
        scales.append(1.0 / pltpu.roll(mixed, HEAD, 1))
        outs.append(mixed * scales[-1])
    left = lane_is(outs[0].shape, 0)
    o_ref[...] = low(jnp.where(left, outs[0], outs[1]))
    scale_ref[...] = jnp.where(left, scales[0], scales[1])

    if comm is not None:
        @pl.when(point == PAIRS * steps - 1)
        def _():
            for p in range(PAIRS):
                for i in range(2):
                    to_core(i, p).wait_send()
            comm.finish()


def self_forward(q2, keys, values, comm=None):
    rows = q2.shape[0]
    block = min(rows, 256)
    parts = len(keys)
    total = sum(k.shape[0] for k in keys) * (1 if comm is None else 2)
    whole = lambda array: (array, (array.shape[0], LANES), lambda p, i: (0, p))
    more = ((rows, D), BF16, (rows, LANES), lambda p, i: (0, p))
    beside = comm is not None
    return call(
        functools.partial(self_forward_kernel, parts, rows // block, comm),
        (PAIRS, rows // block),
        [(q2, (block, LANES), lambda p, i: (i, p))]
        + [whole(k) for k in keys]
        + [whole(v) for v in values]
        + ([(keys[0], None, None), (values[0], None, None)] if beside else []),
        [
            ((rows, D), BF16, (block, LANES), lambda p, i: (i, p)),
            ((HEADS, rows, total), BF16, (2, block, total), lambda p, i: (p, i, 0)),
            ((rows, D), F32, (block, LANES), lambda p, i: (i, p)),
        ]
        + ([more, more] if beside else []),
        [pltpu.VMEM((2, k.shape[0], LANES), BF16) for k in keys * (2 if beside else 1)]
        + ([pltpu.VMEM((2, PAIRS, rows, LANES), BF16)] + sem_pair(2, PAIRS) if beside else []),
        comm=comm,
        collective_id=3,
    )


def run_beside(comm, point, plan, odd):
    for when, work in plan.items():
        if when % 2 != odd:
            continue
        def run(when=when, work=work):
            if when == 0:
                comm.here.greet()
            for name, k in work:
                getattr(comm, name)(k)
        pl.when(point == when)(run)


SELF_PLAN = {
    0: (("start", 0), ("start", 1), ("start", 2)),
    4: (("in_chip", 0),),
    6: (("in_chip", 1),),
    7: (("in_chip", 2),),
    10: (("in_pairs", 0),),
    15: (("in_pairs", 1),),
    16: (("in_pairs", 2),),
    18: (("in_plane", 0),),
    20: (("in_plane", 1), ("turn0", 0)),
    21: (("in_plane", 2),),
    22: (("turn1", 0), ("turn0", 1)),
    24: (("turn2", 0), ("turn1", 1), ("turn0", 2)),
    26: (("in_line", 0), ("turn2", 1), ("turn1", 2)),
    28: (("in_line", 1), ("turn2", 2)),
    30: (("in_line", 2),),
    31: (("end", 0), ("end", 1), ("end", 2)),
}


def self_backward_kernel(parts, steps, comm, q_ref, do_ref, o_ref, scale_ref, p_ref, *refs):
    refs = list(refs)
    take = lambda n: [refs.pop(0) for _ in range(n)]
    pair, step = pl.program_id(0), pl.program_id(1)
    point = 2 * (pair * steps + step)
    k_refs, v_refs = take(parts), take(parts)
    if comm is None:
        (dq_ref,), dk_refs, dv_refs = take(1), take(parts), take(parts)
        dk_sums, dv_sums = take(parts), take(parts)
    else:
        ins = take(len(comm.inputs))
        dq_ref, dk_ref, dv_ref, *landed = take(5)
        outs = take(len(comm.out_shapes))
        dk_sums, dv_sums, (stage,), sems = take(parts), take(parts), take(1), take(2)
        comm.bind(ins, outs, refs)
        dk_refs, dv_refs = (dk_ref, stage.at[0, pair]), (dv_ref, stage.at[1, pair])

        def to_core(i, p):
            cols = pl.ds(pl.multiple_of(p * LANES, LANES), LANES)
            return send(stage.at[i, p], landed[i].at[:, cols], sems, (i, p), comm.here.to_core)

        run_beside(comm, point, SELF_PLAN, 0)

    @pl.when(step == 0)
    def _():
        for ref in (*dk_sums, *dv_sums):
            ref[...] = jnp.zeros_like(ref)

    q = q_ref[...]
    do = low(do_ref[...].astype(F32) * scale_ref[...])
    product = do.astype(F32) * o_ref[...].astype(F32)
    q_turned, do_turned = jnp.transpose(q), jnp.transpose(do)
    dqs = []
    for head in range(2):
        rows = slice(head * HEAD, (head + 1) * HEAD)
        doz = only(do, head)
        delta = jnp.sum(only(product, head), axis=1, keepdims=True)
        dq, first = None, 0
        for k_ref, v_ref, dk_sum, dv_sum in zip(k_refs, v_refs, dk_sums, dv_sums):
            count = k_ref.shape[0]
            p = p_ref[head, :, first : first + count]
            first += count
            ds = low(p.astype(F32) * (dot_nt(doz, v_ref[...]) - delta))
            dv_sum[rows, :] += dot(do_turned[rows], p)
            dk_sum[rows, :] += dot(q_turned[rows], ds)
            term = dot(ds, k_ref[...])
            dq = term if dq is None else dq + term
        dqs.append(dq)
    dq_ref[...] = low(jnp.where(lane_is(dqs[0].shape, 0), dqs[0], dqs[1]) * SELF_SCALE)

    @pl.when(step == steps - 1)
    def _():
        for ref, total in zip((*dk_refs, *dv_refs), (*dk_sums, *dv_sums)):
            ref[...] = jnp.transpose(low(total[...]))
        if comm is not None:
            for i in range(2):
                to_core(i, pair).start()

    if comm is not None:
        run_beside(comm, point + 1, SELF_PLAN, 1)

        @pl.when(point == 2 * (PAIRS * steps - 1))
        def _():
            for p in range(PAIRS):
                for i in range(2):
                    to_core(i, p).wait()


def self_backward(q2, do2, o2, scale2, p2, keys, values, comm=None):
    rows = q2.shape[0]
    block = min(rows, 256)
    parts = len(keys)
    whole = lambda array: (array, (array.shape[0], LANES), lambda p, i: (0, p))
    made = lambda array: (array.shape, BF16, (array.shape[0], LANES), lambda p, i: (0, p))
    if comm is None:
        outs, extra = [made(k) for k in keys] + [made(v) for v in values], []
    else:
        outs = [made(keys[0]), made(values[0])] + [((rows, D), BF16, None, None)] * 2
        extra = [pltpu.VMEM((2, PAIRS, rows, LANES), BF16)] + sem_pair(2, PAIRS)
    out = call(
        functools.partial(self_backward_kernel, parts, rows // block, comm),
        (PAIRS, rows // block),
        [
            (q2, (block, LANES), lambda p, i: (i, p)),
            (do2, (block, LANES), lambda p, i: (i, p)),
            (o2, (block, LANES), lambda p, i: (i, p)),
            (scale2, (block, LANES), lambda p, i: (i, p)),
            (p2, (2, block, p2.shape[2]), lambda p, i: (p, i, 0)),
        ]
        + [whole(k) for k in keys]
        + [whole(v) for v in values],
        [((rows, D), BF16, (block, LANES), lambda p, i: (i, p))] + outs,
        [pltpu.VMEM((LANES, k.shape[0]), F32) for k in (*keys, *values)] + extra,
        comm=comm,
        collective_id=1,
    )
    return out[0], out[1 : 1 + len(outs)], out[1 + len(outs) :]


def second_kernel(
    steps, x2_ref, o2_ref, og_ref, gain_ref, wso_ref, wup_ref, wdown_ref,
    out_ref, g3_ref, do_ref, dwup_ref, dwdown_ref, dwso_ref, dgain_ref,
    m_ref, f_ref, dm_ref,
):
    c = pl.program_id(0)

    @pl.when(c == 0)
    def _():
        x3 = x2_ref[...] + dot(o2_ref[...], wso_ref[...])
        unit, _ = normed(x3)
        m_ref[...] = low(unit * gain_ref[4:5, :])
        out_ref[...] = x3
        f_ref[...] = jnp.zeros_like(f_ref)
        dm_ref[...] = jnp.zeros_like(dm_ref)

    m, og = m_ref[...], og_ref[...]
    h, slope = gelu_both(dot(m, wup_ref[...]))
    h = low(h)
    f_ref[...] += dot(h, wdown_ref[...])
    dwdown_ref[...] = low(dot_tn(h, og))
    du = low(slope * dot_nt(og, wdown_ref[...]))
    dwup_ref[...] = low(dot_tn(m, du))
    dm_ref[...] += dot_nt(du, wup_ref[...])

    @pl.when(c == steps - 1)
    def _():
        x3 = out_ref[...]
        unit, factor = normed(x3)
        out_ref[...] = x3 + f_ref[...]
        back, dgain = norm_back(dm_ref[...], unit, factor, gain_ref[4:5, :])
        g3 = og_ref[...].astype(F32) + back
        g3_ref[...] = g3
        dgain_ref[...] = jnp.broadcast_to(dgain, dgain_ref.shape)
        b3 = low(g3)
        o2 = o2_ref[...]
        dwso_ref[...] = low(dot_tn(o2, b3))
        do_ref[...] = low(dot_nt(b3, wso_ref[...]))


def second(x2, o2, og, gains, so, up2, down2):
    rows = x2.shape[0]
    steps = FF // FF_STEP
    r = (rows, D)
    return call(
        functools.partial(second_kernel, steps),
        (steps,),
        [
            (x2, r, flat),
            (o2, r, flat),
            (og, r, flat),
            (gains, (8, D), flat),
            (so, (D, D), flat),
            (up2, (D, FF_STEP), lambda c: (0, c)),
            (down2, (FF_STEP, D), lambda c: (c, 0)),
        ],
        [
            (r, F32, r, flat),
            (r, F32, r, flat),
            (r, BF16, r, flat),
            ((D, FF), BF16, (D, FF_STEP), lambda c: (0, c)),
            ((FF, D), BF16, (FF_STEP, D), lambda c: (c, 0)),
            ((D, D), BF16, (D, D), flat),
            ((8, D), F32, (8, D), flat),
        ],
        [pltpu.VMEM(r, BF16), pltpu.VMEM(r, F32), pltpu.VMEM(r, F32)],
    )


def qkv_back_kernel(
    x2_ref, g3_ref, dq_ref, dk_ref, dk_more_ref, dv_ref, dv_more_ref, gain_ref, w_ref,
    g2_ref, dw_ref, dgain_ref,
):
    unit, factor = normed(x2_ref[...])
    gain = gain_ref[3:4, :]
    bn = low(unit * gain)
    dq = dq_ref[...]
    dk = low(dk_ref[...].astype(F32) + dk_more_ref[...].astype(F32))
    dv = low(dv_ref[...].astype(F32) + dv_more_ref[...].astype(F32))
    dbn = None
    for i, part in enumerate((dq, dk, dv)):
        cols = slice(i * D, (i + 1) * D)
        dw_ref[:, cols] = low(dot_tn(bn, part))
        term = dot_nt(part, w_ref[:, cols])
        dbn = term if dbn is None else dbn + term
    back, dgain = norm_back(dbn, unit, factor, gain)
    g2_ref[...] = g3_ref[...] + back
    dgain_ref[...] = jnp.broadcast_to(dgain, dgain_ref.shape)


def qkv_back(x2, g3, dq, dk, dk_more, dv, dv_more, gains, qkv):
    rows = x2.shape[0]
    r = (rows, D)
    return call(
        qkv_back_kernel,
        (1,),
        [(a, r, flat) for a in (x2, g3, dq, dk, dk_more, dv, dv_more)]
        + [(gains, (8, D), flat), (qkv, (D, 3 * D), flat)],
        [
            (r, F32, r, flat),
            ((D, 3 * D), BF16, (D, 3 * D), flat),
            ((8, D), F32, (8, D), flat),
        ],
    )


def first_back_kernel(
    steps, x1_ref, g2_ref, o_ref, gain_ref, wout_ref, wup_ref, wdown_ref,
    g1_ref, do_ref, dwup_ref, dwdown_ref, dwout_ref, dgain_ref,
    m_ref, b_ref, dm_ref,
):
    c = pl.program_id(0)

    @pl.when(c == 0)
    def _():
        unit, _ = normed(x1_ref[...])
        m_ref[...] = low(unit * gain_ref[2:3, :])
        b_ref[...] = low(g2_ref[...])
        dm_ref[...] = jnp.zeros_like(dm_ref)

    m, b = m_ref[...], b_ref[...]
    h, slope = gelu_both(dot(m, wup_ref[...]))
    dwdown_ref[...] = low(dot_tn(low(h), b))
    du = low(slope * dot_nt(b, wdown_ref[...]))
    dwup_ref[...] = low(dot_tn(m, du))
    dm_ref[...] += dot_nt(du, wup_ref[...])

    @pl.when(c == steps - 1)
    def _():
        unit, factor = normed(x1_ref[...])
        back, dgain = norm_back(dm_ref[...], unit, factor, gain_ref[2:3, :])
        g1 = g2_ref[...] + back
        g1_ref[...] = g1
        dgain_ref[...] = jnp.broadcast_to(dgain, dgain_ref.shape)
        b1 = low(g1)
        dwout_ref[...] = low(dot_tn(o_ref[...], b1))
        do_ref[...] = low(dot_nt(b1, wout_ref[...]))


def first_back(x1, g2, o, gains, mix, up1, down1):
    rows = x1.shape[0]
    steps = FF // FF_STEP
    r = (rows, D)
    return call(
        functools.partial(first_back_kernel, steps),
        (steps,),
        [
            (x1, r, flat),
            (g2, r, flat),
            (o, r, flat),
            (gains, (8, D), flat),
            (mix, (D, D), column(3)),
            (up1, (D, FF_STEP), lambda c: (0, c)),
            (down1, (FF_STEP, D), lambda c: (c, 0)),
        ],
        [
            (r, F32, r, flat),
            (r, BF16, r, flat),
            ((D, FF), BF16, (D, FF_STEP), lambda c: (0, c)),
            ((FF, D), BF16, (FF_STEP, D), lambda c: (c, 0)),
            ((D, D), BF16, (D, D), flat),
            ((8, D), F32, (8, D), flat),
        ],
        [pltpu.VMEM(r, BF16), pltpu.VMEM(r, BF16), pltpu.VMEM(r, F32)],
    )


def cross_back_kernel(
    steps, lat_ref, g1_ref, do_ref, p_ref, q_ref, kv_ref, gain_ref, wq_ref,
    lg_ref, dwq_ref, dkv_ref, dgain_ref, dk_sum, dv_sum, dwq_sum,
):
    i = pl.program_id(0)

    @pl.when(i == 0)
    def _():
        for ref in (dk_sum, dv_sum, dwq_sum, dgain_ref):
            ref[...] = jnp.zeros_like(ref)

    p, do, q = p_ref[...], do_ref[...], q_ref[...]
    dp = dot_nt(do, kv_ref[:, D:])
    wide_p = p.astype(F32)
    ds = low(wide_p * (dp - jnp.sum(wide_p * dp, axis=1, keepdims=True)))
    dq = low(dot(ds, kv_ref[:, :D]) * CROSS_SCALE)
    dk_sum[...] += dot_tn(ds, q)
    dv_sum[...] += dot_tn(p, do)
    unit, factor = normed(lat_ref[...].astype(F32))
    gain = gain_ref[0:1, :]
    dwq_sum[...] += dot_tn(low(unit * gain), dq)
    back, dgain = norm_back(dot_nt(dq, wq_ref[...]), unit, factor, gain)
    lg_ref[...] = g1_ref[...] + back
    dgain_ref[...] += jnp.broadcast_to(dgain, dgain_ref.shape)

    @pl.when(i == steps - 1)
    def _():
        dwq_ref[...] = low(dwq_sum[...])
        dkv_ref[:, :D] = low(dk_sum[...] * CROSS_SCALE)
        dkv_ref[:, D:] = low(dv_sum[...])


def cross_back(latents, g1, do, p, q, kv, gains, mix):
    rows, span = p.shape
    block = min(rows, 512)
    r = (block, D)
    return call(
        functools.partial(cross_back_kernel, rows // block),
        (rows // block,),
        [
            (latents, r, rows_of),
            (g1, r, rows_of),
            (do, r, rows_of),
            (p, (block, span), rows_of),
            (q, r, rows_of),
            (kv, (span, 2 * D), flat),
            (gains, (8, D), flat),
            (mix, (D, D), column(2)),
        ],
        [
            ((rows, D), F32, r, rows_of),
            ((D, D), BF16, (D, D), flat),
            ((span, 2 * D), BF16, (span, 2 * D), flat),
            ((8, D), F32, (8, D), flat),
        ],
        [pltpu.VMEM((span, D), F32), pltpu.VMEM((span, D), F32), pltpu.VMEM((D, D), F32)],
    )


def token_back_kernel(tok_ref, dkv_ref, more_ref, gain_ref, w_ref, tg_ref, dw_ref, dgain_ref):
    unit, factor = normed(tok_ref[...].astype(F32))
    gain = gain_ref[1:2, :]
    dkv = low(dkv_ref[...].astype(F32) + more_ref[...].astype(F32))
    dw_ref[...] = low(dot_tn(low(unit * gain), dkv))
    back, dgain = norm_back(dot_nt(dkv, w_ref[...]), unit, factor, gain)
    tg_ref[...] = low(back)
    dgain_ref[...] = jnp.broadcast_to(dgain, dgain_ref.shape)


def token_back(tokens, dkv, more, gains, mix):
    rows = tokens.shape[0]
    return call(
        token_back_kernel,
        (1,),
        [
            (tokens, (rows, D), flat),
            (dkv, (rows, 2 * D), flat),
            (more, (rows, 2 * D), flat),
            (gains, (8, D), flat),
            (mix, (D, 2 * D), column(0)),
        ],
        [
            ((rows, D), BF16, (rows, D), flat),
            ((D, 2 * D), BF16, (D, 2 * D), flat),
            ((8, D), F32, (8, D), flat),
        ],
    )


MESH = pl.DeviceIdType.MESH
UP, DOWN = 0, 1


class Place:
    def __init__(self):
        row, lat = lax.axis_index("row"), lax.axis_index("lat")
        self.x, self.y, self.z, self.c = row % 2, row // 2, lat // 2, lat % 2
        self.r = row
        self.rx = self.y * 2 + 1 - self.x
        self.ry = (1 - self.y) * 2 + self.x
        self.rd = (1 - self.y) * 2 + 1 - self.x
        self.to_x, self.to_y = (self.rx, lat), (self.ry, lat)
        self.to_core = (row, self.z * 2 + 1 - self.c)
        self.to_z = ((row, lat + 2), (row, lat - 2))
        self.more = (self.z < 3, self.z > 0)

    def greet(self):
        barrier = pltpu.get_barrier_semaphore()
        for device in (self.to_x, self.to_y, self.to_core):
            pl.semaphore_signal(barrier, inc=1, device_id=device, device_id_type=MESH)
        for way in (UP, DOWN):
            @pl.when(self.more[way])
            def _():
                pl.semaphore_signal(barrier, inc=1, device_id=self.to_z[way], device_id_type=MESH)
        pl.semaphore_wait(barrier, 3 + jnp.minimum(self.z, 1) + jnp.minimum(3 - self.z, 1))

    def source(self, way, hop):
        return (self.z - hop, self.z >= hop) if way == UP else (self.z + hop, self.z + hop <= 3)


def send(src, dst, sems, index, device):
    return pltpu.make_async_remote_copy(
        src_ref=src, dst_ref=dst, send_sem=sems[0].at[index], recv_sem=sems[1].at[index],
        device_id=device, device_id_type=MESH,
    )


def sem_pair(*shape):
    return [pltpu.SemaphoreType.DMA(shape), pltpu.SemaphoreType.DMA(shape)]


TOKEN_PARTS = 4
AHEAD = 2
GAP = 2
SHIFT = 3
WEIGHT, TOKENS, NOTES = range(3)


class Gather:
    def __init__(self, weights, tokens=None, notes=()):
        self.inputs, self.out_shapes, self.chunks = [], [], []
        self.shards = []
        for shards in weights:
            shape = (4, shards[0].shape[0] // 4)
            self.shards.append([])
            for shard in shards:
                self.shards[-1].append((len(self.inputs), shard.shape[1]))
                self.inputs.append(shard.reshape(shape + shard.shape[1:]))
            cols = sum(shard.shape[1] for shard in shards)
            self.out_shapes.append(jax.ShapeDtypeStruct((4, 2) + shape + (cols,), BF16))
        self.chunks = [(WEIGHT, k) for k in range(len(weights))]
        self.out_specs = [ANYWHERE] * len(weights)
        self.copies = len(self.inputs)
        self.scratch = []
        self.noted = len(notes)
        if tokens is not None:
            self.inputs += [tokens, *notes]
            self.out_shapes += [
                jax.ShapeDtypeStruct((4, 2) + tokens.shape, BF16),
                jax.ShapeDtypeStruct((8, tokens.shape[0]), BF16),
                jax.ShapeDtypeStruct((8, D), F32),
            ]
            self.out_specs += [ANYWHERE] + [inside(made.shape) for made in self.out_shapes[-2:]]
            self.chunks = [(NOTES, 0)] + self.chunks + [(TOKENS, k) for k in range(TOKEN_PARTS)]
            self.scratch.append(pltpu.VMEM((4, 2, 16, tokens.shape[0]), BF16))
            self.copies += 1
        self.in_specs = [inside(array.shape) for array in self.inputs]
        n = len(self.chunks)
        self.scratch += [pltpu.SemaphoreType.DMA((self.copies,))]
        for shape in ((n, 2, 3), (n, 2, 3, 2), (n, 2, 3, 2), (n, 7)):
            self.scratch += sem_pair(*shape)
        self.steps = n + 4 * GAP + 1

    def bind(self, ins, outs, scratch):
        self.here, self.ins, self.outs = Place(), ins, outs
        scratch = list(scratch)
        take = lambda n: [scratch.pop(0) for _ in range(n)]
        if self.noted:
            self.notes = take(1)[0]
        self.local = take(1)[0]
        self.z_sems, self.p_sems, self.q_sems, self.c_sems = (take(2) for _ in range(4))

    def block(self, k, source, core=None):
        kind, index = self.chunks[k]
        core = self.here.c if core is None else core
        if kind == NOTES:
            return self.notes.at[source, core]
        if kind == TOKENS:
            tokens = self.outs[len(self.shards)]
            rows = tokens.shape[2] // TOKEN_PARTS
            return tokens.at[source, core, pl.ds(index * rows, rows)]
        return self.outs[index].at[source, core]

    def piece(self, k, source, quarter, half=None):
        if not self.shared(k):
            return self.block(k, source)
        ref = self.outs[self.chunks[k][1]]
        if half is None:
            return ref.at[source, self.here.c, quarter]
        width = ref.shape[-1] // 2
        return ref.at[source, self.here.c, quarter, :, pl.ds(half * width, width)]

    def shared(self, k):
        return self.chunks[k][0] == WEIGHT

    def z_send(self, k, way, hop):
        source, _ = self.here.source(way, hop - 1)
        ref = self.piece(k, source, self.here.r)
        return send(ref, ref, self.z_sems, (k, way, hop - 1), self.here.to_z[way])

    def z_recv(self, k, way, hop):
        source, _ = self.here.source(way, hop)
        ref = self.piece(k, source, self.here.r)
        return send(ref, ref, self.z_sems, (k, way, hop - 1), self.here.to_z[way])

    def p_copy(self, k, way, hop, axis, mine):
        here = self.here
        source, _ = here.source(way, hop)
        ref = self.piece(k, source, here.r if mine else (here.rx, here.ry)[axis])
        return send(ref, ref, self.p_sems, (k, way, hop - 1, axis), (here.to_x, here.to_y)[axis])

    def q_copy(self, k, way, hop, half, mine):
        here = self.here
        source, _ = here.source(way, hop)
        ref = self.piece(k, source, (here.rx, here.ry)[half] if mine else here.rd, half)
        return send(ref, ref, self.q_sems, (k, way, hop - 1, half), (here.to_y, here.to_x)[half])

    def c_copy(self, k, source, index, mine):
        ref = self.block(k, source, self.here.c if mine else 1 - self.here.c)
        return send(ref, ref, self.c_sems, (k, index), self.here.to_core)

    def ways(self, hop, fn):
        for way in (UP, DOWN):
            source, valid = self.here.source(way, hop)
            pl.when(valid)(functools.partial(fn, way, hop, source))

    @staticmethod
    def index_of(way, hop):
        return 1 + way * 3 + hop - 1

    def first_sends(self, k):
        for way in (UP, DOWN):
            pl.when(self.here.more[way])(lambda way=way: self.z_send(k, way, 1).start())
        self.c_copy(k, self.here.z, 0, True).start()

    def stage_z(self, k, hop):
        def arrive(way, hop, source):
            self.z_recv(k, way, hop).wait_recv()
            if hop < 3:
                pl.when(self.here.more[way])(lambda: self.z_send(k, way, hop + 1).start())
            if self.shared(k):
                self.p_copy(k, way, hop, 0, True).start()
                self.p_copy(k, way, hop, 1, True).start()
            else:
                self.c_copy(k, source, self.index_of(way, hop), True).start()
        self.ways(hop, arrive)

    def stage_p(self, k, hop):
        def arrive(way, hop, source):
            for axis in (0, 1):
                self.p_copy(k, way, hop, axis, False).wait_recv()
                self.q_copy(k, way, hop, axis, True).start()
        self.ways(hop, arrive)

    def stage_q(self, k, hop):
        def arrive(way, hop, source):
            self.q_copy(k, way, hop, 0, False).wait_recv()
            self.q_copy(k, way, hop, 1, False).wait_recv()
            self.c_copy(k, source, self.index_of(way, hop), True).start()
        self.ways(hop, arrive)

    def local_copies(self):
        z, c = self.here.z, self.here.c
        copies = []
        for k, shards in enumerate(self.shards):
            first = 0
            for index, width in shards:
                copies.append(pltpu.make_async_copy(
                    self.ins[index], self.outs[k].at[z, c, :, :, pl.ds(first, width)],
                    self.local.at[len(copies)]))
                first += width
        if self.noted:
            copies.append(pltpu.make_async_copy(
                self.ins[len(copies)], self.outs[len(self.shards)].at[z, c], self.local.at[len(copies)]))
        return copies

    def begin(self):
        for copy in self.local_copies():
            copy.start()
        if self.noted:
            z, c = self.here.z, self.here.c
            scenes, mask, *gains = self.ins[self.copies :]
            self.notes[z, c] = jnp.zeros(self.notes.shape[2:], BF16)
            self.notes[z, c, 0:1, :] = low(jnp.where(mask[...] == 1, scenes[...], -1).astype(F32))
            for i, gain in enumerate(gains):
                self.notes[z, c, 1 + i : 2 + i, : gain.shape[1]] = gain[...]

    def begin_sends(self):
        for copy in self.local_copies():
            copy.wait()
        for k in range(min(AHEAD, len(self.chunks))):
            self.first_sends(k)

    def step(self, step):
        total = len(self.chunks)
        if step + AHEAD < total:
            self.first_sends(step + AHEAD)
        for lag, stage in ((0, self.stage_z), (GAP, self.stage_p), (2 * GAP, self.stage_q)):
            for hop in (1, 2, 3):
                k = step - lag - GAP * (hop - 1)
                if 0 <= k < total and (lag == 0 or self.shared(k)):
                    stage(k, hop)

    def finish(self):
        here = self.here
        for k in range(len(self.chunks)):
            for way in (UP, DOWN):
                for hop in (1, 2, 3):
                    _, valid = here.source(way, hop - 1)
                    pl.when(valid & here.more[way])(
                        lambda k=k, way=way, hop=hop: self.z_send(k, way, hop).wait_send())
            self.c_copy(k, here.z, 0, True).wait_send()
            self.c_copy(k, here.z, 0, False).wait_recv()

            def settle(way, hop, source):
                self.c_copy(k, source, self.index_of(way, hop), True).wait_send()
                self.c_copy(k, source, self.index_of(way, hop), False).wait_recv()
                if self.shared(k):
                    for axis in (0, 1):
                        self.p_copy(k, way, hop, axis, True).wait_send()
                        self.q_copy(k, way, hop, axis, True).wait_send()
            for hop in (1, 2, 3):
                self.ways(hop, settle)
        if self.noted:
            tags, gains = self.outs[-2:]
            width = D // 8
            gains[...] = jnp.zeros_like(gains)
            for i in range(8):
                tags[i : i + 1, :] = self.notes[i // 2, i % 2, 0:1, :]
                for j in range(5):
                    gains[j : j + 1, i * width : (i + 1) * width] = self.notes[
                        i // 2, i % 2, 1 + j : 2 + j, :width
                    ].astype(F32)


def gather_kernel(comm, *refs):
    n_in, n_out = len(comm.inputs), len(comm.out_shapes)
    comm.bind(refs[:n_in], refs[n_in : n_in + n_out], refs[n_in + n_out :])
    comm.here.greet()
    comm.begin()
    comm.begin_sends()
    for step in range(comm.steps):
        comm.step(step)
    comm.finish()


def gather_now(comm):
    return call(functools.partial(gather_kernel, comm), (1,), [], [], comm=comm, collective_id=0)


class Peers(Place):
    def __init__(self):
        super().__init__()
        lat = lax.axis_index("lat")
        self.plane = (self.to_x, self.to_y, (self.rd, lat))
        self.quarters = (self.rx, self.ry, self.rd)
        self.above = [lax.rem(self.z + 1 + i, 4) for i in range(3)]
        self.line = [(self.r, z * 2 + self.c) for z in self.above]

    def greet(self):
        barrier = pltpu.get_barrier_semaphore()
        others = (self.to_core, *self.plane, *self.line)
        for device in others:
            pl.semaphore_signal(barrier, inc=1, device_id=device, device_id_type=MESH)
        pl.semaphore_wait(barrier, len(others))


LINE = (
    ((1, UP, 3), (2, DOWN, 0)),
    ((1, UP, 2), (2, DOWN, 1), (2, UP, 3), (1, DOWN, 0)),
    ((1, UP, 1), (2, DOWN, 2), (2, UP, 2), (1, DOWN, 1)),
    ((3, UP, 3), (0, DOWN, 0)),
)


class LineSum:
    def __init__(self, here, block, arrived, sems):
        self.here, self.block, self.arrived, self.sems = here, block, arrived, sems

    def copy(self, way, dest):
        index = (way, dest - 1 if way == UP else dest)
        return send(self.block(dest), self.arrived.at[index], [s for s in self.sems], index, self.here.to_z[way])

    def start(self):
        @pl.when(self.here.z == 0)
        def _():
            for dest in (3, 2, 1):
                self.copy(UP, dest).start()

        @pl.when(self.here.z == 3)
        def _():
            for dest in (0, 1, 2):
                self.copy(DOWN, dest).start()

    def turn(self, group):
        for device, way, dest in LINE[group]:
            @pl.when(self.here.z == device)
            def _(device=device, way=way, dest=dest):
                self.copy(way, dest).wait_recv()
                ref = self.block(dest)
                ref[...] = ref[...] + self.arrived[way, dest - 1 if way == UP else dest]
                if dest != device:
                    self.copy(way, dest).start()

    def finish(self):
        for dest in (1, 2, 3):
            pl.when(self.here.z < dest)(lambda dest=dest: self.copy(UP, dest).wait_send())
        for dest in (0, 1, 2):
            pl.when(self.here.z > dest)(lambda dest=dest: self.copy(DOWN, dest).wait_send())


class Staged:
    def __init__(self, rows, cols):
        self.shape = (rows, cols)


class WeightSum:
    def __init__(self, chunks, gains=None, tokens=None):
        self.chunks, self.inputs, self.scratch, self.staged = [], [], [], []
        self.sources = 0
        for chunk in chunks:
            parts = []
            for array in chunk:
                shape = (4, 2, 4, array.shape[0] // 32, array.shape[1])
                if isinstance(array, Staged):
                    parts.append((self.sources, None, len(self.staged), shape[-1]))
                    self.staged.append(pltpu.VMEM(shape, BF16))
                else:
                    parts.append((self.sources, len(self.inputs), None, shape[-1]))
                    self.inputs.append(array.reshape(shape))
                self.sources += 1
            self.chunks.append((parts, shape[3], sum(part[3] for part in parts)))
        self.out_shapes = [
            jax.ShapeDtypeStruct((4, rows, cols), BF16) for _, rows, cols in self.chunks
        ]
        for _, rows, cols in self.chunks:
            half = cols // 2
            self.scratch += [
                pltpu.VMEM((4, 2, 2, rows, cols), BF16),
                pltpu.VMEM((4, 2, 2, rows, cols), BF16),
                pltpu.VMEM((2, 4, 2, rows, half), BF16),
                pltpu.VMEM((2, 4, rows, half), BF16),
                pltpu.VMEM((2, 3, rows, cols), BF16),
                pltpu.VMEM((4, rows, cols), BF16),
            ]
        n = len(self.chunks)
        self.scratch += self.staged
        self.scratch += [pltpu.SemaphoreType.DMA((self.sources, 2))]
        for shape in ((self.sources, 2), (n, 2), (n, 2), (n, 2, 3), (n, 3)):
            self.scratch += sem_pair(*shape)
        self.gains, self.tokens = gains, tokens
        if gains is not None:
            self.out_shapes.append(jax.ShapeDtypeStruct(gains, F32))
            self.scratch += [pltpu.VMEM(shape + gains, F32) for shape in ((), (), (4,), (3,))]
            self.scratch += sem_pair(1) + sem_pair(3) + sem_pair(3)
        if tokens is not None:
            self.out_shapes.append(jax.ShapeDtypeStruct((tokens // 8, D), BF16))
            self.scratch += [pltpu.VMEM((4, tokens // 8, D), BF16)]
            self.scratch += [pltpu.VMEM((2, tokens // 8, D), BF16)]
            self.scratch += [pltpu.VMEM((2, 3, tokens // 8, D), BF16)]
            self.scratch += sem_pair(1) + sem_pair(2, 3)
        self.in_specs = [ANYWHERE] * len(self.inputs)
        self.out_specs = [inside(made.shape) for made in self.out_shapes]

    def bind(self, ins, outs, scratch):
        self.here = Peers()
        self.ins, self.outs = ins, outs
        scratch = list(scratch)
        take = lambda n: [scratch.pop(0) for _ in range(n)]
        self.buffers = [take(6) for _ in self.chunks]
        self.stages = take(len(self.staged))
        self.local = take(1)[0]
        self.c_sems, self.x_sems, self.y_sems, self.z_sems, self.g_sems = (take(2) for _ in range(5))
        if self.gains is not None:
            self.gain_buffers = take(4)
            self.gain_sems = [take(2) for _ in range(3)]
        if self.tokens is not None:
            self.token_mine, self.token_window, arrived = take(3)
            self.token_sems = take(2)
            self.token_line = LineSum(self.here, lambda z: self.token_mine.at[z], arrived, take(2))


    def parts(self, k):
        first = 0
        for source, given, staged, width in self.chunks[k][0]:
            ref = self.stages[staged] if given is None else self.ins[given]
            yield source, ref, pl.ds(first, width)
            first += width

    def halves(self, k):
        half = self.chunks[k][2] // 2
        return pl.ds(0, half), pl.ds(half, half)

    def own(self, k):
        for source, ref, cols in self.parts(k):
            for y in range(2):
                yield pltpu.make_async_copy(
                    ref.at[:, self.here.c, pl.ds(2 * y, 2)],
                    self.buffers[k][0].at[:, y, :, :, cols],
                    self.local.at[source, y],
                )

    def to_core(self, k):
        for source, ref, cols in self.parts(k):
            for y in range(2):
                yield send(
                    ref.at[:, 1 - self.here.c, pl.ds(2 * y, 2)],
                    self.buffers[k][1].at[:, y, :, :, cols],
                    self.c_sems, (source, y), self.here.to_core,
                )

    def first_turn(self, k):
        mine, theirs, here = self.buffers[k][0], self.buffers[k][2], self.here
        left, right = self.halves(k)
        yield send(mine.at[:, :, 1 - here.x, :, left], theirs.at[0], self.x_sems, (k, 0), here.to_x)
        yield send(mine.at[:, 1 - here.y, :, :, right], theirs.at[1], self.x_sems, (k, 1), here.to_y)

    def second_turn(self, k):
        mine, theirs, here = self.buffers[k][0], self.buffers[k][3], self.here
        left, right = self.halves(k)
        yield send(mine.at[:, 1 - here.y, here.x, :, left], theirs.at[0], self.y_sems, (k, 0), here.to_y)
        yield send(mine.at[:, here.y, 1 - here.x, :, right], theirs.at[1], self.y_sems, (k, 1), here.to_x)

    def line(self, k):
        here, buffers = self.here, self.buffers[k]
        sems = [sem.at[k] for sem in self.z_sems]
        return LineSum(here, lambda z: buffers[0].at[z, here.y, here.x], buffers[4], sems)

    def finished(self, k):
        for i in range(3):
            mine = self.buffers[k][5].at[self.here.r]
            yield send(mine, mine, self.g_sems, (k, i), self.here.plane[i])

    def arriving(self, k):
        for i in range(3):
            theirs = self.buffers[k][5].at[self.here.quarters[i]]
            yield send(theirs, theirs, self.g_sems, (k, i), self.here.plane[i])


    def start(self, k):
        for copy in (*self.own(k), *self.to_core(k)):
            copy.start()

    def in_chip(self, k):
        for copy in self.own(k):
            copy.wait()
        for copy in self.to_core(k):
            copy.wait_recv()
        mine, theirs = self.buffers[k][:2]
        for z in range(4):
            for y in range(2):
                for x in range(2):
                    mine[z, y, x] = mine[z, y, x] + theirs[z, y, x]
        for copy in self.first_turn(k):
            copy.start()

    def in_pairs(self, k):
        for copy in self.first_turn(k):
            copy.wait()
        mine, theirs, here = self.buffers[k][0], self.buffers[k][2], self.here
        left, right = self.halves(k)
        for z in range(4):
            for i in range(2):
                mine[z, i, here.x, :, left] = mine[z, i, here.x, :, left] + theirs[0, z, i]
                mine[z, here.y, i, :, right] = mine[z, here.y, i, :, right] + theirs[1, z, i]
        for copy in self.second_turn(k):
            copy.start()

    def in_plane(self, k):
        for copy in self.second_turn(k):
            copy.wait()
        mine, theirs, here = self.buffers[k][0], self.buffers[k][3], self.here
        for z in range(4):
            for i, cols in enumerate(self.halves(k)):
                mine[z, here.y, here.x, :, cols] = mine[z, here.y, here.x, :, cols] + theirs[i, z]
        self.line(k).start()

    def turn0(self, k):
        self.line(k).turn(0)

    def turn1(self, k):
        self.line(k).turn(1)

    def turn2(self, k):
        self.line(k).turn(2)

    def in_line(self, k):
        self.line(k).turn(3)
        mine, done, here = self.buffers[k][0], self.buffers[k][5], self.here
        done[here.r] = mine[here.z, here.y, here.x]
        for copy in self.finished(k):
            copy.start()

    def end(self, k):
        for copy in self.arriving(k):
            copy.wait_recv()
        for copy in (*self.to_core(k), *self.finished(k)):
            copy.wait_send()
        self.line(k).finish()
        self.outs[k][...] = self.buffers[k][5][...]


    def gain_copy(self, stage, i):
        mine, core, plane, line = self.gain_buffers
        if stage == 0:
            return send(mine, core, self.gain_sems[0], 0, self.here.to_core)
        if stage == 1:
            return send(mine, plane.at[self.here.r], self.gain_sems[1], i, self.here.plane[i])
        return send(mine, line.at[i], self.gain_sems[2], i, self.here.line[i])

    def gain_plane_recv(self, i):
        mine, _, plane, _ = self.gain_buffers
        return send(mine, plane.at[self.here.quarters[i]], self.gain_sems[1], i, self.here.plane[i])

    def gain_step(self, stage):
        mine, core, plane, line = self.gain_buffers
        if stage == 0:
            self.gain_copy(0, 0).start()
        elif stage == 1:
            self.gain_copy(0, 0).wait()
            mine[...] += core[...]
            plane[self.here.r] = mine[...]
            for i in range(3):
                self.gain_copy(1, i).start()
        elif stage == 2:
            for i in range(3):
                self.gain_copy(1, i).wait_send()
                self.gain_plane_recv(i).wait_recv()
            mine[...] = (plane[0] + plane[1]) + (plane[2] + plane[3])
            for i in range(3):
                self.gain_copy(2, i).start()
        else:
            for i in range(3):
                self.gain_copy(2, i).wait()
            self.outs[len(self.chunks)][...] = (mine[...] + line[0]) + (line[1] + line[2])


    def token_core(self):
        mine = self.token_window.at[self.here.c]
        return send(mine, mine, self.token_sems, 0, self.here.to_core)

    def token_core_recv(self):
        theirs = self.token_window.at[1 - self.here.c]
        return send(theirs, theirs, self.token_sems, 0, self.here.to_core)

    def token_place(self, start):
        self.token_core().wait_send()
        self.token_core_recv().wait_recv()
        count, rows = 2 * self.token_window.shape[1], self.token_mine.shape[1]
        window = self.token_window[...].reshape(count, D)
        for z in range(4):
            slot = lax.broadcasted_iota(jnp.int32, (rows, count), 0) + (2 * z + self.here.c) * rows
            row = lax.broadcasted_iota(jnp.int32, (rows, count), 1) + start
            self.token_mine[z] = low(dot(low(jnp.where(slot == row, 1.0, 0.0)), window))
        self.token_line.start()

    def token_end(self):
        self.token_line.turn(3)
        self.outs[-1][...] = self.token_mine[self.here.z]
        self.token_line.finish()


def tail_kernel(
    comm, lat_ref, do_ref, p_ref, q_ref, kv_ref, gain_ref, wq_ref, wkv_ref, win_ref, start_ref,
    dm1_ref, ds_ref, dm2_ref, *refs,
):
    n_in, n_out = len(comm.inputs), len(comm.out_shapes)
    ins, lg_ref = refs[:n_in], refs[n_in]
    outs, scratch = refs[n_in + 1 : n_in + 1 + n_out], refs[n_in + 1 + n_out :]
    kv_sum, dkv_ref, more_ref, kv_sems = scratch[0], scratch[1], scratch[2], scratch[3:5]
    comm.bind(ins, outs, scratch[5:])
    here = comm.here
    mixed = len(comm.chunks) - 1
    early = range(mixed)
    rows, span = p_ref.shape
    gains = comm.gain_buffers[0]

    here.greet()
    for k in early:
        comm.start(k)
    block = rows // 2
    dwq = None
    gains[...] = jnp.zeros_like(gains)
    for i in range(2):
        at = slice(i * block, (i + 1) * block)
        p, do, q = p_ref[at], do_ref[at], q_ref[at]
        dp = dot_nt(do, kv_ref[:, D:])
        wide_p = p.astype(F32)
        ds = low(wide_p * (dp - jnp.sum(wide_p * dp, axis=1, keepdims=True)))
        dq = low(dot(ds, kv_ref[:, :D]) * CROSS_SCALE)
        dk, dv = dot_tn(ds, q), dot_tn(p, do)
        if i == 0:
            kv_sum[:, :D], kv_sum[:, D:] = dk, dv
        else:
            dkv_ref[:, :D] = low((kv_sum[:, :D] + dk) * CROSS_SCALE)
            dkv_ref[:, D:] = low(kv_sum[:, D:] + dv)
        unit, factor = normed(lat_ref[at].astype(F32))
        gain = gain_ref[0:1, :]
        term = dot_tn(low(unit * gain), dq)
        dwq = term if dwq is None else dwq + term
        back, dgain = norm_back(dot_nt(dq, wq_ref[...]), unit, factor, gain)
        lg_ref[at] = low(back)
        gains[0:1] += dgain
        if i < mixed:
            comm.in_chip(i)
    for k in range(2, mixed):
        comm.in_chip(k)
    half = span // 2
    to_core = send(
        dkv_ref.at[pl.ds(half * (1 - here.c), half)], more_ref, kv_sems, 0, here.to_core)
    to_core.start()
    comm.stages[1][...] = low(dwq).reshape(comm.stages[1].shape)
    gains[2:3], gains[3:4], gains[4:5] = dm1_ref[0:1], ds_ref[0:1], dm2_ref[0:1]
    unit, factor = normed(win_ref[pl.ds(half * here.c, half)].astype(F32))
    gain = gain_ref[1:2, :]
    to_core.wait()
    dkv = low(dkv_ref[pl.ds(half * here.c, half)].astype(F32) + more_ref[...].astype(F32))
    back, dgain = norm_back(dot_nt(dkv, wkv_ref[...]), unit, factor, gain)
    comm.token_window[here.c] = low(back)
    comm.token_core().start()
    gains[1:2] = dgain
    comm.gain_step(0)
    comm.stages[0][...] = low(dot_tn(low(unit * gain), dkv)).reshape(comm.stages[0].shape)
    comm.start(mixed)
    comm.token_place(start_ref[0:1, 0:1])
    for k in early:
        comm.in_pairs(k)
    comm.in_chip(mixed)
    comm.gain_step(1)
    comm.token_line.turn(0)
    for k in early:
        comm.in_plane(k)
    comm.in_pairs(mixed)
    for k in early:
        comm.turn0(k)
    comm.token_line.turn(1)
    for k in early:
        comm.turn1(k)
    comm.in_plane(mixed)
    comm.gain_step(2)
    for k in early:
        comm.turn2(k)
    comm.turn0(mixed)
    comm.token_line.turn(2)
    for k in early:
        comm.in_line(k)
    comm.turn1(mixed)
    comm.gain_step(3)
    comm.turn2(mixed)
    comm.token_end()
    comm.in_line(mixed)
    for k in range(mixed + 1):
        comm.end(k)


def tail(comm, latents, do, p, q, kv, gains, mix, window, start, dgains):
    rows, span = p.shape
    r = (rows, D)
    return call(
        functools.partial(tail_kernel, comm),
        (1,),
        [
            (latents, r, flat),
            (do, r, flat),
            (p, p.shape, flat),
            (q, r, flat),
            (kv, kv.shape, flat),
            (gains, (8, D), flat),
            (mix, (D, D), column(2)),
            (mix, (D, 2 * D), column(0)),
            (window, (span, D), flat),
            (start, start.shape, flat),
        ]
        + [(g, (8, D), flat) for g in dgains],
        [(r, BF16, r, flat)],
        [
            pltpu.VMEM((span, 2 * D), F32),
            pltpu.VMEM((span, 2 * D), BF16),
            pltpu.VMEM((span // 2, 2 * D), BF16),
        ]
        + sem_pair(1),
        comm=comm,
        collective_id=2,
    )


def widen_kernel(cuts, base_ref, term_ref, *refs):
    sources, (sum_ref, *targets) = refs[: len(cuts)], refs[len(cuts) :]
    sum_ref[...] = base_ref[...] + term_ref[...].astype(F32)
    for source, widths in zip(sources, cuts):
        first = 0
        for width in widths:
            targets.pop(0)[...] = source[:, first : first + width].astype(F32)
            first += width


def widen(base, term, arrays, cuts):
    steps = 4
    rows = lambda array: array.shape[0] // steps
    return call(
        functools.partial(widen_kernel, cuts),
        (steps,),
        [(a, (rows(a), a.shape[1]), rows_of) for a in (base, term, *arrays)],
        [(base.shape, F32, (rows(base), base.shape[1]), rows_of)]
        + [
            ((a.shape[0], width), F32, (rows(a), width), rows_of)
            for a, widths in zip(arrays, cuts)
            for width in widths
        ],
    )


def from_partner(shard, bit):
    return lax.ppermute(shard, "lat", [(i, i ^ 1 << bit) for i in range(lax.axis_size("lat"))])


def gather_lat(shard):
    return lax.all_gather(shard, "lat", axis=0, tiled=True)


def halve(value, place, bits):
    kept, more = value, jnp.zeros_like(value)
    for bit in reversed(range(bits)):
        value = low(kept.astype(F32) + more.astype(F32))
        half = value.shape[0] // 2
        upper = place // 2**bit % 2
        kept = lax.dynamic_slice_in_dim(value, upper * half, half)
        more = from_partner(lax.dynamic_slice_in_dim(value, (1 - upper) * half, half), bit)
    return kept, more


def reduce_weights(grad):
    share = lax.psum_scatter(grad, "lat", scatter_dimension=0, tiled=True)
    return lax.psum(share, "row").astype(F32)


def local(
    tokens, latents, segment_ids, pad_mask, block_scene, out_grad,
    gain_cross_q, gain_cross_kv, w_cross_q, w_cross_kv, w_cross_out,
    gain_mlp1, w_up1, w_down1, gain_self, w_self_qkv, w_self_out, gain_mlp2, w_up2, w_down2,
):
    tokens, latents, og = tokens[0], latents[0], out_grad[0]
    rows, slots = latents.shape[0], tokens.shape[0] * lax.axis_size("lat")
    scenes = block_scene.shape[1]
    span = slots // scenes
    place = lax.axis_index("lat")
    group = LAT_SCENE // rows
    bits = group.bit_length() - 1

    block = place * rows // LAT_SCENE
    scene = jnp.sum(jnp.where(jnp.arange(scenes) == block, block_scene[0], 0))
    scene = jnp.broadcast_to(scene, (8, LANES))
    gains = [gain_cross_q, gain_cross_kv, gain_mlp1, gain_self, gain_mlp2]
    first_weights = [[w_cross_kv, w_cross_q, w_cross_out], [w_up1], [w_down1], [w_self_qkv]]
    later_weights = [[w_up2], [w_down2], [w_self_out]]
    planes = lax.axis_size("row") == 4 and lax.axis_size("lat") == 8 and group == 2
    join = lambda gathered: [w.reshape(-1, w.shape[-1]) for w in gathered]
    if planes:
        notes = [segment_ids, pad_mask] + [g.reshape(1, -1) for g in gains]
        *weights, all_tokens, tags, gains = gather_now(Gather(first_weights, tokens, notes))
        mix, up1, down1, qkv, all_tokens = join([*weights, all_tokens])
    else:
        tag = jnp.where(pad_mask == 1, segment_ids, -1)
        tags = gather_lat(low(tag))
        all_tokens = gather_lat(tokens)
        gains = lax.all_gather(jnp.stack(gains), "lat", axis=1, tiled=True)
        gains = jnp.pad(gains.astype(F32), ((0, 3), (0, 0)))
        mix, up1, down1, qkv, up2, down2, so = (
            gather_lat(jnp.concatenate(shards, axis=1)) for shards in first_weights + later_weights
        )

    x1, x2, q, p, o, kv, q2, k2, v2, window, start = front(
        latents, all_tokens, tags, scene, span, gains, mix, up1, down1, qkv
    )
    if planes:
        o2, p2, scale2, k2_more, v2_more, *weights = self_forward(q2, (k2,), (v2,), Gather(later_weights))
        up2, down2, so = join(weights)
        keys, values = (k2, k2_more), (v2, v2_more)
    else:
        for bit in range(bits):
            upper = place // 2**bit % 2 == 1
            more = from_partner((k2, v2), bit)
            k2, v2 = (
                jnp.where(upper, jnp.concatenate([b, a]), jnp.concatenate([a, b]))
                for a, b in zip((k2, v2), more)
            )
        keys, values = (k2,), (v2,)
        o2, p2, scale2 = self_forward(q2, keys, values)
    out, g3, do2, dwup2, dwdown2, dwso, dgain_m2 = second(x2, o2, og, gains, so, up2, down2)
    comm = WeightSum([[dwup2], [dwdown2], [dwso]]) if planes else None
    dq2, dkv2, early = self_backward(q2, do2, o2, scale2, p2, keys, values, comm)
    if planes:
        dk, dv, dk_more, dv_more = dkv2
    else:
        dk, dk_more = halve(dkv2[0], place, bits)
        dv, dv_more = halve(dkv2[1], place, bits)
    g2, dwqkv, dgain_s = qkv_back(x2, g3, dq2, dk, dk_more, dv, dv_more, gains, qkv)
    g1, do, dwup1, dwdown1, dwout, dgain_m1 = first_back(x1, g2, o, gains, mix, up1, down1)
    if planes:
        comm = WeightSum(
            [[dwqkv], [dwup1], [dwdown1], [Staged(D, 2 * D), Staged(D, D), dwout]], gains=(8, D), tokens=slots
        )
        term, *late, dgains, token_grad = tail(
            comm, latents, do, p, q, kv, gains, mix, window, start, (dgain_m1, dgain_s, dgain_m2)
        )
        dgains = lax.dynamic_slice_in_dim(dgains, place * (D // 8), D // 8, axis=1)
        up2, down2, so, qkv, up1, down1, mixed = join([*early, *late])
        latent_grad, token_grad, dwkv, dwq, dwout, *others = widen(
            g1, term, [token_grad, mixed, up1, down1, qkv, so, up2, down2],
            ((D,), (2 * D, D, D), (FF,), (D,), (3 * D,), (D,), (FF,), (D,)),
        )
        sums = dwq, dwkv, dwout, *others
    else:
        latent_grad, dwq, dkv, dgain_q = cross_back(latents, g1, do, p, q, kv, gains, mix)
        mine, more = halve(dkv, place, bits)
        first = place % group * (span // group)
        token_rows = lax.dynamic_slice_in_dim(window, first, span // group)
        token_part, dwkv, dgain_kv = token_back(token_rows, mine, more, gains, mix)
        token_part = lax.dynamic_update_slice_in_dim(
            jnp.zeros((slots, D), BF16), token_part, start[0, 0] + first, 0
        )
        token_grad = lax.psum_scatter(token_part, "lat", scatter_dimension=0, tiled=True).astype(F32)
        dgains = jnp.stack([g[0] for g in (dgain_q, dgain_kv, dgain_m1, dgain_s, dgain_m2)])
        dgains = lax.psum_scatter(low(dgains), "lat", scatter_dimension=1, tiled=True)
        dgains = lax.psum(dgains, "row").astype(F32)
        sums = [
            reduce_weights(g) for g in (dwq, dwkv, dwout, dwup1, dwdown1, dwqkv, dwso, dwup2, dwdown2)
        ]
    dwq, dwkv, dwout, dwup1, dwdown1, dwqkv, dwso, dwup2, dwdown2 = sums
    return (
        out[None],
        latent_grad[None],
        token_grad[None],
        dgains[0],
        dgains[1],
        dwq,
        dwkv,
        dwout,
        dgains[2],
        dwup1,
        dwdown1,
        dgains[3],
        dwqkv,
        dwso,
        dgains[4],
        dwup2,
        dwdown2,
    )


def solution(mesh):
    by_row = P("row", "lat", None)
    weight = P("lat", None)
    gain = P("lat")
    parameters = (
        gain, gain, weight, weight, weight, gain, weight, weight, gain, weight, weight, gain,
        weight, weight,
    )
    return jax.shard_map(
        local,
        mesh=mesh,
        in_specs=(by_row, by_row, P("row", "lat"), P("row", "lat"), P("row", None), by_row)
        + parameters,
        out_specs=(by_row, by_row, by_row) + parameters,
        check_vma=False,
    )
```

```python
import functools

import jax
import jax.numpy as jnp
from jax import lax
from jax.experimental import pallas as pl
from jax.experimental.pallas import tpu as pltpu
from jax.sharding import PartitionSpec as P

D = 512
FF = 2048
HEADS = 8
LAT_SCENE = 2048
HEAD = D // HEADS
PAIRS = HEADS // 2
LANES = 128
FF_STEP = 512
EPS = 1e-05
NEG = -1e30
CROSS_SCALE = D ** (-0.5)
SELF_SCALE = HEAD ** (-0.5)
GELU_C = 0.7978845608028654
GELU_K = 0.044715
VMEM_LIMIT = 60 * 1024 * 1024
F32 = jnp.float32
BF16 = jnp.bfloat16


def low(value):
    return value.astype(BF16)


def dot(left, right):
    return jnp.dot(left, right, preferred_element_type=F32)


def dot_nt(left, right):
    return lax.dot_general(left, right, (((1,), (1,)), ((), ())), preferred_element_type=F32)


def dot_tn(left, right):
    return lax.dot_general(left, right, (((0,), (0,)), ((), ())), preferred_element_type=F32)


def normed(value):
    centered = value - jnp.mean(value, axis=-1, keepdims=True)
    factor = lax.rsqrt(jnp.mean(centered * centered, axis=-1, keepdims=True) + EPS)
    return centered * factor, factor


def norm_back(grad, unit, factor, gain):
    scaled = grad * gain
    inner = (
        scaled
        - jnp.mean(scaled, axis=-1, keepdims=True)
        - unit * jnp.mean(scaled * unit, axis=-1, keepdims=True)
    )
    return factor * inner, jnp.sum(grad * unit, axis=0, keepdims=True)


def gelu(u):
    return 0.5 * u * (1.0 + jnp.tanh(GELU_C * (u + GELU_K * u * u * u)))


def gelu_both(u):
    square = u * u
    t = jnp.tanh(GELU_C * u * (1.0 + GELU_K * square))
    half = 0.5 * (1.0 + t)
    slope = half + 0.5 * u * (1.0 - t * t) * (GELU_C * (1.0 + 3.0 * GELU_K * square))
    return u * half, slope


def call(kernel, grid, ins, outs, scratch=(), comm=None, collective_id=None):
    in_specs = [ANYWHERE if block is None else pl.BlockSpec(block, index) for _, block, index in ins]
    out_specs = [ANYWHERE if block is None else pl.BlockSpec(block, index) for _, _, block, index in outs]
    out_shape = [jax.ShapeDtypeStruct(shape, kind) for shape, kind, _, _ in outs]
    arrays, scratch = [array for array, _, _ in ins], list(scratch)
    if comm is not None:
        arrays += comm.inputs
        in_specs += comm.in_specs
        out_shape += comm.out_shapes
        out_specs += comm.out_specs
        scratch += comm.scratch
    return pl.pallas_call(
        kernel,
        grid=grid,
        in_specs=in_specs,
        out_specs=out_specs,
        out_shape=out_shape,
        scratch_shapes=scratch,
        compiler_params=pltpu.CompilerParams(
            vmem_limit_bytes=VMEM_LIMIT,
            collective_id=None if comm is None else collective_id,
            has_side_effects=comm is not None,
        ),
    )(*arrays)


def inside(shape):
    return pl.BlockSpec(shape, lambda *_: (0,) * len(shape))


ANYWHERE = pl.BlockSpec(memory_space=pl.ANY)


def flat(*_):
    return (0, 0)


def column(c):
    return lambda *_: (0, c)


def rows_of(i, *_):
    return (i, 0)


def front_kernel(
    lat_rows, lat_ref, tok_ref, tags_ref, scene_ref, gain_ref, wq_ref, wkv_ref, wout_ref, wup_ref, wdown_ref, wqkv_ref,
    x1_ref, x2_ref, q_ref, p_ref, o_ref, kv_ref, q2_ref, k2_ref, v2_ref, win_ref, start_ref,
    bias_ref, sem,
):
    @pl.when(pl.program_id(0) == 0)
    def _():
        span, slots = win_ref.shape[0], tok_ref.shape[0]
        tags, scenes = tags_ref[...].astype(F32), scene_ref[...]
        own = lax.axis_index("lat") * lat_rows // LAT_SCENE
        own = lax.broadcasted_iota(jnp.int32, scenes.shape, 1) == own
        scene = jnp.sum(jnp.where(own, scenes, 0).astype(F32))
        count = lambda chosen: jnp.sum(jnp.where(chosen, 1.0, 0.0)).astype(jnp.int32)
        before = count((tags >= 0.0) & (tags < scene))
        length = count(tags == scene)
        start = pl.multiple_of(jnp.minimum(before // 16 * 16, slots - span), 16)
        copy = pltpu.make_async_copy(tok_ref.at[pl.ds(start, span)], win_ref, sem)
        copy.start()
        start_ref[...] = jnp.full(start_ref.shape, start, jnp.int32)
        slot = lax.broadcasted_iota(jnp.int32, bias_ref.shape, 1) + start
        bias_ref[...] = jnp.where((slot >= before) & (slot < before + length), 0.0, NEG)
        copy.wait()
        unit, _ = normed(win_ref[...].astype(F32))
        kv_ref[...] = low(dot(low(unit * gain_ref[1:2, :]), wkv_ref[...]))

    x = lat_ref[...].astype(F32)
    unit, _ = normed(x)
    q = low(dot(low(unit * gain_ref[0:1, :]), wq_ref[...]))
    q_ref[...] = q
    s = dot_nt(q, kv_ref[:, :D]) * CROSS_SCALE + bias_ref[0:1, :]
    e = jnp.exp(s - jnp.max(s, axis=1, keepdims=True))
    p = low(e / jnp.sum(e, axis=1, keepdims=True))
    p_ref[...] = p
    o = low(dot(p, kv_ref[:, D:]))
    o_ref[...] = o
    x1 = x + dot(o, wout_ref[...])
    x1_ref[...] = x1
    unit, _ = normed(x1)
    m1 = low(unit * gain_ref[2:3, :])
    total = x1
    for c in range(FF // FF_STEP):
        cols = slice(c * FF_STEP, (c + 1) * FF_STEP)
        h = low(gelu(dot(m1, wup_ref[:, cols])))
        total = total + dot(h, wdown_ref[cols, :])
    x2_ref[...] = total
    unit, _ = normed(total)
    bn = low(unit * gain_ref[3:4, :])
    q2_ref[...] = low(dot(bn, wqkv_ref[:, :D])) * SELF_SCALE
    k2_ref[...] = low(dot(bn, wqkv_ref[:, D : 2 * D]))
    v2_ref[...] = low(dot(bn, wqkv_ref[:, 2 * D :]))


def front(latents, tokens, tags, scene, span, gains, mix, up1, down1, qkv):
    rows = latents.shape[0]
    block = min(rows, 512)
    r = (block, D)
    return call(
        functools.partial(front_kernel, rows),
        (rows // block,),
        [
            (latents, r, rows_of),
            (tokens, None, None),
            (tags, tags.shape, flat),
            (scene, scene.shape, flat),
            (gains, (8, D), flat),
            (mix, (D, D), column(2)),
            (mix, (D, 2 * D), column(0)),
            (mix, (D, D), column(3)),
            (up1, (D, FF), flat),
            (down1, (FF, D), flat),
            (qkv, (D, 3 * D), flat),
        ],
        [
            ((rows, D), F32, r, rows_of),
            ((rows, D), F32, r, rows_of),
            ((rows, D), BF16, r, rows_of),
            ((rows, span), BF16, (block, span), rows_of),
            ((rows, D), BF16, r, rows_of),
            ((span, 2 * D), BF16, (span, 2 * D), flat),
            ((rows, D), BF16, r, rows_of),
            ((rows, D), BF16, r, rows_of),
            ((rows, D), BF16, r, rows_of),
            ((span, D), BF16, (span, D), flat),
            ((8, LANES), jnp.int32, (8, LANES), flat),
        ],
        [pltpu.VMEM((8, span), F32), pltpu.SemaphoreType.DMA],
    )


def lane_is(shape, head):
    lane = lax.broadcasted_iota(jnp.int32, shape, 1)
    return (lane < HEAD) if head == 0 else (lane >= HEAD)


def only(value, head):
    return jnp.where(lane_is(value.shape, head), value, jnp.zeros_like(value))


def self_forward_kernel(parts, steps, comm, q_ref, *refs):
    refs = list(refs)
    take = lambda n: [refs.pop(0) for _ in range(n)]
    pair, step = pl.program_id(0), pl.program_id(1)
    point = pair * steps + step
    if comm is None:
        k_refs, v_refs = take(parts), take(parts)
        o_ref, p_ref, scale_ref = take(3)
        ones_refs = refs
    else:
        (k_ref,), (v_ref,) = take(1), take(1)
        both = take(2)
        ins = take(len(comm.inputs))
        o_ref, p_ref, scale_ref, k_more, v_more = take(5)
        outs = take(len(comm.out_shapes))
        ones_refs, (landed,), sems = take(2), take(1), take(2)
        comm.bind(ins, outs, refs)
        k_refs, v_refs = (k_ref, k_more), (v_ref, v_more)

        def to_core(i, p):
            cols = pl.ds(p * LANES, LANES)
            return send(both[i].at[:, cols], landed.at[i, p], sems, (i, p), comm.here.to_core)

        @pl.when(point == 0)
        def _():
            comm.here.greet()
            for p in range(PAIRS):
                for i in range(2):
                    to_core(i, p).start()
            comm.begin()

        pl.when(point == 1)(comm.begin_sends)
        for i in range(comm.steps):
            pl.when(point == SHIFT + i)(functools.partial(comm.step, i))

        @pl.when(step == 0)
        def _():
            for i, ref in enumerate((k_more, v_more)):
                arrived = landed.at[i, pair]
                send(arrived, arrived, sems, (i, pair), comm.here.to_core).wait_recv()
                ref[...] = arrived[...]

    @pl.when(step == 0)
    def _():
        for v_ref, ones_ref in zip(v_refs, ones_refs):
            v = v_ref[...]
            for head in range(2):
                ones_ref[head] = jnp.where(lane_is(v.shape, head), v, jnp.ones_like(v))

    q = q_ref[...]
    outs, scales = [], []
    for head in range(2):
        scores = [dot_nt(only(q, head), k_ref[...]) for k_ref in k_refs]
        top = functools.reduce(jnp.maximum, [jnp.max(s, axis=1, keepdims=True) for s in scores])
        mixed, first = None, 0
        for s, ones_ref in zip(scores, ones_refs):
            p = low(jnp.exp(s - top))
            p_ref[head, :, first : first + p.shape[1]] = p
            first += p.shape[1]
            term = dot(p, ones_ref[head])
            mixed = term if mixed is None else mixed + term
        scales.append(1.0 / pltpu.roll(mixed, HEAD, 1))
        outs.append(mixed * scales[-1])
    left = lane_is(outs[0].shape, 0)
    o_ref[...] = low(jnp.where(left, outs[0], outs[1]))
    scale_ref[...] = jnp.where(left, scales[0], scales[1])

    if comm is not None:
        @pl.when(point == PAIRS * steps - 1)
        def _():
            for p in range(PAIRS):
                for i in range(2):
                    to_core(i, p).wait_send()
            comm.finish()


def self_forward(q2, keys, values, comm=None):
    rows = q2.shape[0]
    block = min(rows, 256)
    parts = len(keys)
    total = sum(k.shape[0] for k in keys) * (1 if comm is None else 2)
    whole = lambda array: (array, (array.shape[0], LANES), lambda p, i: (0, p))
    more = ((rows, D), BF16, (rows, LANES), lambda p, i: (0, p))
    beside = comm is not None
    return call(
        functools.partial(self_forward_kernel, parts, rows // block, comm),
        (PAIRS, rows // block),
        [(q2, (block, LANES), lambda p, i: (i, p))]
        + [whole(k) for k in keys]
        + [whole(v) for v in values]
        + ([(keys[0], None, None), (values[0], None, None)] if beside else []),
        [
            ((rows, D), BF16, (block, LANES), lambda p, i: (i, p)),
            ((HEADS, rows, total), BF16, (2, block, total), lambda p, i: (p, i, 0)),
            ((rows, D), F32, (block, LANES), lambda p, i: (i, p)),
        ]
        + ([more, more] if beside else []),
        [pltpu.VMEM((2, k.shape[0], LANES), BF16) for k in keys * (2 if beside else 1)]
        + ([pltpu.VMEM((2, PAIRS, rows, LANES), BF16)] + sem_pair(2, PAIRS) if beside else []),
        comm=comm,
        collective_id=3,
    )


def run_beside(comm, point, plan, odd):
    for when, work in plan.items():
        if when % 2 != odd:
            continue
        def run(when=when, work=work):
            if when == 0:
                comm.here.greet()
            for name, k in work:
                getattr(comm, name)(k)
        pl.when(point == when)(run)


SELF_PLAN = {
    0: (("start", 0), ("start", 1), ("start", 2)),
    4: (("in_chip", 0),),
    6: (("in_chip", 1),),
    7: (("in_chip", 2),),
    10: (("in_pairs", 0),),
    14: (("in_pairs", 1),),
    16: (("in_pairs", 2),),
    17: (("in_plane", 0),),
    20: (("in_plane", 1),),
    21: (("in_plane", 2),),
    23: (("in_line", 0),),
    27: (("in_line", 1),),
    29: (("in_line", 2),),
    31: (("end", 0), ("end", 1), ("end", 2)),
}


def self_backward_kernel(parts, steps, comm, q_ref, do_ref, o_ref, scale_ref, p_ref, *refs):
    refs = list(refs)
    take = lambda n: [refs.pop(0) for _ in range(n)]
    pair, step = pl.program_id(0), pl.program_id(1)
    point = 2 * (pair * steps + step)
    k_refs, v_refs = take(parts), take(parts)
    if comm is None:
        (dq_ref,), dk_refs, dv_refs = take(1), take(parts), take(parts)
        dk_sums, dv_sums = take(parts), take(parts)
    else:
        ins = take(len(comm.inputs))
        dq_ref, dk_ref, dv_ref, *landed = take(5)
        outs = take(len(comm.out_shapes))
        dk_sums, dv_sums, (stage,), sems = take(parts), take(parts), take(1), take(2)
        comm.bind(ins, outs, refs)
        dk_refs, dv_refs = (dk_ref, stage.at[0, pair]), (dv_ref, stage.at[1, pair])

        def to_core(i, p):
            cols = pl.ds(pl.multiple_of(p * LANES, LANES), LANES)
            return send(stage.at[i, p], landed[i].at[:, cols], sems, (i, p), comm.here.to_core)

        run_beside(comm, point, SELF_PLAN, 0)

    @pl.when(step == 0)
    def _():
        for ref in (*dk_sums, *dv_sums):
            ref[...] = jnp.zeros_like(ref)

    q = q_ref[...]
    do = low(do_ref[...].astype(F32) * scale_ref[...])
    product = do.astype(F32) * o_ref[...].astype(F32)
    q_turned, do_turned = jnp.transpose(q), jnp.transpose(do)
    dqs = []
    for head in range(2):
        rows = slice(head * HEAD, (head + 1) * HEAD)
        doz = only(do, head)
        delta = jnp.sum(only(product, head), axis=1, keepdims=True)
        dq, first = None, 0
        for k_ref, v_ref, dk_sum, dv_sum in zip(k_refs, v_refs, dk_sums, dv_sums):
            count = k_ref.shape[0]
            p = p_ref[head, :, first : first + count]
            first += count
            ds = low(p.astype(F32) * (dot_nt(doz, v_ref[...]) - delta))
            dv_sum[rows, :] += dot(do_turned[rows], p)
            dk_sum[rows, :] += dot(q_turned[rows], ds)
            term = dot(ds, k_ref[...])
            dq = term if dq is None else dq + term
        dqs.append(dq)
    dq_ref[...] = low(jnp.where(lane_is(dqs[0].shape, 0), dqs[0], dqs[1]) * SELF_SCALE)

    @pl.when(step == steps - 1)
    def _():
        for ref, total in zip((*dk_refs, *dv_refs), (*dk_sums, *dv_sums)):
            ref[...] = jnp.transpose(low(total[...]))
        if comm is not None:
            for i in range(2):
                to_core(i, pair).start()

    if comm is not None:
        run_beside(comm, point + 1, SELF_PLAN, 1)

        @pl.when(point == 2 * (PAIRS * steps - 1))
        def _():
            for p in range(PAIRS):
                for i in range(2):
                    to_core(i, p).wait()


def self_backward(q2, do2, o2, scale2, p2, keys, values, comm=None):
    rows = q2.shape[0]
    block = min(rows, 256)
    parts = len(keys)
    whole = lambda array: (array, (array.shape[0], LANES), lambda p, i: (0, p))
    made = lambda array: (array.shape, BF16, (array.shape[0], LANES), lambda p, i: (0, p))
    if comm is None:
        outs, extra = [made(k) for k in keys] + [made(v) for v in values], []
    else:
        outs = [made(keys[0]), made(values[0])] + [((rows, D), BF16, None, None)] * 2
        extra = [pltpu.VMEM((2, PAIRS, rows, LANES), BF16)] + sem_pair(2, PAIRS)
    out = call(
        functools.partial(self_backward_kernel, parts, rows // block, comm),
        (PAIRS, rows // block),
        [
            (q2, (block, LANES), lambda p, i: (i, p)),
            (do2, (block, LANES), lambda p, i: (i, p)),
            (o2, (block, LANES), lambda p, i: (i, p)),
            (scale2, (block, LANES), lambda p, i: (i, p)),
            (p2, (2, block, p2.shape[2]), lambda p, i: (p, i, 0)),
        ]
        + [whole(k) for k in keys]
        + [whole(v) for v in values],
        [((rows, D), BF16, (block, LANES), lambda p, i: (i, p))] + outs,
        [pltpu.VMEM((LANES, k.shape[0]), F32) for k in (*keys, *values)] + extra,
        comm=comm,
        collective_id=1,
    )
    return out[0], out[1 : 1 + len(outs)], out[1 + len(outs) :]


def second_kernel(
    steps, x2_ref, o2_ref, og_ref, gain_ref, wso_ref, wup_ref, wdown_ref,
    out_ref, g3_ref, do_ref, dwup_ref, dwdown_ref, dwso_ref, dgain_ref,
    m_ref, f_ref, dm_ref,
):
    c = pl.program_id(0)

    @pl.when(c == 0)
    def _():
        x3 = x2_ref[...] + dot(o2_ref[...], wso_ref[...])
        unit, _ = normed(x3)
        m_ref[...] = low(unit * gain_ref[4:5, :])
        out_ref[...] = x3
        f_ref[...] = jnp.zeros_like(f_ref)
        dm_ref[...] = jnp.zeros_like(dm_ref)

    m, og = m_ref[...], og_ref[...]
    h, slope = gelu_both(dot(m, wup_ref[...]))
    h = low(h)
    f_ref[...] += dot(h, wdown_ref[...])
    dwdown_ref[...] = low(dot_tn(h, og))
    du = low(slope * dot_nt(og, wdown_ref[...]))
    dwup_ref[...] = low(dot_tn(m, du))
    dm_ref[...] += dot_nt(du, wup_ref[...])

    @pl.when(c == steps - 1)
    def _():
        x3 = out_ref[...]
        unit, factor = normed(x3)
        out_ref[...] = x3 + f_ref[...]
        back, dgain = norm_back(dm_ref[...], unit, factor, gain_ref[4:5, :])
        g3 = og_ref[...].astype(F32) + back
        g3_ref[...] = g3
        dgain_ref[...] = jnp.broadcast_to(dgain, dgain_ref.shape)
        b3 = low(g3)
        o2 = o2_ref[...]
        dwso_ref[...] = low(dot_tn(o2, b3))
        do_ref[...] = low(dot_nt(b3, wso_ref[...]))


def second(x2, o2, og, gains, so, up2, down2):
    rows = x2.shape[0]
    steps = FF // FF_STEP
    r = (rows, D)
    return call(
        functools.partial(second_kernel, steps),
        (steps,),
        [
            (x2, r, flat),
            (o2, r, flat),
            (og, r, flat),
            (gains, (8, D), flat),
            (so, (D, D), flat),
            (up2, (D, FF_STEP), lambda c: (0, c)),
            (down2, (FF_STEP, D), lambda c: (c, 0)),
        ],
        [
            (r, F32, r, flat),
            (r, F32, r, flat),
            (r, BF16, r, flat),
            ((D, FF), BF16, (D, FF_STEP), lambda c: (0, c)),
            ((FF, D), BF16, (FF_STEP, D), lambda c: (c, 0)),
            ((D, D), BF16, (D, D), flat),
            ((8, D), F32, (8, D), flat),
        ],
        [pltpu.VMEM(r, BF16), pltpu.VMEM(r, F32), pltpu.VMEM(r, F32)],
    )


def qkv_back_kernel(
    x2_ref, g3_ref, dq_ref, dk_ref, dk_more_ref, dv_ref, dv_more_ref, gain_ref, w_ref,
    g2_ref, dw_ref, dgain_ref,
):
    unit, factor = normed(x2_ref[...])
    gain = gain_ref[3:4, :]
    bn = low(unit * gain)
    dq = dq_ref[...]
    dk = low(dk_ref[...].astype(F32) + dk_more_ref[...].astype(F32))
    dv = low(dv_ref[...].astype(F32) + dv_more_ref[...].astype(F32))
    dbn = None
    for i, part in enumerate((dq, dk, dv)):
        cols = slice(i * D, (i + 1) * D)
        dw_ref[:, cols] = low(dot_tn(bn, part))
        term = dot_nt(part, w_ref[:, cols])
        dbn = term if dbn is None else dbn + term
    back, dgain = norm_back(dbn, unit, factor, gain)
    g2_ref[...] = g3_ref[...] + back
    dgain_ref[...] = jnp.broadcast_to(dgain, dgain_ref.shape)


def qkv_back(x2, g3, dq, dk, dk_more, dv, dv_more, gains, qkv):
    rows = x2.shape[0]
    r = (rows, D)
    return call(
        qkv_back_kernel,
        (1,),
        [(a, r, flat) for a in (x2, g3, dq, dk, dk_more, dv, dv_more)]
        + [(gains, (8, D), flat), (qkv, (D, 3 * D), flat)],
        [
            (r, F32, r, flat),
            ((D, 3 * D), BF16, (D, 3 * D), flat),
            ((8, D), F32, (8, D), flat),
        ],
    )


def first_back_kernel(
    steps, x1_ref, g2_ref, o_ref, gain_ref, wout_ref, wup_ref, wdown_ref,
    g1_ref, do_ref, dwup_ref, dwdown_ref, dwout_ref, dgain_ref,
    m_ref, b_ref, dm_ref,
):
    c = pl.program_id(0)

    @pl.when(c == 0)
    def _():
        unit, _ = normed(x1_ref[...])
        m_ref[...] = low(unit * gain_ref[2:3, :])
        b_ref[...] = low(g2_ref[...])
        dm_ref[...] = jnp.zeros_like(dm_ref)

    m, b = m_ref[...], b_ref[...]
    h, slope = gelu_both(dot(m, wup_ref[...]))
    dwdown_ref[...] = low(dot_tn(low(h), b))
    du = low(slope * dot_nt(b, wdown_ref[...]))
    dwup_ref[...] = low(dot_tn(m, du))
    dm_ref[...] += dot_nt(du, wup_ref[...])

    @pl.when(c == steps - 1)
    def _():
        unit, factor = normed(x1_ref[...])
        back, dgain = norm_back(dm_ref[...], unit, factor, gain_ref[2:3, :])
        g1 = g2_ref[...] + back
        g1_ref[...] = g1
        dgain_ref[...] = jnp.broadcast_to(dgain, dgain_ref.shape)
        b1 = low(g1)
        dwout_ref[...] = low(dot_tn(o_ref[...], b1))
        do_ref[...] = low(dot_nt(b1, wout_ref[...]))


def first_back(x1, g2, o, gains, mix, up1, down1):
    rows = x1.shape[0]
    steps = FF // FF_STEP
    r = (rows, D)
    return call(
        functools.partial(first_back_kernel, steps),
        (steps,),
        [
            (x1, r, flat),
            (g2, r, flat),
            (o, r, flat),
            (gains, (8, D), flat),
            (mix, (D, D), column(3)),
            (up1, (D, FF_STEP), lambda c: (0, c)),
            (down1, (FF_STEP, D), lambda c: (c, 0)),
        ],
        [
            (r, F32, r, flat),
            (r, BF16, r, flat),
            ((D, FF), BF16, (D, FF_STEP), lambda c: (0, c)),
            ((FF, D), BF16, (FF_STEP, D), lambda c: (c, 0)),
            ((D, D), BF16, (D, D), flat),
            ((8, D), F32, (8, D), flat),
        ],
        [pltpu.VMEM(r, BF16), pltpu.VMEM(r, BF16), pltpu.VMEM(r, F32)],
    )


def cross_back_kernel(
    steps, lat_ref, g1_ref, do_ref, p_ref, q_ref, kv_ref, gain_ref, wq_ref,
    lg_ref, dwq_ref, dkv_ref, dgain_ref, dk_sum, dv_sum, dwq_sum,
):
    i = pl.program_id(0)

    @pl.when(i == 0)
    def _():
        for ref in (dk_sum, dv_sum, dwq_sum, dgain_ref):
            ref[...] = jnp.zeros_like(ref)

    p, do, q = p_ref[...], do_ref[...], q_ref[...]
    dp = dot_nt(do, kv_ref[:, D:])
    wide_p = p.astype(F32)
    ds = low(wide_p * (dp - jnp.sum(wide_p * dp, axis=1, keepdims=True)))
    dq = low(dot(ds, kv_ref[:, :D]) * CROSS_SCALE)
    dk_sum[...] += dot_tn(ds, q)
    dv_sum[...] += dot_tn(p, do)
    unit, factor = normed(lat_ref[...].astype(F32))
    gain = gain_ref[0:1, :]
    dwq_sum[...] += dot_tn(low(unit * gain), dq)
    back, dgain = norm_back(dot_nt(dq, wq_ref[...]), unit, factor, gain)
    lg_ref[...] = g1_ref[...] + back
    dgain_ref[...] += jnp.broadcast_to(dgain, dgain_ref.shape)

    @pl.when(i == steps - 1)
    def _():
        dwq_ref[...] = low(dwq_sum[...])
        dkv_ref[:, :D] = low(dk_sum[...] * CROSS_SCALE)
        dkv_ref[:, D:] = low(dv_sum[...])


def cross_back(latents, g1, do, p, q, kv, gains, mix):
    rows, span = p.shape
    block = min(rows, 512)
    r = (block, D)
    return call(
        functools.partial(cross_back_kernel, rows // block),
        (rows // block,),
        [
            (latents, r, rows_of),
            (g1, r, rows_of),
            (do, r, rows_of),
            (p, (block, span), rows_of),
            (q, r, rows_of),
            (kv, (span, 2 * D), flat),
            (gains, (8, D), flat),
            (mix, (D, D), column(2)),
        ],
        [
            ((rows, D), F32, r, rows_of),
            ((D, D), BF16, (D, D), flat),
            ((span, 2 * D), BF16, (span, 2 * D), flat),
            ((8, D), F32, (8, D), flat),
        ],
        [pltpu.VMEM((span, D), F32), pltpu.VMEM((span, D), F32), pltpu.VMEM((D, D), F32)],
    )


def token_back_kernel(tok_ref, dkv_ref, more_ref, gain_ref, w_ref, tg_ref, dw_ref, dgain_ref):
    unit, factor = normed(tok_ref[...].astype(F32))
    gain = gain_ref[1:2, :]
    dkv = low(dkv_ref[...].astype(F32) + more_ref[...].astype(F32))
    dw_ref[...] = low(dot_tn(low(unit * gain), dkv))
    back, dgain = norm_back(dot_nt(dkv, w_ref[...]), unit, factor, gain)
    tg_ref[...] = low(back)
    dgain_ref[...] = jnp.broadcast_to(dgain, dgain_ref.shape)


def token_back(tokens, dkv, more, gains, mix):
    rows = tokens.shape[0]
    return call(
        token_back_kernel,
        (1,),
        [
            (tokens, (rows, D), flat),
            (dkv, (rows, 2 * D), flat),
            (more, (rows, 2 * D), flat),
            (gains, (8, D), flat),
            (mix, (D, 2 * D), column(0)),
        ],
        [
            ((rows, D), BF16, (rows, D), flat),
            ((D, 2 * D), BF16, (D, 2 * D), flat),
            ((8, D), F32, (8, D), flat),
        ],
    )


MESH = pl.DeviceIdType.MESH
UP, DOWN = 0, 1


class Place:
    def __init__(self):
        row, lat = lax.axis_index("row"), lax.axis_index("lat")
        self.x, self.y, self.z, self.c = row % 2, row // 2, lat // 2, lat % 2
        self.r = row
        self.rx = self.y * 2 + 1 - self.x
        self.ry = (1 - self.y) * 2 + self.x
        self.rd = (1 - self.y) * 2 + 1 - self.x
        self.to_x, self.to_y = (self.rx, lat), (self.ry, lat)
        self.to_core = (row, self.z * 2 + 1 - self.c)
        self.to_z = ((row, lat + 2), (row, lat - 2))
        self.more = (self.z < 3, self.z > 0)

    def greet(self):
        barrier = pltpu.get_barrier_semaphore()
        for device in (self.to_x, self.to_y, self.to_core):
            pl.semaphore_signal(barrier, inc=1, device_id=device, device_id_type=MESH)
        for way in (UP, DOWN):
            @pl.when(self.more[way])
            def _():
                pl.semaphore_signal(barrier, inc=1, device_id=self.to_z[way], device_id_type=MESH)
        pl.semaphore_wait(barrier, 3 + jnp.minimum(self.z, 1) + jnp.minimum(3 - self.z, 1))

    def source(self, way, hop):
        return (self.z - hop, self.z >= hop) if way == UP else (self.z + hop, self.z + hop <= 3)


def send(src, dst, sems, index, device):
    return pltpu.make_async_remote_copy(
        src_ref=src, dst_ref=dst, send_sem=sems[0].at[index], recv_sem=sems[1].at[index],
        device_id=device, device_id_type=MESH,
    )


def sem_pair(*shape):
    return [pltpu.SemaphoreType.DMA(shape), pltpu.SemaphoreType.DMA(shape)]


TOKEN_PARTS = 4
AHEAD = 2
GAP = 2
SHIFT = 3
WEIGHT, TOKENS, NOTES = range(3)


class Gather:
    def __init__(self, weights, tokens=None, notes=()):
        self.inputs, self.out_shapes, self.chunks = [], [], []
        self.shards = []
        for shards in weights:
            shape = (4, shards[0].shape[0] // 4)
            self.shards.append([])
            for shard in shards:
                self.shards[-1].append((len(self.inputs), shard.shape[1]))
                self.inputs.append(shard.reshape(shape + shard.shape[1:]))
            cols = sum(shard.shape[1] for shard in shards)
            self.out_shapes.append(jax.ShapeDtypeStruct((4, 2) + shape + (cols,), BF16))
        self.chunks = [(WEIGHT, k) for k in range(len(weights))]
        self.out_specs = [ANYWHERE] * len(weights)
        self.copies = len(self.inputs)
        self.scratch = []
        self.noted = len(notes)
        if tokens is not None:
            self.inputs += [tokens, *notes]
            self.out_shapes += [
                jax.ShapeDtypeStruct((4, 2) + tokens.shape, BF16),
                jax.ShapeDtypeStruct((8, tokens.shape[0]), BF16),
                jax.ShapeDtypeStruct((8, D), F32),
            ]
            self.out_specs += [ANYWHERE] + [inside(made.shape) for made in self.out_shapes[-2:]]
            self.chunks = [(NOTES, 0)] + self.chunks + [(TOKENS, k) for k in range(TOKEN_PARTS)]
            self.scratch.append(pltpu.VMEM((4, 2, 16, tokens.shape[0]), BF16))
            self.copies += 1
        self.in_specs = [inside(array.shape) for array in self.inputs]
        n = len(self.chunks)
        self.scratch += [pltpu.SemaphoreType.DMA((self.copies,))]
        for shape in ((n, 2, 3), (n, 2, 3, 2), (n, 2, 3, 2), (n, 7)):
            self.scratch += sem_pair(*shape)
        self.steps = n + 4 * GAP + 1

    def bind(self, ins, outs, scratch):
        self.here, self.ins, self.outs = Place(), ins, outs
        scratch = list(scratch)
        take = lambda n: [scratch.pop(0) for _ in range(n)]
        if self.noted:
            self.notes = take(1)[0]
        self.local = take(1)[0]
        self.z_sems, self.p_sems, self.q_sems, self.c_sems = (take(2) for _ in range(4))

    def block(self, k, source, core=None):
        kind, index = self.chunks[k]
        core = self.here.c if core is None else core
        if kind == NOTES:
            return self.notes.at[source, core]
        if kind == TOKENS:
            tokens = self.outs[len(self.shards)]
            rows = tokens.shape[2] // TOKEN_PARTS
            return tokens.at[source, core, pl.ds(index * rows, rows)]
        return self.outs[index].at[source, core]

    def piece(self, k, source, quarter, half=None):
        if not self.shared(k):
            return self.block(k, source)
        ref = self.outs[self.chunks[k][1]]
        if half is None:
            return ref.at[source, self.here.c, quarter]
        width = ref.shape[-1] // 2
        return ref.at[source, self.here.c, quarter, :, pl.ds(half * width, width)]

    def shared(self, k):
        return self.chunks[k][0] == WEIGHT

    def z_send(self, k, way, hop):
        source, _ = self.here.source(way, hop - 1)
        ref = self.piece(k, source, self.here.r)
        return send(ref, ref, self.z_sems, (k, way, hop - 1), self.here.to_z[way])

    def z_recv(self, k, way, hop):
        source, _ = self.here.source(way, hop)
        ref = self.piece(k, source, self.here.r)
        return send(ref, ref, self.z_sems, (k, way, hop - 1), self.here.to_z[way])

    def p_copy(self, k, way, hop, axis, mine):
        here = self.here
        source, _ = here.source(way, hop)
        ref = self.piece(k, source, here.r if mine else (here.rx, here.ry)[axis])
        return send(ref, ref, self.p_sems, (k, way, hop - 1, axis), (here.to_x, here.to_y)[axis])

    def q_copy(self, k, way, hop, half, mine):
        here = self.here
        source, _ = here.source(way, hop)
        ref = self.piece(k, source, (here.rx, here.ry)[half] if mine else here.rd, half)
        return send(ref, ref, self.q_sems, (k, way, hop - 1, half), (here.to_y, here.to_x)[half])

    def c_copy(self, k, source, index, mine):
        ref = self.block(k, source, self.here.c if mine else 1 - self.here.c)
        return send(ref, ref, self.c_sems, (k, index), self.here.to_core)

    def ways(self, hop, fn):
        for way in (UP, DOWN):
            source, valid = self.here.source(way, hop)
            pl.when(valid)(functools.partial(fn, way, hop, source))

    @staticmethod
    def index_of(way, hop):
        return 1 + way * 3 + hop - 1

    def first_sends(self, k):
        for way in (UP, DOWN):
            pl.when(self.here.more[way])(lambda way=way: self.z_send(k, way, 1).start())
        self.c_copy(k, self.here.z, 0, True).start()

    def stage_z(self, k, hop):
        def arrive(way, hop, source):
            self.z_recv(k, way, hop).wait_recv()
            if hop < 3:
                pl.when(self.here.more[way])(lambda: self.z_send(k, way, hop + 1).start())
            if self.shared(k):
                self.p_copy(k, way, hop, 0, True).start()
                self.p_copy(k, way, hop, 1, True).start()
            else:
                self.c_copy(k, source, self.index_of(way, hop), True).start()
        self.ways(hop, arrive)

    def stage_p(self, k, hop):
        def arrive(way, hop, source):
            for axis in (0, 1):
                self.p_copy(k, way, hop, axis, False).wait_recv()
                self.q_copy(k, way, hop, axis, True).start()
        self.ways(hop, arrive)

    def stage_q(self, k, hop):
        def arrive(way, hop, source):
            self.q_copy(k, way, hop, 0, False).wait_recv()
            self.q_copy(k, way, hop, 1, False).wait_recv()
            self.c_copy(k, source, self.index_of(way, hop), True).start()
        self.ways(hop, arrive)

    def local_copies(self):
        z, c = self.here.z, self.here.c
        copies = []
        for k, shards in enumerate(self.shards):
            first = 0
            for index, width in shards:
                copies.append(pltpu.make_async_copy(
                    self.ins[index], self.outs[k].at[z, c, :, :, pl.ds(first, width)],
                    self.local.at[len(copies)]))
                first += width
        if self.noted:
            copies.append(pltpu.make_async_copy(
                self.ins[len(copies)], self.outs[len(self.shards)].at[z, c], self.local.at[len(copies)]))
        return copies

    def begin(self):
        for copy in self.local_copies():
            copy.start()
        if self.noted:
            z, c = self.here.z, self.here.c
            scenes, mask, *gains = self.ins[self.copies :]
            self.notes[z, c] = jnp.zeros(self.notes.shape[2:], BF16)
            self.notes[z, c, 0:1, :] = low(jnp.where(mask[...] == 1, scenes[...], -1).astype(F32))
            for i, gain in enumerate(gains):
                self.notes[z, c, 1 + i : 2 + i, : gain.shape[1]] = gain[...]

    def begin_sends(self):
        for copy in self.local_copies():
            copy.wait()
        for k in range(min(AHEAD, len(self.chunks))):
            self.first_sends(k)

    def step(self, step):
        total = len(self.chunks)
        if step + AHEAD < total:
            self.first_sends(step + AHEAD)
        for lag, stage in ((0, self.stage_z), (GAP, self.stage_p), (2 * GAP, self.stage_q)):
            for hop in (1, 2, 3):
                k = step - lag - GAP * (hop - 1)
                if 0 <= k < total and (lag == 0 or self.shared(k)):
                    stage(k, hop)

    def finish(self):
        here = self.here
        for k in range(len(self.chunks)):
            for way in (UP, DOWN):
                for hop in (1, 2, 3):
                    _, valid = here.source(way, hop - 1)
                    pl.when(valid & here.more[way])(
                        lambda k=k, way=way, hop=hop: self.z_send(k, way, hop).wait_send())
            self.c_copy(k, here.z, 0, True).wait_send()
            self.c_copy(k, here.z, 0, False).wait_recv()

            def settle(way, hop, source):
                self.c_copy(k, source, self.index_of(way, hop), True).wait_send()
                self.c_copy(k, source, self.index_of(way, hop), False).wait_recv()
                if self.shared(k):
                    for axis in (0, 1):
                        self.p_copy(k, way, hop, axis, True).wait_send()
                        self.q_copy(k, way, hop, axis, True).wait_send()
            for hop in (1, 2, 3):
                self.ways(hop, settle)
        if self.noted:
            tags, gains = self.outs[-2:]
            width = D // 8
            gains[...] = jnp.zeros_like(gains)
            for i in range(8):
                tags[i : i + 1, :] = self.notes[i // 2, i % 2, 0:1, :]
                for j in range(5):
                    gains[j : j + 1, i * width : (i + 1) * width] = self.notes[
                        i // 2, i % 2, 1 + j : 2 + j, :width
                    ].astype(F32)


def gather_kernel(comm, *refs):
    n_in, n_out = len(comm.inputs), len(comm.out_shapes)
    comm.bind(refs[:n_in], refs[n_in : n_in + n_out], refs[n_in + n_out :])
    comm.here.greet()
    comm.begin()
    comm.begin_sends()
    for step in range(comm.steps):
        comm.step(step)
    comm.finish()


def gather_now(comm):
    return call(functools.partial(gather_kernel, comm), (1,), [], [], comm=comm, collective_id=0)


class Peers(Place):
    def __init__(self):
        super().__init__()
        lat = lax.axis_index("lat")
        self.plane = (self.to_x, self.to_y, (self.rd, lat))
        self.quarters = (self.rx, self.ry, self.rd)
        self.above = [lax.rem(self.z + 1 + i, 4) for i in range(3)]
        self.line = [(self.r, z * 2 + self.c) for z in self.above]

    def greet(self):
        barrier = pltpu.get_barrier_semaphore()
        others = (self.to_core, *self.plane, *self.line)
        for device in others:
            pl.semaphore_signal(barrier, inc=1, device_id=device, device_id_type=MESH)
        pl.semaphore_wait(barrier, len(others))


LINE = (
    ((1, UP, 3), (2, DOWN, 0)),
    ((1, UP, 2), (2, DOWN, 1), (2, UP, 3), (1, DOWN, 0)),
    ((1, UP, 1), (2, DOWN, 2), (2, UP, 2), (1, DOWN, 1)),
    ((3, UP, 3), (0, DOWN, 0)),
)


class LineSum:
    def __init__(self, here, block, arrived, sems):
        self.here, self.block, self.arrived, self.sems = here, block, arrived, sems

    def copy(self, way, dest):
        index = (way, dest - 1 if way == UP else dest)
        return send(self.block(dest), self.arrived.at[index], self.sems, index, self.here.to_z[way])

    def start(self):
        @pl.when(self.here.z == 0)
        def _():
            for dest in (3, 2, 1):
                self.copy(UP, dest).start()

        @pl.when(self.here.z == 3)
        def _():
            for dest in (0, 1, 2):
                self.copy(DOWN, dest).start()

    def turn(self, group):
        for device, way, dest in LINE[group]:
            @pl.when(self.here.z == device)
            def _(device=device, way=way, dest=dest):
                self.copy(way, dest).wait_recv()
                ref = self.block(dest)
                ref[...] = ref[...] + self.arrived[way, dest - 1 if way == UP else dest]
                if dest != device:
                    self.copy(way, dest).start()

    def finish(self):
        for dest in (1, 2, 3):
            pl.when(self.here.z < dest)(lambda dest=dest: self.copy(UP, dest).wait_send())
        for dest in (0, 1, 2):
            pl.when(self.here.z > dest)(lambda dest=dest: self.copy(DOWN, dest).wait_send())


class DirectSum(LineSum):
    def copy(self, i):
        return send(self.block(self.here.above[i]), self.arrived.at[0, i], self.sems, (0, i), self.here.line[i])

    def start(self):
        for i in range(3):
            self.copy(i).start()

    def turn(self, group):
        if group == len(LINE) - 1:
            for i in range(3):
                self.copy(i).wait()
            ref, arrived = self.block(self.here.z), self.arrived
            total = ref[...].astype(F32) + arrived[0, 0].astype(F32)
            ref[...] = low(total + arrived[0, 1].astype(F32) + arrived[0, 2].astype(F32))

    def finish(self):
        pass


class Staged:
    def __init__(self, rows, cols):
        self.shape = (rows, cols)


class WeightSum:
    def __init__(self, chunks, gains=None, tokens=None, direct=()):
        self.direct = direct
        self.chunks, self.inputs, self.scratch, self.staged = [], [], [], []
        self.sources = 0
        for chunk in chunks:
            parts = []
            for array in chunk:
                shape = (4, 2, 4, array.shape[0] // 32, array.shape[1])
                if isinstance(array, Staged):
                    parts.append((self.sources, None, len(self.staged), shape[-1]))
                    self.staged.append(pltpu.VMEM(shape, BF16))
                else:
                    parts.append((self.sources, len(self.inputs), None, shape[-1]))
                    self.inputs.append(array.reshape(shape))
                self.sources += 1
            self.chunks.append((parts, shape[3], sum(part[3] for part in parts)))
        self.out_shapes = [
            jax.ShapeDtypeStruct((4, rows, cols), BF16) for _, rows, cols in self.chunks
        ]
        for _, rows, cols in self.chunks:
            half = cols // 2
            self.scratch += [
                pltpu.VMEM((4, 2, 2, rows, cols), BF16),
                pltpu.VMEM((4, 2, 2, rows, cols), BF16),
                pltpu.VMEM((2, 4, 2, rows, half), BF16),
                pltpu.VMEM((2, 4, rows, half), BF16),
                pltpu.VMEM((2, 3, rows, cols), BF16),
                pltpu.VMEM((4, rows, cols), BF16),
            ]
        n = len(self.chunks)
        self.scratch += self.staged
        self.scratch += [pltpu.SemaphoreType.DMA((self.sources, 2))]
        for shape in ((self.sources, 2), (n, 2), (n, 2), (n, 2, 3), (n, 3)):
            self.scratch += sem_pair(*shape)
        self.gains, self.tokens = gains, tokens
        if gains is not None:
            self.out_shapes.append(jax.ShapeDtypeStruct(gains, F32))
            self.scratch += [pltpu.VMEM(shape + gains, F32) for shape in ((), (), (4,), (3,))]
            self.scratch += sem_pair(1) + sem_pair(3) + sem_pair(3)
        if tokens is not None:
            self.out_shapes.append(jax.ShapeDtypeStruct((tokens // 8, D), BF16))
            self.scratch += [pltpu.VMEM((4, tokens // 8, D), BF16)]
            self.scratch += [pltpu.VMEM((2, tokens // 8, D), BF16)]
            self.scratch += [pltpu.VMEM((2, 3, tokens // 8, D), BF16)]
            self.scratch += sem_pair(1) + sem_pair(2, 3)
        self.in_specs = [ANYWHERE] * len(self.inputs)
        self.out_specs = [inside(made.shape) for made in self.out_shapes]

    def bind(self, ins, outs, scratch):
        self.here = Peers()
        self.ins, self.outs = ins, outs
        scratch = list(scratch)
        take = lambda n: [scratch.pop(0) for _ in range(n)]
        self.buffers = [take(6) for _ in self.chunks]
        self.stages = take(len(self.staged))
        self.local = take(1)[0]
        self.c_sems, self.x_sems, self.y_sems, self.z_sems, self.g_sems = (take(2) for _ in range(5))
        if self.gains is not None:
            self.gain_buffers = take(4)
            self.gain_sems = [take(2) for _ in range(3)]
        if self.tokens is not None:
            self.token_mine, self.token_window, arrived = take(3)
            self.token_sems = take(2)
            self.token_line = LineSum(self.here, lambda z: self.token_mine.at[z], arrived, take(2))


    def parts(self, k):
        first = 0
        for source, given, staged, width in self.chunks[k][0]:
            ref = self.stages[staged] if given is None else self.ins[given]
            yield source, ref, pl.ds(first, width)
            first += width

    def halves(self, k):
        half = self.chunks[k][2] // 2
        return pl.ds(0, half), pl.ds(half, half)

    def own(self, k):
        for source, ref, cols in self.parts(k):
            for y in range(2):
                yield pltpu.make_async_copy(
                    ref.at[:, self.here.c, pl.ds(2 * y, 2)],
                    self.buffers[k][0].at[:, y, :, :, cols],
                    self.local.at[source, y],
                )

    def to_core(self, k):
        for source, ref, cols in self.parts(k):
            for y in range(2):
                yield send(
                    ref.at[:, 1 - self.here.c, pl.ds(2 * y, 2)],
                    self.buffers[k][1].at[:, y, :, :, cols],
                    self.c_sems, (source, y), self.here.to_core,
                )

    def first_turn(self, k):
        mine, theirs, here = self.buffers[k][0], self.buffers[k][2], self.here
        left, right = self.halves(k)
        yield send(mine.at[:, :, 1 - here.x, :, left], theirs.at[0], self.x_sems, (k, 0), here.to_x)
        yield send(mine.at[:, 1 - here.y, :, :, right], theirs.at[1], self.x_sems, (k, 1), here.to_y)

    def second_turn(self, k):
        mine, theirs, here = self.buffers[k][0], self.buffers[k][3], self.here
        left, right = self.halves(k)
        yield send(mine.at[:, 1 - here.y, here.x, :, left], theirs.at[0], self.y_sems, (k, 0), here.to_y)
        yield send(mine.at[:, here.y, 1 - here.x, :, right], theirs.at[1], self.y_sems, (k, 1), here.to_x)

    def line(self, k):
        here, buffers = self.here, self.buffers[k]
        sems = [sem.at[k] for sem in self.z_sems]
        kind = DirectSum if k in self.direct else LineSum
        return kind(here, lambda z: buffers[0].at[z, here.y, here.x], buffers[4], sems)

    def finished(self, k):
        for i in range(3):
            mine = self.buffers[k][5].at[self.here.r]
            yield send(mine, mine, self.g_sems, (k, i), self.here.plane[i])

    def arriving(self, k):
        for i in range(3):
            theirs = self.buffers[k][5].at[self.here.quarters[i]]
            yield send(theirs, theirs, self.g_sems, (k, i), self.here.plane[i])


    def start(self, k):
        for copy in (*self.own(k), *self.to_core(k)):
            copy.start()

    def in_chip(self, k):
        for copy in self.own(k):
            copy.wait()
        for copy in self.to_core(k):
            copy.wait_recv()
        mine, theirs = self.buffers[k][:2]
        for z in range(4):
            for y in range(2):
                for x in range(2):
                    mine[z, y, x] = mine[z, y, x] + theirs[z, y, x]
        for copy in self.first_turn(k):
            copy.start()

    def in_pairs(self, k):
        for copy in self.first_turn(k):
            copy.wait()
        mine, theirs, here = self.buffers[k][0], self.buffers[k][2], self.here
        left, right = self.halves(k)
        for z in range(4):
            for i in range(2):
                mine[z, i, here.x, :, left] = mine[z, i, here.x, :, left] + theirs[0, z, i]
                mine[z, here.y, i, :, right] = mine[z, here.y, i, :, right] + theirs[1, z, i]
        for copy in self.second_turn(k):
            copy.start()

    def in_plane(self, k):
        for copy in self.second_turn(k):
            copy.wait()
        mine, theirs, here = self.buffers[k][0], self.buffers[k][3], self.here
        for z in range(4):
            for i, cols in enumerate(self.halves(k)):
                mine[z, here.y, here.x, :, cols] = mine[z, here.y, here.x, :, cols] + theirs[i, z]
        self.line(k).start()

    def turn0(self, k):
        self.line(k).turn(0)

    def turn1(self, k):
        self.line(k).turn(1)

    def turn2(self, k):
        self.line(k).turn(2)

    def in_line(self, k):
        self.line(k).turn(3)
        mine, done, here = self.buffers[k][0], self.buffers[k][5], self.here
        done[here.r] = mine[here.z, here.y, here.x]
        for copy in self.finished(k):
            copy.start()

    def end(self, k):
        for copy in self.arriving(k):
            copy.wait_recv()
        for copy in (*self.to_core(k), *self.finished(k)):
            copy.wait_send()
        self.line(k).finish()
        self.outs[k][...] = self.buffers[k][5][...]


    def gain_copy(self, stage, i):
        mine, core, plane, line = self.gain_buffers
        if stage == 0:
            return send(mine, core, self.gain_sems[0], 0, self.here.to_core)
        if stage == 1:
            return send(mine, plane.at[self.here.r], self.gain_sems[1], i, self.here.plane[i])
        return send(mine, line.at[i], self.gain_sems[2], i, self.here.line[i])

    def gain_plane_recv(self, i):
        mine, _, plane, _ = self.gain_buffers
        return send(mine, plane.at[self.here.quarters[i]], self.gain_sems[1], i, self.here.plane[i])

    def gain_step(self, stage):
        mine, core, plane, line = self.gain_buffers
        if stage == 0:
            self.gain_copy(0, 0).start()
        elif stage == 1:
            self.gain_copy(0, 0).wait()
            mine[...] += core[...]
            plane[self.here.r] = mine[...]
            for i in range(3):
                self.gain_copy(1, i).start()
        elif stage == 2:
            for i in range(3):
                self.gain_copy(1, i).wait_send()
                self.gain_plane_recv(i).wait_recv()
            mine[...] = (plane[0] + plane[1]) + (plane[2] + plane[3])
            for i in range(3):
                self.gain_copy(2, i).start()
        else:
            for i in range(3):
                self.gain_copy(2, i).wait()
            self.outs[len(self.chunks)][...] = (mine[...] + line[0]) + (line[1] + line[2])


    def token_core(self):
        mine = self.token_window.at[self.here.c]
        return send(mine, mine, self.token_sems, 0, self.here.to_core)

    def token_core_recv(self):
        theirs = self.token_window.at[1 - self.here.c]
        return send(theirs, theirs, self.token_sems, 0, self.here.to_core)

    def token_place(self, start):
        self.token_core().wait_send()
        self.token_core_recv().wait_recv()
        count, rows = 2 * self.token_window.shape[1], self.token_mine.shape[1]
        window = self.token_window[...].reshape(count, D)
        for z in range(4):
            slot = lax.broadcasted_iota(jnp.int32, (rows, count), 0) + (2 * z + self.here.c) * rows
            row = lax.broadcasted_iota(jnp.int32, (rows, count), 1) + start
            self.token_mine[z] = low(dot(low(jnp.where(slot == row, 1.0, 0.0)), window))
        self.token_line.start()

    def token_end(self):
        self.token_line.turn(3)
        self.outs[-1][...] = self.token_mine[self.here.z]
        self.token_line.finish()


def tail_kernel(
    comm, lat_ref, do_ref, p_ref, q_ref, kv_ref, gain_ref, wq_ref, wkv_ref, win_ref, start_ref,
    dm1_ref, ds_ref, dm2_ref, *refs,
):
    n_in, n_out = len(comm.inputs), len(comm.out_shapes)
    ins, lg_ref = refs[:n_in], refs[n_in]
    outs, scratch = refs[n_in + 1 : n_in + 1 + n_out], refs[n_in + 1 + n_out :]
    kv_sum, dkv_ref, more_ref, kv_sems = scratch[0], scratch[1], scratch[2], scratch[3:5]
    comm.bind(ins, outs, scratch[5:])
    here = comm.here
    mixed = len(comm.chunks) - 2
    early, last = range(mixed), mixed + 1
    rows, span = p_ref.shape
    gains = comm.gain_buffers[0]

    here.greet()
    for k in early:
        comm.start(k)
    block = rows // 2
    dwq = None
    gains[...] = jnp.zeros_like(gains)
    for i in range(2):
        at = slice(i * block, (i + 1) * block)
        p, do, q = p_ref[at], do_ref[at], q_ref[at]
        dp = dot_nt(do, kv_ref[:, D:])
        wide_p = p.astype(F32)
        ds = low(wide_p * (dp - jnp.sum(wide_p * dp, axis=1, keepdims=True)))
        dq = low(dot(ds, kv_ref[:, :D]) * CROSS_SCALE)
        dk, dv = dot_tn(ds, q), dot_tn(p, do)
        if i == 0:
            kv_sum[:, :D], kv_sum[:, D:] = dk, dv
        else:
            dkv_ref[:, :D] = low((kv_sum[:, :D] + dk) * CROSS_SCALE)
            dkv_ref[:, D:] = low(kv_sum[:, D:] + dv)
        unit, factor = normed(lat_ref[at].astype(F32))
        gain = gain_ref[0:1, :]
        term = dot_tn(low(unit * gain), dq)
        dwq = term if dwq is None else dwq + term
        back, dgain = norm_back(dot_nt(dq, wq_ref[...]), unit, factor, gain)
        lg_ref[at] = low(back)
        gains[0:1] += dgain
        if i < mixed:
            comm.in_chip(i)
    for k in range(2, mixed):
        comm.in_chip(k)
    half = span // 2
    to_core = send(
        dkv_ref.at[pl.ds(half * (1 - here.c), half)], more_ref, kv_sems, 0, here.to_core)
    to_core.start()
    comm.stages[0][...] = low(dwq).reshape(comm.stages[0].shape)
    comm.start(mixed)
    gains[2:3], gains[3:4], gains[4:5] = dm1_ref[0:1], ds_ref[0:1], dm2_ref[0:1]
    unit, factor = normed(win_ref[pl.ds(half * here.c, half)].astype(F32))
    gain = gain_ref[1:2, :]
    to_core.wait()
    dkv = low(dkv_ref[pl.ds(half * here.c, half)].astype(F32) + more_ref[...].astype(F32))
    back, dgain = norm_back(dot_nt(dkv, wkv_ref[...]), unit, factor, gain)
    comm.token_window[here.c] = low(back)
    comm.token_core().start()
    gains[1:2] = dgain
    comm.gain_step(0)
    comm.stages[1][...] = low(dot_tn(low(unit * gain), dkv)).reshape(comm.stages[1].shape)
    comm.start(last)
    comm.token_place(start_ref[0:1, 0:1])
    comm.in_chip(mixed)
    comm.in_pairs(0)
    comm.in_pairs(1)
    comm.gain_step(1)
    comm.in_chip(last)
    comm.token_line.turn(0)
    comm.in_pairs(2)
    comm.in_plane(0)
    comm.in_pairs(mixed)
    comm.in_plane(1)
    comm.token_line.turn(1)
    comm.in_pairs(last)
    for k in (0, 1):
        comm.turn0(k)
    comm.in_plane(2)
    comm.gain_step(2)
    for k in (0, 1):
        comm.turn1(k)
    comm.in_plane(mixed)
    comm.token_line.turn(2)
    comm.in_plane(last)
    for k in (0, 1):
        comm.turn2(k)
    for k in (2, mixed):
        comm.turn0(k)
    for k in (0, 1):
        comm.in_line(k)
    for k in (2, mixed):
        comm.turn1(k)
    comm.gain_step(3)
    for k in (2, mixed):
        comm.turn2(k)
    comm.in_line(last)
    comm.token_end()
    for k in (2, mixed):
        comm.in_line(k)
    for k in range(last + 1):
        comm.end(k)


def tail(comm, latents, do, p, q, kv, gains, mix, window, start, dgains):
    rows, span = p.shape
    r = (rows, D)
    return call(
        functools.partial(tail_kernel, comm),
        (1,),
        [
            (latents, r, flat),
            (do, r, flat),
            (p, p.shape, flat),
            (q, r, flat),
            (kv, kv.shape, flat),
            (gains, (8, D), flat),
            (mix, (D, D), column(2)),
            (mix, (D, 2 * D), column(0)),
            (window, (span, D), flat),
            (start, start.shape, flat),
        ]
        + [(g, (8, D), flat) for g in dgains],
        [(r, BF16, r, flat)],
        [
            pltpu.VMEM((span, 2 * D), F32),
            pltpu.VMEM((span, 2 * D), BF16),
            pltpu.VMEM((span // 2, 2 * D), BF16),
        ]
        + sem_pair(1),
        comm=comm,
        collective_id=2,
    )


def widen_kernel(cuts, base_ref, term_ref, *refs):
    sources, (sum_ref, *targets) = refs[: len(cuts)], refs[len(cuts) :]
    sum_ref[...] = base_ref[...] + term_ref[...].astype(F32)
    for source, widths in zip(sources, cuts):
        first = 0
        for width in widths:
            targets.pop(0)[...] = source[:, first : first + width].astype(F32)
            first += width


def widen(base, term, arrays, cuts):
    steps = 4
    rows = lambda array: array.shape[0] // steps
    return call(
        functools.partial(widen_kernel, cuts),
        (steps,),
        [(a, (rows(a), a.shape[1]), rows_of) for a in (base, term, *arrays)],
        [(base.shape, F32, (rows(base), base.shape[1]), rows_of)]
        + [
            ((a.shape[0], width), F32, (rows(a), width), rows_of)
            for a, widths in zip(arrays, cuts)
            for width in widths
        ],
    )


def from_partner(shard, bit):
    return lax.ppermute(shard, "lat", [(i, i ^ 1 << bit) for i in range(lax.axis_size("lat"))])


def gather_lat(shard):
    return lax.all_gather(shard, "lat", axis=0, tiled=True)


def halve(value, place, bits):
    kept, more = value, jnp.zeros_like(value)
    for bit in reversed(range(bits)):
        value = low(kept.astype(F32) + more.astype(F32))
        half = value.shape[0] // 2
        upper = place // 2**bit % 2
        kept = lax.dynamic_slice_in_dim(value, upper * half, half)
        more = from_partner(lax.dynamic_slice_in_dim(value, (1 - upper) * half, half), bit)
    return kept, more


def reduce_weights(grad):
    share = lax.psum_scatter(grad, "lat", scatter_dimension=0, tiled=True)
    return lax.psum(share, "row").astype(F32)


def local(
    tokens, latents, segment_ids, pad_mask, block_scene, out_grad,
    gain_cross_q, gain_cross_kv, w_cross_q, w_cross_kv, w_cross_out,
    gain_mlp1, w_up1, w_down1, gain_self, w_self_qkv, w_self_out, gain_mlp2, w_up2, w_down2,
):
    tokens, latents, og = tokens[0], latents[0], out_grad[0]
    rows, slots = latents.shape[0], tokens.shape[0] * lax.axis_size("lat")
    scenes = block_scene.shape[1]
    span = slots // scenes
    place = lax.axis_index("lat")
    group = LAT_SCENE // rows
    bits = group.bit_length() - 1

    gains = [gain_cross_q, gain_cross_kv, gain_mlp1, gain_self, gain_mlp2]
    first_weights = [[w_cross_kv, w_cross_q, w_cross_out], [w_up1], [w_down1], [w_self_qkv]]
    later_weights = [[w_up2], [w_down2], [w_self_out]]
    planes = lax.axis_size("row") == 4 and lax.axis_size("lat") == 8 and group == 2
    join = lambda gathered: [w.reshape(-1, w.shape[-1]) for w in gathered]
    if planes:
        notes = [segment_ids, pad_mask] + [g.reshape(1, -1) for g in gains]
        *weights, all_tokens, tags, gains = gather_now(Gather(first_weights, tokens, notes))
        mix, up1, down1, qkv, all_tokens = join([*weights, all_tokens])
    else:
        tag = jnp.where(pad_mask == 1, segment_ids, -1)
        tags = gather_lat(low(tag))
        all_tokens = gather_lat(tokens)
        gains = lax.all_gather(jnp.stack(gains), "lat", axis=1, tiled=True)
        gains = jnp.pad(gains.astype(F32), ((0, 3), (0, 0)))
        mix, up1, down1, qkv, up2, down2, so = (
            gather_lat(jnp.concatenate(shards, axis=1)) for shards in first_weights + later_weights
        )

    x1, x2, q, p, o, kv, q2, k2, v2, window, start = front(
        latents, all_tokens, tags, block_scene, span, gains, mix, up1, down1, qkv
    )
    if planes:
        o2, p2, scale2, k2_more, v2_more, *weights = self_forward(q2, (k2,), (v2,), Gather(later_weights))
        up2, down2, so = join(weights)
        keys, values = (k2, k2_more), (v2, v2_more)
    else:
        for bit in range(bits):
            upper = place // 2**bit % 2 == 1
            more = from_partner((k2, v2), bit)
            k2, v2 = (
                jnp.where(upper, jnp.concatenate([b, a]), jnp.concatenate([a, b]))
                for a, b in zip((k2, v2), more)
            )
        keys, values = (k2,), (v2,)
        o2, p2, scale2 = self_forward(q2, keys, values)
    out, g3, do2, dwup2, dwdown2, dwso, dgain_m2 = second(x2, o2, og, gains, so, up2, down2)
    comm = WeightSum([[dwup2], [dwdown2], [dwso]], direct=(0, 1, 2)) if planes else None
    dq2, dkv2, early = self_backward(q2, do2, o2, scale2, p2, keys, values, comm)
    if planes:
        dk, dv, dk_more, dv_more = dkv2
    else:
        dk, dk_more = halve(dkv2[0], place, bits)
        dv, dv_more = halve(dkv2[1], place, bits)
    g2, dwqkv, dgain_s = qkv_back(x2, g3, dq2, dk, dk_more, dv, dv_more, gains, qkv)
    g1, do, dwup1, dwdown1, dwout, dgain_m1 = first_back(x1, g2, o, gains, mix, up1, down1)
    if planes:
        comm = WeightSum(
            [[dwqkv], [dwup1], [dwdown1], [Staged(D, D), dwout], [Staged(D, 2 * D)]], gains=(8, D), tokens=slots,
            direct=(4,),
        )
        term, *late, dgains, token_grad = tail(
            comm, latents, do, p, q, kv, gains, mix, window, start, (dgain_m1, dgain_s, dgain_m2)
        )
        dgains = lax.dynamic_slice_in_dim(dgains, place * (D // 8), D // 8, axis=1)
        up2, down2, so, qkv, up1, down1, mixed, dwkv = join([*early, *late])
        latent_grad, token_grad, dwq, dwout, dwkv, *others = widen(
            g1, term, [token_grad, mixed, dwkv, up1, down1, qkv, so, up2, down2],
            ((D,), (D, D), (2 * D,), (FF,), (D,), (3 * D,), (D,), (FF,), (D,)),
        )
        sums = dwq, dwkv, dwout, *others
    else:
        latent_grad, dwq, dkv, dgain_q = cross_back(latents, g1, do, p, q, kv, gains, mix)
        mine, more = halve(dkv, place, bits)
        first = place % group * (span // group)
        token_rows = lax.dynamic_slice_in_dim(window, first, span // group)
        token_part, dwkv, dgain_kv = token_back(token_rows, mine, more, gains, mix)
        token_part = lax.dynamic_update_slice_in_dim(
            jnp.zeros((slots, D), BF16), token_part, start[0, 0] + first, 0
        )
        token_grad = lax.psum_scatter(token_part, "lat", scatter_dimension=0, tiled=True).astype(F32)
        dgains = jnp.stack([g[0] for g in (dgain_q, dgain_kv, dgain_m1, dgain_s, dgain_m2)])
        dgains = lax.psum_scatter(low(dgains), "lat", scatter_dimension=1, tiled=True)
        dgains = lax.psum(dgains, "row").astype(F32)
        sums = [
            reduce_weights(g) for g in (dwq, dwkv, dwout, dwup1, dwdown1, dwqkv, dwso, dwup2, dwdown2)
        ]
    dwq, dwkv, dwout, dwup1, dwdown1, dwqkv, dwso, dwup2, dwdown2 = sums
    return (
        out[None],
        latent_grad[None],
        token_grad[None],
        dgains[0],
        dgains[1],
        dwq,
        dwkv,
        dwout,
        dgains[2],
        dwup1,
        dwdown1,
        dgains[3],
        dwqkv,
        dwso,
        dgains[4],
        dwup2,
        dwdown2,
    )


def solution(mesh):
    by_row = P("row", "lat", None)
    weight = P("lat", None)
    gain = P("lat")
    parameters = (
        gain, gain, weight, weight, weight, gain, weight, weight, gain, weight, weight, gain,
        weight, weight,
    )
    return jax.shard_map(
        local,
        mesh=mesh,
        in_specs=(by_row, by_row, P("row", "lat"), P("row", "lat"), P("row", None), by_row)
        + parameters,
        out_specs=(by_row, by_row, by_row) + parameters,
        check_vma=False,
    )
```

```python
import functools

import jax
import jax.numpy as jnp
from jax import lax
from jax.experimental import pallas as pl
from jax.experimental.pallas import tpu as pltpu
from jax.sharding import PartitionSpec as P

D = 512
FF = 2048
HEADS = 8
LAT_SCENE = 2048
HEAD = D // HEADS
PAIRS = HEADS // 2
LANES = 128
FF_STEP = 512
EPS = 1e-05
NEG = -1e30
CROSS_SCALE = D ** (-0.5)
SELF_SCALE = HEAD ** (-0.5)
GELU_C = 0.7978845608028654
GELU_K = 0.044715
VMEM_LIMIT = 60 * 1024 * 1024
F32 = jnp.float32
BF16 = jnp.bfloat16


def low(value):
    return value.astype(BF16)


def dot(left, right):
    return jnp.dot(left, right, preferred_element_type=F32)


def dot_nt(left, right):
    return lax.dot_general(left, right, (((1,), (1,)), ((), ())), preferred_element_type=F32)


def dot_tn(left, right):
    return lax.dot_general(left, right, (((0,), (0,)), ((), ())), preferred_element_type=F32)


def normed(value):
    centered = value - jnp.mean(value, axis=-1, keepdims=True)
    factor = lax.rsqrt(jnp.mean(centered * centered, axis=-1, keepdims=True) + EPS)
    return centered * factor, factor


def norm_back(grad, unit, factor, gain):
    scaled = grad * gain
    inner = (
        scaled
        - jnp.mean(scaled, axis=-1, keepdims=True)
        - unit * jnp.mean(scaled * unit, axis=-1, keepdims=True)
    )
    return factor * inner, jnp.sum(grad * unit, axis=0, keepdims=True)


def gelu(u):
    return 0.5 * u * (1.0 + jnp.tanh(GELU_C * (u + GELU_K * u * u * u)))


def gelu_both(u):
    square = u * u
    t = jnp.tanh(GELU_C * u * (1.0 + GELU_K * square))
    half = 0.5 * (1.0 + t)
    slope = half + 0.5 * u * (1.0 - t * t) * (GELU_C * (1.0 + 3.0 * GELU_K * square))
    return u * half, slope


def call(kernel, grid, ins, outs, scratch=(), comm=None, collective_id=None):
    in_specs = [ANYWHERE if block is None else pl.BlockSpec(block, index) for _, block, index in ins]
    out_specs = [ANYWHERE if block is None else pl.BlockSpec(block, index) for _, _, block, index in outs]
    out_shape = [jax.ShapeDtypeStruct(shape, kind) for shape, kind, _, _ in outs]
    arrays, scratch = [array for array, _, _ in ins], list(scratch)
    if comm is not None:
        arrays += comm.inputs
        in_specs += comm.in_specs
        out_shape += comm.out_shapes
        out_specs += comm.out_specs
        scratch += comm.scratch
    return pl.pallas_call(
        kernel,
        grid=grid,
        in_specs=in_specs,
        out_specs=out_specs,
        out_shape=out_shape,
        scratch_shapes=scratch,
        compiler_params=pltpu.CompilerParams(
            vmem_limit_bytes=VMEM_LIMIT,
            collective_id=None if comm is None else collective_id,
            has_side_effects=comm is not None,
        ),
    )(*arrays)


def inside(shape):
    return pl.BlockSpec(shape, lambda *_: (0,) * len(shape))


ANYWHERE = pl.BlockSpec(memory_space=pl.ANY)


def flat(*_):
    return (0, 0)


def column(c):
    return lambda *_: (0, c)


def rows_of(i, *_):
    return (i, 0)


def front_kernel(
    lat_rows, lat_ref, tok_ref, tags_ref, scene_ref, gain_ref, wq_ref, wkv_ref, wout_ref, wup_ref, wdown_ref, wqkv_ref,
    x1_ref, x2_ref, q_ref, p_ref, o_ref, kv_ref, q2_ref, k2_ref, v2_ref, win_ref, start_ref,
    bias_ref, sem,
):
    @pl.when(pl.program_id(0) == 0)
    def _():
        span, slots = win_ref.shape[0], tok_ref.shape[0]
        tags, scenes = tags_ref[...].astype(F32), scene_ref[...]
        own = lax.axis_index("lat") * lat_rows // LAT_SCENE
        own = lax.broadcasted_iota(jnp.int32, scenes.shape, 1) == own
        scene = jnp.sum(jnp.where(own, scenes, 0).astype(F32))
        count = lambda chosen: jnp.sum(jnp.where(chosen, 1.0, 0.0)).astype(jnp.int32)
        before = count((tags >= 0.0) & (tags < scene))
        length = count(tags == scene)
        start = pl.multiple_of(jnp.minimum(before // 16 * 16, slots - span), 16)
        copy = pltpu.make_async_copy(tok_ref.at[pl.ds(start, span)], win_ref, sem)
        copy.start()
        start_ref[...] = jnp.full(start_ref.shape, start, jnp.int32)
        slot = lax.broadcasted_iota(jnp.int32, bias_ref.shape, 1) + start
        bias_ref[...] = jnp.where((slot >= before) & (slot < before + length), 0.0, NEG)
        copy.wait()
        unit, _ = normed(win_ref[...].astype(F32))
        kv_ref[...] = low(dot(low(unit * gain_ref[1:2, :]), wkv_ref[...]))

    x = lat_ref[...].astype(F32)
    unit, _ = normed(x)
    q = low(dot(low(unit * gain_ref[0:1, :]), wq_ref[...]))
    q_ref[...] = q
    s = dot_nt(q, kv_ref[:, :D]) * CROSS_SCALE + bias_ref[0:1, :]
    e = jnp.exp(s - jnp.max(s, axis=1, keepdims=True))
    p = low(e / jnp.sum(e, axis=1, keepdims=True))
    p_ref[...] = p
    o = low(dot(p, kv_ref[:, D:]))
    o_ref[...] = o
    x1 = x + dot(o, wout_ref[...])
    x1_ref[...] = x1
    unit, _ = normed(x1)
    m1 = low(unit * gain_ref[2:3, :])
    total = x1
    for c in range(FF // FF_STEP):
        cols = slice(c * FF_STEP, (c + 1) * FF_STEP)
        h = low(gelu(dot(m1, wup_ref[:, cols])))
        total = total + dot(h, wdown_ref[cols, :])
    x2_ref[...] = total
    unit, _ = normed(total)
    bn = low(unit * gain_ref[3:4, :])
    q2_ref[...] = low(dot(bn, wqkv_ref[:, :D])) * SELF_SCALE
    k2_ref[...] = low(dot(bn, wqkv_ref[:, D : 2 * D]))
    v2_ref[...] = low(dot(bn, wqkv_ref[:, 2 * D :]))


def front(latents, tokens, tags, scene, span, gains, mix, up1, down1, qkv):
    rows = latents.shape[0]
    block = min(rows, 512)
    r = (block, D)
    return call(
        functools.partial(front_kernel, rows),
        (rows // block,),
        [
            (latents, r, rows_of),
            (tokens, None, None),
            (tags, tags.shape, flat),
            (scene, scene.shape, flat),
            (gains, (8, D), flat),
            (mix, (D, D), column(2)),
            (mix, (D, 2 * D), column(0)),
            (mix, (D, D), column(3)),
            (up1, (D, FF), flat),
            (down1, (FF, D), flat),
            (qkv, (D, 3 * D), flat),
        ],
        [
            ((rows, D), F32, r, rows_of),
            ((rows, D), F32, r, rows_of),
            ((rows, D), BF16, r, rows_of),
            ((rows, span), BF16, (block, span), rows_of),
            ((rows, D), BF16, r, rows_of),
            ((span, 2 * D), BF16, (span, 2 * D), flat),
            ((rows, D), BF16, r, rows_of),
            ((rows, D), BF16, r, rows_of),
            ((rows, D), BF16, r, rows_of),
            ((span, D), BF16, (span, D), flat),
            ((8, LANES), jnp.int32, (8, LANES), flat),
        ],
        [pltpu.VMEM((8, span), F32), pltpu.SemaphoreType.DMA],
    )


def lane_is(shape, head):
    lane = lax.broadcasted_iota(jnp.int32, shape, 1)
    return (lane < HEAD) if head == 0 else (lane >= HEAD)


def only(value, head):
    return jnp.where(lane_is(value.shape, head), value, jnp.zeros_like(value))


def self_forward_kernel(parts, steps, comm, q_ref, *refs):
    refs = list(refs)
    take = lambda n: [refs.pop(0) for _ in range(n)]
    pair, step = pl.program_id(0), pl.program_id(1)
    point = pair * steps + step
    if comm is None:
        k_refs, v_refs = take(parts), take(parts)
        o_ref, p_ref, scale_ref = take(3)
        ones_refs = refs
    else:
        (k_ref,), (v_ref,) = take(1), take(1)
        both = take(2)
        ins = take(len(comm.inputs))
        o_ref, p_ref, scale_ref, k_more, v_more = take(5)
        outs = take(len(comm.out_shapes))
        ones_refs, (landed,), sems = take(2), take(1), take(2)
        comm.bind(ins, outs, refs)
        k_refs, v_refs = (k_ref, k_more), (v_ref, v_more)

        def to_core(i, p):
            cols = pl.ds(p * LANES, LANES)
            return send(both[i].at[:, cols], landed.at[i, p], sems, (i, p), comm.here.to_core)

        @pl.when(point == 0)
        def _():
            comm.here.greet()
            for p in range(PAIRS):
                for i in range(2):
                    to_core(i, p).start()
            comm.begin()

        pl.when(point == 1)(comm.begin_sends)
        for i in range(comm.steps):
            pl.when(point == SHIFT + i)(functools.partial(comm.step, i))

        @pl.when(step == 0)
        def _():
            for i, ref in enumerate((k_more, v_more)):
                arrived = landed.at[i, pair]
                send(arrived, arrived, sems, (i, pair), comm.here.to_core).wait_recv()
                ref[...] = arrived[...]

    @pl.when(step == 0)
    def _():
        for v_ref, ones_ref in zip(v_refs, ones_refs):
            v = v_ref[...]
            for head in range(2):
                ones_ref[head] = jnp.where(lane_is(v.shape, head), v, jnp.ones_like(v))

    q = q_ref[...]
    outs, scales = [], []
    for head in range(2):
        scores = [dot_nt(only(q, head), k_ref[...]) for k_ref in k_refs]
        top = functools.reduce(jnp.maximum, [jnp.max(s, axis=1, keepdims=True) for s in scores])
        mixed, first = None, 0
        for s, ones_ref in zip(scores, ones_refs):
            p = low(jnp.exp(s - top))
            p_ref[head, :, first : first + p.shape[1]] = p
            first += p.shape[1]
            term = dot(p, ones_ref[head])
            mixed = term if mixed is None else mixed + term
        scales.append(1.0 / pltpu.roll(mixed, HEAD, 1))
        outs.append(mixed * scales[-1])
    left = lane_is(outs[0].shape, 0)
    o_ref[...] = low(jnp.where(left, outs[0], outs[1]))
    scale_ref[...] = jnp.where(left, scales[0], scales[1])

    if comm is not None:
        @pl.when(point == PAIRS * steps - 1)
        def _():
            for p in range(PAIRS):
                for i in range(2):
                    to_core(i, p).wait_send()
            comm.finish()


def self_forward(q2, keys, values, comm=None):
    rows = q2.shape[0]
    block = min(rows, 256)
    parts = len(keys)
    total = sum(k.shape[0] for k in keys) * (1 if comm is None else 2)
    whole = lambda array: (array, (array.shape[0], LANES), lambda p, i: (0, p))
    more = ((rows, D), BF16, (rows, LANES), lambda p, i: (0, p))
    beside = comm is not None
    return call(
        functools.partial(self_forward_kernel, parts, rows // block, comm),
        (PAIRS, rows // block),
        [(q2, (block, LANES), lambda p, i: (i, p))]
        + [whole(k) for k in keys]
        + [whole(v) for v in values]
        + ([(keys[0], None, None), (values[0], None, None)] if beside else []),
        [
            ((rows, D), BF16, (block, LANES), lambda p, i: (i, p)),
            ((HEADS, rows, total), BF16, (2, block, total), lambda p, i: (p, i, 0)),
            ((rows, D), F32, (block, LANES), lambda p, i: (i, p)),
        ]
        + ([more, more] if beside else []),
        [pltpu.VMEM((2, k.shape[0], LANES), BF16) for k in keys * (2 if beside else 1)]
        + ([pltpu.VMEM((2, PAIRS, rows, LANES), BF16)] + sem_pair(2, PAIRS) if beside else []),
        comm=comm,
        collective_id=3,
    )


def run_beside(comm, point, plan, odd):
    for when, work in plan.items():
        if when % 2 != odd:
            continue
        def run(when=when, work=work):
            if when == 0:
                comm.here.greet()
            for name, k in work:
                getattr(comm, name)(k)
        pl.when(point == when)(run)


SELF_PLAN = {
    0: (("start", 0), ("start", 1), ("start", 2)),
    4: (("in_chip", 0),),
    6: (("in_chip", 1),),
    7: (("in_chip", 2),),
    10: (("in_pairs", 0),),
    14: (("in_pairs", 1),),
    16: (("in_pairs", 2),),
    17: (("in_plane", 0),),
    20: (("in_plane", 1),),
    21: (("in_plane", 2),),
    23: (("in_line", 0),),
    27: (("in_line", 1),),
    29: (("in_line", 2),),
    31: (("end", 0), ("end", 1), ("end", 2)),
}


def self_backward_kernel(parts, steps, comm, q_ref, do_ref, o_ref, scale_ref, p_ref, *refs):
    refs = list(refs)
    take = lambda n: [refs.pop(0) for _ in range(n)]
    pair, step = pl.program_id(0), pl.program_id(1)
    point = 2 * (pair * steps + step)
    k_refs, v_refs = take(parts), take(parts)
    if comm is None:
        (dq_ref,), dk_refs, dv_refs = take(1), take(parts), take(parts)
        dk_sums, dv_sums = take(parts), take(parts)
    else:
        ins = take(len(comm.inputs))
        dq_ref, dk_ref, dv_ref, *landed = take(5)
        outs = take(len(comm.out_shapes))
        dk_sums, dv_sums, (stage,), sems = take(parts), take(parts), take(1), take(2)
        comm.bind(ins, outs, refs)
        dk_refs, dv_refs = (dk_ref, stage.at[0, pair]), (dv_ref, stage.at[1, pair])

        def to_core(i, p):
            cols = pl.ds(pl.multiple_of(p * LANES, LANES), LANES)
            return send(stage.at[i, p], landed[i].at[:, cols], sems, (i, p), comm.here.to_core)

        run_beside(comm, point, SELF_PLAN, 0)

    @pl.when(step == 0)
    def _():
        for ref in (*dk_sums, *dv_sums):
            ref[...] = jnp.zeros_like(ref)

    q = q_ref[...]
    do = low(do_ref[...].astype(F32) * scale_ref[...])
    product = do.astype(F32) * o_ref[...].astype(F32)
    q_turned, do_turned = jnp.transpose(q), jnp.transpose(do)
    dqs = []
    for head in range(2):
        rows = slice(head * HEAD, (head + 1) * HEAD)
        doz = only(do, head)
        delta = jnp.sum(only(product, head), axis=1, keepdims=True)
        dq, first = None, 0
        for k_ref, v_ref, dk_sum, dv_sum in zip(k_refs, v_refs, dk_sums, dv_sums):
            count = k_ref.shape[0]
            p = p_ref[head, :, first : first + count]
            first += count
            ds = low(p.astype(F32) * (dot_nt(doz, v_ref[...]) - delta))
            dv_sum[rows, :] += dot(do_turned[rows], p)
            dk_sum[rows, :] += dot(q_turned[rows], ds)
            term = dot(ds, k_ref[...])
            dq = term if dq is None else dq + term
        dqs.append(dq)
    dq_ref[...] = low(jnp.where(lane_is(dqs[0].shape, 0), dqs[0], dqs[1]) * SELF_SCALE)

    @pl.when(step == steps - 1)
    def _():
        for ref, total in zip((*dk_refs, *dv_refs), (*dk_sums, *dv_sums)):
            ref[...] = jnp.transpose(low(total[...]))
        if comm is not None:
            for i in range(2):
                to_core(i, pair).start()

    if comm is not None:
        run_beside(comm, point + 1, SELF_PLAN, 1)

        @pl.when(point == 2 * (PAIRS * steps - 1))
        def _():
            for p in range(PAIRS):
                for i in range(2):
                    to_core(i, p).wait()


def self_backward(q2, do2, o2, scale2, p2, keys, values, comm=None):
    rows = q2.shape[0]
    block = min(rows, 256)
    parts = len(keys)
    whole = lambda array: (array, (array.shape[0], LANES), lambda p, i: (0, p))
    made = lambda array: (array.shape, BF16, (array.shape[0], LANES), lambda p, i: (0, p))
    if comm is None:
        outs, extra = [made(k) for k in keys] + [made(v) for v in values], []
    else:
        outs = [made(keys[0]), made(values[0])] + [((rows, D), BF16, None, None)] * 2
        extra = [pltpu.VMEM((2, PAIRS, rows, LANES), BF16)] + sem_pair(2, PAIRS)
    out = call(
        functools.partial(self_backward_kernel, parts, rows // block, comm),
        (PAIRS, rows // block),
        [
            (q2, (block, LANES), lambda p, i: (i, p)),
            (do2, (block, LANES), lambda p, i: (i, p)),
            (o2, (block, LANES), lambda p, i: (i, p)),
            (scale2, (block, LANES), lambda p, i: (i, p)),
            (p2, (2, block, p2.shape[2]), lambda p, i: (p, i, 0)),
        ]
        + [whole(k) for k in keys]
        + [whole(v) for v in values],
        [((rows, D), BF16, (block, LANES), lambda p, i: (i, p))] + outs,
        [pltpu.VMEM((LANES, k.shape[0]), F32) for k in (*keys, *values)] + extra,
        comm=comm,
        collective_id=1,
    )
    return out[0], out[1 : 1 + len(outs)], out[1 + len(outs) :]


def second_kernel(
    steps, x2_ref, o2_ref, og_ref, gain_ref, wso_ref, wup_ref, wdown_ref,
    out_ref, g3_ref, do_ref, dwup_ref, dwdown_ref, dwso_ref, dgain_ref,
    m_ref, f_ref, dm_ref,
):
    c = pl.program_id(0)

    @pl.when(c == 0)
    def _():
        x3 = x2_ref[...] + dot(o2_ref[...], wso_ref[...])
        unit, _ = normed(x3)
        m_ref[...] = low(unit * gain_ref[4:5, :])
        out_ref[...] = x3
        f_ref[...] = jnp.zeros_like(f_ref)
        dm_ref[...] = jnp.zeros_like(dm_ref)

    m, og = m_ref[...], og_ref[...]
    h, slope = gelu_both(dot(m, wup_ref[...]))
    h = low(h)
    f_ref[...] += dot(h, wdown_ref[...])
    dwdown_ref[...] = low(dot_tn(h, og))
    du = low(slope * dot_nt(og, wdown_ref[...]))
    dwup_ref[...] = low(dot_tn(m, du))
    dm_ref[...] += dot_nt(du, wup_ref[...])

    @pl.when(c == steps - 1)
    def _():
        x3 = out_ref[...]
        unit, factor = normed(x3)
        out_ref[...] = x3 + f_ref[...]
        back, dgain = norm_back(dm_ref[...], unit, factor, gain_ref[4:5, :])
        g3 = og_ref[...].astype(F32) + back
        g3_ref[...] = g3
        dgain_ref[...] = jnp.broadcast_to(dgain, dgain_ref.shape)
        b3 = low(g3)
        o2 = o2_ref[...]
        dwso_ref[...] = low(dot_tn(o2, b3))
        do_ref[...] = low(dot_nt(b3, wso_ref[...]))


def second(x2, o2, og, gains, so, up2, down2):
    rows = x2.shape[0]
    steps = FF // FF_STEP
    r = (rows, D)
    return call(
        functools.partial(second_kernel, steps),
        (steps,),
        [
            (x2, r, flat),
            (o2, r, flat),
            (og, r, flat),
            (gains, (8, D), flat),
            (so, (D, D), flat),
            (up2, (D, FF_STEP), lambda c: (0, c)),
            (down2, (FF_STEP, D), lambda c: (c, 0)),
        ],
        [
            (r, F32, r, flat),
            (r, F32, r, flat),
            (r, BF16, r, flat),
            ((D, FF), BF16, (D, FF_STEP), lambda c: (0, c)),
            ((FF, D), BF16, (FF_STEP, D), lambda c: (c, 0)),
            ((D, D), BF16, (D, D), flat),
            ((8, D), F32, (8, D), flat),
        ],
        [pltpu.VMEM(r, BF16), pltpu.VMEM(r, F32), pltpu.VMEM(r, F32)],
    )


def middle_back_kernel(
    blocks, steps,
    x2_ref, g3_ref, dq_ref, dk_ref, dk_more_ref, dv_ref, dv_more_ref, x1_ref,
    o_ref, gain_ref, wqkv_ref, wout_ref, wup_ref, wdown_ref,
    g1_ref, do_ref, dwqkv_ref, dwup_ref, dwdown_ref, dwout_ref, dgain_s_ref, dgain_m_ref,
    dw_sum, g2_ref, unit_ref, factor_ref, m_ref, b_ref, dm_ref,
):
    step = pl.program_id(0)

    @pl.when(step == 0)
    def _():
        dw_sum[...] = jnp.zeros_like(dw_sum)
        dm_ref[...] = jnp.zeros_like(dm_ref)
        dgain_s_ref[...] = jnp.zeros_like(dgain_s_ref)

    @pl.when(step < blocks)
    def _():
        count = x2_ref.shape[0]
        at = pl.ds(pl.multiple_of(step * count, count), count)
        unit, factor = normed(x2_ref[...])
        gain = gain_ref[3:4, :]
        bn = low(unit * gain)
        dk = low(dk_ref[...].astype(F32) + dk_more_ref[...].astype(F32))
        dv = low(dv_ref[...].astype(F32) + dv_more_ref[...].astype(F32))
        dbn = None
        for i, part in enumerate((dq_ref[...], dk, dv)):
            cols = slice(i * D, (i + 1) * D)
            dw_sum[:, cols] += dot_tn(bn, part)
            term = dot_nt(part, wqkv_ref[:, cols])
            dbn = term if dbn is None else dbn + term
        back, dgain = norm_back(dbn, unit, factor, gain)
        g2 = g3_ref[...] + back
        g2_ref[at] = g2
        b_ref[at] = low(g2)
        dgain_s_ref[...] += jnp.broadcast_to(dgain, dgain_s_ref.shape)
        unit, factor = normed(x1_ref[...])
        unit_ref[at] = unit
        factor_ref[at] = jnp.broadcast_to(factor, (count, LANES))
        m_ref[at] = low(unit * gain_ref[2:3, :])

    @pl.when(step >= blocks)
    def _():
        m, b = m_ref[...], b_ref[...]
        h, slope = gelu_both(dot(m, wup_ref[...]))
        dwdown_ref[...] = low(dot_tn(low(h), b))
        du = low(slope * dot_nt(b, wdown_ref[...]))
        dwup_ref[...] = low(dot_tn(m, du))
        dm_ref[...] += dot_nt(du, wup_ref[...])

    @pl.when(step == blocks + steps - 1)
    def _():
        dwqkv_ref[...] = low(dw_sum[...])
        back, dgain = norm_back(dm_ref[...], unit_ref[...], factor_ref[:, 0:1], gain_ref[2:3, :])
        g1 = g2_ref[...] + back
        g1_ref[...] = g1
        dgain_m_ref[...] = jnp.broadcast_to(dgain, dgain_m_ref.shape)
        b1 = low(g1)
        dwout_ref[...] = low(dot_tn(o_ref[...], b1))
        do_ref[...] = low(dot_nt(b1, wout_ref[...]))


def middle_back(x2, g3, dq, dk, dk_more, dv, dv_more, x1, o, gains, qkv, mix, up1, down1):
    rows = x1.shape[0]
    block = min(rows, 512)
    blocks, steps = rows // block, FF // FF_STEP
    r = (rows, D)
    row_block = lambda s: (jnp.minimum(s, blocks - 1), 0)
    part = lambda s: jnp.maximum(s - blocks, 0)
    return call(
        functools.partial(middle_back_kernel, blocks, steps),
        (blocks + steps,),
        [(a, (block, D), row_block) for a in (x2, g3, dq, dk, dk_more, dv, dv_more, x1)]
        + [
            (o, r, flat),
            (gains, (8, D), flat),
            (qkv, (D, 3 * D), flat),
            (mix, (D, D), column(3)),
            (up1, (D, FF_STEP), lambda s: (0, part(s))),
            (down1, (FF_STEP, D), lambda s: (part(s), 0)),
        ],
        [
            (r, F32, r, flat),
            (r, BF16, r, flat),
            ((D, 3 * D), BF16, (D, 3 * D), flat),
            ((D, FF), BF16, (D, FF_STEP), lambda s: (0, part(s))),
            ((FF, D), BF16, (FF_STEP, D), lambda s: (part(s), 0)),
            ((D, D), BF16, (D, D), flat),
            ((8, D), F32, (8, D), flat),
            ((8, D), F32, (8, D), flat),
        ],
        [
            pltpu.VMEM((D, 3 * D), F32),
            pltpu.VMEM(r, F32),
            pltpu.VMEM(r, F32),
            pltpu.VMEM((rows, LANES), F32),
            pltpu.VMEM(r, BF16),
            pltpu.VMEM(r, BF16),
            pltpu.VMEM(r, F32),
        ],
    )


def cross_back_kernel(
    steps, lat_ref, g1_ref, do_ref, p_ref, q_ref, kv_ref, gain_ref, wq_ref,
    lg_ref, dwq_ref, dkv_ref, dgain_ref, dk_sum, dv_sum, dwq_sum,
):
    i = pl.program_id(0)

    @pl.when(i == 0)
    def _():
        for ref in (dk_sum, dv_sum, dwq_sum, dgain_ref):
            ref[...] = jnp.zeros_like(ref)

    p, do, q = p_ref[...], do_ref[...], q_ref[...]
    dp = dot_nt(do, kv_ref[:, D:])
    wide_p = p.astype(F32)
    ds = low(wide_p * (dp - jnp.sum(wide_p * dp, axis=1, keepdims=True)))
    dq = low(dot(ds, kv_ref[:, :D]) * CROSS_SCALE)
    dk_sum[...] += dot_tn(ds, q)
    dv_sum[...] += dot_tn(p, do)
    unit, factor = normed(lat_ref[...].astype(F32))
    gain = gain_ref[0:1, :]
    dwq_sum[...] += dot_tn(low(unit * gain), dq)
    back, dgain = norm_back(dot_nt(dq, wq_ref[...]), unit, factor, gain)
    lg_ref[...] = g1_ref[...] + back
    dgain_ref[...] += jnp.broadcast_to(dgain, dgain_ref.shape)

    @pl.when(i == steps - 1)
    def _():
        dwq_ref[...] = low(dwq_sum[...])
        dkv_ref[:, :D] = low(dk_sum[...] * CROSS_SCALE)
        dkv_ref[:, D:] = low(dv_sum[...])


def cross_back(latents, g1, do, p, q, kv, gains, mix):
    rows, span = p.shape
    block = min(rows, 512)
    r = (block, D)
    return call(
        functools.partial(cross_back_kernel, rows // block),
        (rows // block,),
        [
            (latents, r, rows_of),
            (g1, r, rows_of),
            (do, r, rows_of),
            (p, (block, span), rows_of),
            (q, r, rows_of),
            (kv, (span, 2 * D), flat),
            (gains, (8, D), flat),
            (mix, (D, D), column(2)),
        ],
        [
            ((rows, D), F32, r, rows_of),
            ((D, D), BF16, (D, D), flat),
            ((span, 2 * D), BF16, (span, 2 * D), flat),
            ((8, D), F32, (8, D), flat),
        ],
        [pltpu.VMEM((span, D), F32), pltpu.VMEM((span, D), F32), pltpu.VMEM((D, D), F32)],
    )


def token_back_kernel(tok_ref, dkv_ref, more_ref, gain_ref, w_ref, tg_ref, dw_ref, dgain_ref):
    unit, factor = normed(tok_ref[...].astype(F32))
    gain = gain_ref[1:2, :]
    dkv = low(dkv_ref[...].astype(F32) + more_ref[...].astype(F32))
    dw_ref[...] = low(dot_tn(low(unit * gain), dkv))
    back, dgain = norm_back(dot_nt(dkv, w_ref[...]), unit, factor, gain)
    tg_ref[...] = low(back)
    dgain_ref[...] = jnp.broadcast_to(dgain, dgain_ref.shape)


def token_back(tokens, dkv, more, gains, mix):
    rows = tokens.shape[0]
    return call(
        token_back_kernel,
        (1,),
        [
            (tokens, (rows, D), flat),
            (dkv, (rows, 2 * D), flat),
            (more, (rows, 2 * D), flat),
            (gains, (8, D), flat),
            (mix, (D, 2 * D), column(0)),
        ],
        [
            ((rows, D), BF16, (rows, D), flat),
            ((D, 2 * D), BF16, (D, 2 * D), flat),
            ((8, D), F32, (8, D), flat),
        ],
    )


MESH = pl.DeviceIdType.MESH
UP, DOWN = 0, 1


class Place:
    def __init__(self):
        row, lat = lax.axis_index("row"), lax.axis_index("lat")
        self.x, self.y, self.z, self.c = row % 2, row // 2, lat // 2, lat % 2
        self.r = row
        self.rx = self.y * 2 + 1 - self.x
        self.ry = (1 - self.y) * 2 + self.x
        self.rd = (1 - self.y) * 2 + 1 - self.x
        self.to_x, self.to_y = (self.rx, lat), (self.ry, lat)
        self.to_core = (row, self.z * 2 + 1 - self.c)
        self.to_z = ((row, lat + 2), (row, lat - 2))
        self.more = (self.z < 3, self.z > 0)

    def greet(self):
        barrier = pltpu.get_barrier_semaphore()
        for device in (self.to_x, self.to_y, self.to_core):
            pl.semaphore_signal(barrier, inc=1, device_id=device, device_id_type=MESH)
        for way in (UP, DOWN):
            @pl.when(self.more[way])
            def _():
                pl.semaphore_signal(barrier, inc=1, device_id=self.to_z[way], device_id_type=MESH)
        pl.semaphore_wait(barrier, 3 + jnp.minimum(self.z, 1) + jnp.minimum(3 - self.z, 1))

    def source(self, way, hop):
        return (self.z - hop, self.z >= hop) if way == UP else (self.z + hop, self.z + hop <= 3)


def send(src, dst, sems, index, device):
    return pltpu.make_async_remote_copy(
        src_ref=src, dst_ref=dst, send_sem=sems[0].at[index], recv_sem=sems[1].at[index],
        device_id=device, device_id_type=MESH,
    )


def sem_pair(*shape):
    return [pltpu.SemaphoreType.DMA(shape), pltpu.SemaphoreType.DMA(shape)]


TOKEN_PARTS = 4
AHEAD = 2
GAP = 2
SHIFT = 3
WEIGHT, TOKENS, NOTES = range(3)


class Gather:
    def __init__(self, weights, tokens=None, notes=()):
        self.inputs, self.out_shapes, self.chunks = [], [], []
        self.shards = []
        for shards in weights:
            shape = (4, shards[0].shape[0] // 4)
            self.shards.append([])
            for shard in shards:
                self.shards[-1].append((len(self.inputs), shard.shape[1]))
                self.inputs.append(shard.reshape(shape + shard.shape[1:]))
            cols = sum(shard.shape[1] for shard in shards)
            self.out_shapes.append(jax.ShapeDtypeStruct((4, 2) + shape + (cols,), BF16))
        self.chunks = [(WEIGHT, k) for k in range(len(weights))]
        self.out_specs = [ANYWHERE] * len(weights)
        self.copies = len(self.inputs)
        self.scratch = []
        self.noted = len(notes)
        if tokens is not None:
            self.inputs += [tokens, *notes]
            self.out_shapes += [
                jax.ShapeDtypeStruct((4, 2) + tokens.shape, BF16),
                jax.ShapeDtypeStruct((8, tokens.shape[0]), BF16),
                jax.ShapeDtypeStruct((8, D), F32),
            ]
            self.out_specs += [ANYWHERE] + [inside(made.shape) for made in self.out_shapes[-2:]]
            self.chunks = [(NOTES, 0)] + self.chunks + [(TOKENS, k) for k in range(TOKEN_PARTS)]
            self.scratch.append(pltpu.VMEM((4, 2, 16, tokens.shape[0]), BF16))
            self.copies += 1
        self.in_specs = [inside(array.shape) for array in self.inputs]
        n = len(self.chunks)
        self.scratch += [pltpu.SemaphoreType.DMA((self.copies,))]
        for shape in ((n, 2, 3), (n, 2, 3, 2), (n, 2, 3, 2), (n, 7)):
            self.scratch += sem_pair(*shape)
        self.steps = n + 4 * GAP + 1

    def bind(self, ins, outs, scratch):
        self.here, self.ins, self.outs = Place(), ins, outs
        scratch = list(scratch)
        take = lambda n: [scratch.pop(0) for _ in range(n)]
        if self.noted:
            self.notes = take(1)[0]
        self.local = take(1)[0]
        self.z_sems, self.p_sems, self.q_sems, self.c_sems = (take(2) for _ in range(4))

    def block(self, k, source, core=None):
        kind, index = self.chunks[k]
        core = self.here.c if core is None else core
        if kind == NOTES:
            return self.notes.at[source, core]
        if kind == TOKENS:
            tokens = self.outs[len(self.shards)]
            rows = tokens.shape[2] // TOKEN_PARTS
            return tokens.at[source, core, pl.ds(index * rows, rows)]
        return self.outs[index].at[source, core]

    def piece(self, k, source, quarter, half=None):
        if not self.shared(k):
            return self.block(k, source)
        ref = self.outs[self.chunks[k][1]]
        if half is None:
            return ref.at[source, self.here.c, quarter]
        width = ref.shape[-1] // 2
        return ref.at[source, self.here.c, quarter, :, pl.ds(half * width, width)]

    def shared(self, k):
        return self.chunks[k][0] == WEIGHT

    def z_send(self, k, way, hop):
        source, _ = self.here.source(way, hop - 1)
        ref = self.piece(k, source, self.here.r)
        return send(ref, ref, self.z_sems, (k, way, hop - 1), self.here.to_z[way])

    def z_recv(self, k, way, hop):
        source, _ = self.here.source(way, hop)
        ref = self.piece(k, source, self.here.r)
        return send(ref, ref, self.z_sems, (k, way, hop - 1), self.here.to_z[way])

    def p_copy(self, k, way, hop, axis, mine):
        here = self.here
        source, _ = here.source(way, hop)
        ref = self.piece(k, source, here.r if mine else (here.rx, here.ry)[axis])
        return send(ref, ref, self.p_sems, (k, way, hop - 1, axis), (here.to_x, here.to_y)[axis])

    def q_copy(self, k, way, hop, half, mine):
        here = self.here
        source, _ = here.source(way, hop)
        ref = self.piece(k, source, (here.rx, here.ry)[half] if mine else here.rd, half)
        return send(ref, ref, self.q_sems, (k, way, hop - 1, half), (here.to_y, here.to_x)[half])

    def c_copy(self, k, source, index, mine):
        ref = self.block(k, source, self.here.c if mine else 1 - self.here.c)
        return send(ref, ref, self.c_sems, (k, index), self.here.to_core)

    def ways(self, hop, fn):
        for way in (UP, DOWN):
            source, valid = self.here.source(way, hop)
            pl.when(valid)(functools.partial(fn, way, hop, source))

    @staticmethod
    def index_of(way, hop):
        return 1 + way * 3 + hop - 1

    def first_sends(self, k):
        for way in (UP, DOWN):
            pl.when(self.here.more[way])(lambda way=way: self.z_send(k, way, 1).start())
        self.c_copy(k, self.here.z, 0, True).start()

    def stage_z(self, k, hop):
        def arrive(way, hop, source):
            self.z_recv(k, way, hop).wait_recv()
            if hop < 3:
                pl.when(self.here.more[way])(lambda: self.z_send(k, way, hop + 1).start())
            if self.shared(k):
                self.p_copy(k, way, hop, 0, True).start()
                self.p_copy(k, way, hop, 1, True).start()
            else:
                self.c_copy(k, source, self.index_of(way, hop), True).start()
        self.ways(hop, arrive)

    def stage_p(self, k, hop):
        def arrive(way, hop, source):
            for axis in (0, 1):
                self.p_copy(k, way, hop, axis, False).wait_recv()
                self.q_copy(k, way, hop, axis, True).start()
        self.ways(hop, arrive)

    def stage_q(self, k, hop):
        def arrive(way, hop, source):
            self.q_copy(k, way, hop, 0, False).wait_recv()
            self.q_copy(k, way, hop, 1, False).wait_recv()
            self.c_copy(k, source, self.index_of(way, hop), True).start()
        self.ways(hop, arrive)

    def local_copies(self):
        z, c = self.here.z, self.here.c
        copies = []
        for k, shards in enumerate(self.shards):
            first = 0
            for index, width in shards:
                copies.append(pltpu.make_async_copy(
                    self.ins[index], self.outs[k].at[z, c, :, :, pl.ds(first, width)],
                    self.local.at[len(copies)]))
                first += width
        if self.noted:
            copies.append(pltpu.make_async_copy(
                self.ins[len(copies)], self.outs[len(self.shards)].at[z, c], self.local.at[len(copies)]))
        return copies

    def begin(self):
        for copy in self.local_copies():
            copy.start()
        if self.noted:
            z, c = self.here.z, self.here.c
            scenes, mask, *gains = self.ins[self.copies :]
            self.notes[z, c] = jnp.zeros(self.notes.shape[2:], BF16)
            self.notes[z, c, 0:1, :] = low(jnp.where(mask[...] == 1, scenes[...], -1).astype(F32))
            for i, gain in enumerate(gains):
                self.notes[z, c, 1 + i : 2 + i, : gain.shape[1]] = gain[...]

    def begin_sends(self):
        for copy in self.local_copies():
            copy.wait()
        for k in range(min(AHEAD, len(self.chunks))):
            self.first_sends(k)

    def step(self, step):
        total = len(self.chunks)
        if step + AHEAD < total:
            self.first_sends(step + AHEAD)
        for lag, stage in ((0, self.stage_z), (GAP, self.stage_p), (2 * GAP, self.stage_q)):
            for hop in (1, 2, 3):
                k = step - lag - GAP * (hop - 1)
                if 0 <= k < total and (lag == 0 or self.shared(k)):
                    stage(k, hop)

    def finish(self):
        here = self.here
        for k in range(len(self.chunks)):
            for way in (UP, DOWN):
                for hop in (1, 2, 3):
                    _, valid = here.source(way, hop - 1)
                    pl.when(valid & here.more[way])(
                        lambda k=k, way=way, hop=hop: self.z_send(k, way, hop).wait_send())
            self.c_copy(k, here.z, 0, True).wait_send()
            self.c_copy(k, here.z, 0, False).wait_recv()

            def settle(way, hop, source):
                self.c_copy(k, source, self.index_of(way, hop), True).wait_send()
                self.c_copy(k, source, self.index_of(way, hop), False).wait_recv()
                if self.shared(k):
                    for axis in (0, 1):
                        self.p_copy(k, way, hop, axis, True).wait_send()
                        self.q_copy(k, way, hop, axis, True).wait_send()
            for hop in (1, 2, 3):
                self.ways(hop, settle)
        if self.noted:
            tags, gains = self.outs[-2:]
            width = D // 8
            gains[...] = jnp.zeros_like(gains)
            for i in range(8):
                tags[i : i + 1, :] = self.notes[i // 2, i % 2, 0:1, :]
                for j in range(5):
                    gains[j : j + 1, i * width : (i + 1) * width] = self.notes[
                        i // 2, i % 2, 1 + j : 2 + j, :width
                    ].astype(F32)


def gather_kernel(comm, *refs):
    n_in, n_out = len(comm.inputs), len(comm.out_shapes)
    comm.bind(refs[:n_in], refs[n_in : n_in + n_out], refs[n_in + n_out :])
    comm.here.greet()
    comm.begin()
    comm.begin_sends()
    for step in range(comm.steps):
        comm.step(step)
    comm.finish()


def gather_now(comm):
    return call(functools.partial(gather_kernel, comm), (1,), [], [], comm=comm, collective_id=0)


class Peers(Place):
    def __init__(self):
        super().__init__()
        lat = lax.axis_index("lat")
        self.plane = (self.to_x, self.to_y, (self.rd, lat))
        self.quarters = (self.rx, self.ry, self.rd)
        self.above = [lax.rem(self.z + 1 + i, 4) for i in range(3)]
        self.line = [(self.r, z * 2 + self.c) for z in self.above]

    def greet(self):
        barrier = pltpu.get_barrier_semaphore()
        others = (self.to_core, *self.plane, *self.line)
        for device in others:
            pl.semaphore_signal(barrier, inc=1, device_id=device, device_id_type=MESH)
        pl.semaphore_wait(barrier, len(others))


LINE = (
    ((1, UP, 3), (2, DOWN, 0)),
    ((1, UP, 2), (2, DOWN, 1), (2, UP, 3), (1, DOWN, 0)),
    ((1, UP, 1), (2, DOWN, 2), (2, UP, 2), (1, DOWN, 1)),
    ((3, UP, 3), (0, DOWN, 0)),
)


class LineSum:
    def __init__(self, here, block, arrived, sems):
        self.here, self.block, self.arrived, self.sems = here, block, arrived, sems

    def copy(self, way, dest):
        index = (way, dest - 1 if way == UP else dest)
        return send(self.block(dest), self.arrived.at[index], self.sems, index, self.here.to_z[way])

    def start(self):
        @pl.when(self.here.z == 0)
        def _():
            for dest in (3, 2, 1):
                self.copy(UP, dest).start()

        @pl.when(self.here.z == 3)
        def _():
            for dest in (0, 1, 2):
                self.copy(DOWN, dest).start()

    def turn(self, group):
        for device, way, dest in LINE[group]:
            @pl.when(self.here.z == device)
            def _(device=device, way=way, dest=dest):
                self.copy(way, dest).wait_recv()
                ref = self.block(dest)
                ref[...] = ref[...] + self.arrived[way, dest - 1 if way == UP else dest]
                if dest != device:
                    self.copy(way, dest).start()

    def finish(self):
        for dest in (1, 2, 3):
            pl.when(self.here.z < dest)(lambda dest=dest: self.copy(UP, dest).wait_send())
        for dest in (0, 1, 2):
            pl.when(self.here.z > dest)(lambda dest=dest: self.copy(DOWN, dest).wait_send())


class DirectSum(LineSum):
    def copy(self, i):
        return send(self.block(self.here.above[i]), self.arrived.at[0, i], self.sems, (0, i), self.here.line[i])

    def start(self):
        for i in range(3):
            self.copy(i).start()

    def turn(self, group):
        if group == len(LINE) - 1:
            for i in range(3):
                self.copy(i).wait()
            ref, arrived = self.block(self.here.z), self.arrived
            total = ref[...].astype(F32) + arrived[0, 0].astype(F32)
            ref[...] = low(total + arrived[0, 1].astype(F32) + arrived[0, 2].astype(F32))

    def finish(self):
        pass


class Staged:
    def __init__(self, rows, cols):
        self.shape = (rows, cols)


class WeightSum:
    def __init__(self, chunks, gains=None, tokens=None, direct=()):
        self.direct = direct
        self.chunks, self.inputs, self.scratch, self.staged = [], [], [], []
        self.sources = 0
        for chunk in chunks:
            parts = []
            for array in chunk:
                shape = (4, 2, 4, array.shape[0] // 32, array.shape[1])
                if isinstance(array, Staged):
                    parts.append((self.sources, None, len(self.staged), shape[-1]))
                    self.staged.append(pltpu.VMEM(shape, BF16))
                else:
                    parts.append((self.sources, len(self.inputs), None, shape[-1]))
                    self.inputs.append(array.reshape(shape))
                self.sources += 1
            self.chunks.append((parts, shape[3], sum(part[3] for part in parts)))
        self.out_shapes = [
            jax.ShapeDtypeStruct((4, rows, cols), BF16) for _, rows, cols in self.chunks
        ]
        for _, rows, cols in self.chunks:
            half = cols // 2
            self.scratch += [
                pltpu.VMEM((4, 2, 2, rows, cols), BF16),
                pltpu.VMEM((4, 2, 2, rows, cols), BF16),
                pltpu.VMEM((2, 4, 2, rows, half), BF16),
                pltpu.VMEM((2, 4, rows, half), BF16),
                pltpu.VMEM((2, 3, rows, cols), BF16),
                pltpu.VMEM((4, rows, cols), BF16),
            ]
        n = len(self.chunks)
        self.scratch += self.staged
        self.scratch += [pltpu.SemaphoreType.DMA((self.sources, 2))]
        for shape in ((self.sources, 2), (n, 2), (n, 2), (n, 2, 3), (n, 3)):
            self.scratch += sem_pair(*shape)
        self.gains, self.tokens = gains, tokens
        if gains is not None:
            self.out_shapes.append(jax.ShapeDtypeStruct(gains, F32))
            self.scratch += [pltpu.VMEM(shape + gains, F32) for shape in ((), (), (4,), (3,))]
            self.scratch += sem_pair(1) + sem_pair(3) + sem_pair(3)
        if tokens is not None:
            self.out_shapes.append(jax.ShapeDtypeStruct((tokens // 8, D), BF16))
            self.scratch += [pltpu.VMEM((4, tokens // 8, D), BF16)]
            self.scratch += [pltpu.VMEM((2, tokens // 8, D), BF16)]
            self.scratch += [pltpu.VMEM((2, 3, tokens // 8, D), BF16)]
            self.scratch += sem_pair(1) + sem_pair(2, 3)
        self.in_specs = [ANYWHERE] * len(self.inputs)
        self.out_specs = [inside(made.shape) for made in self.out_shapes]

    def bind(self, ins, outs, scratch):
        self.here = Peers()
        self.ins, self.outs = ins, outs
        scratch = list(scratch)
        take = lambda n: [scratch.pop(0) for _ in range(n)]
        self.buffers = [take(6) for _ in self.chunks]
        self.stages = take(len(self.staged))
        self.local = take(1)[0]
        self.c_sems, self.x_sems, self.y_sems, self.z_sems, self.g_sems = (take(2) for _ in range(5))
        if self.gains is not None:
            self.gain_buffers = take(4)
            self.gain_sems = [take(2) for _ in range(3)]
        if self.tokens is not None:
            self.token_mine, self.token_window, arrived = take(3)
            self.token_sems = take(2)
            self.token_line = LineSum(self.here, lambda z: self.token_mine.at[z], arrived, take(2))


    def parts(self, k):
        first = 0
        for source, given, staged, width in self.chunks[k][0]:
            ref = self.stages[staged] if given is None else self.ins[given]
            yield source, ref, pl.ds(first, width)
            first += width

    def halves(self, k):
        half = self.chunks[k][2] // 2
        return pl.ds(0, half), pl.ds(half, half)

    def own(self, k):
        for source, ref, cols in self.parts(k):
            for y in range(2):
                yield pltpu.make_async_copy(
                    ref.at[:, self.here.c, pl.ds(2 * y, 2)],
                    self.buffers[k][0].at[:, y, :, :, cols],
                    self.local.at[source, y],
                )

    def to_core(self, k):
        for source, ref, cols in self.parts(k):
            for y in range(2):
                yield send(
                    ref.at[:, 1 - self.here.c, pl.ds(2 * y, 2)],
                    self.buffers[k][1].at[:, y, :, :, cols],
                    self.c_sems, (source, y), self.here.to_core,
                )

    def first_turn(self, k):
        mine, theirs, here = self.buffers[k][0], self.buffers[k][2], self.here
        left, right = self.halves(k)
        yield send(mine.at[:, :, 1 - here.x, :, left], theirs.at[0], self.x_sems, (k, 0), here.to_x)
        yield send(mine.at[:, 1 - here.y, :, :, right], theirs.at[1], self.x_sems, (k, 1), here.to_y)

    def second_turn(self, k):
        mine, theirs, here = self.buffers[k][0], self.buffers[k][3], self.here
        left, right = self.halves(k)
        yield send(mine.at[:, 1 - here.y, here.x, :, left], theirs.at[0], self.y_sems, (k, 0), here.to_y)
        yield send(mine.at[:, here.y, 1 - here.x, :, right], theirs.at[1], self.y_sems, (k, 1), here.to_x)

    def line(self, k):
        here, buffers = self.here, self.buffers[k]
        sems = [sem.at[k] for sem in self.z_sems]
        kind = DirectSum if k in self.direct else LineSum
        return kind(here, lambda z: buffers[0].at[z, here.y, here.x], buffers[4], sems)

    def finished(self, k):
        for i in range(3):
            mine = self.buffers[k][5].at[self.here.r]
            yield send(mine, mine, self.g_sems, (k, i), self.here.plane[i])

    def arriving(self, k):
        for i in range(3):
            theirs = self.buffers[k][5].at[self.here.quarters[i]]
            yield send(theirs, theirs, self.g_sems, (k, i), self.here.plane[i])


    def start(self, k):
        for copy in (*self.own(k), *self.to_core(k)):
            copy.start()

    def in_chip(self, k):
        for copy in self.own(k):
            copy.wait()
        for copy in self.to_core(k):
            copy.wait_recv()
        mine, theirs = self.buffers[k][:2]
        for z in range(4):
            for y in range(2):
                for x in range(2):
                    mine[z, y, x] = mine[z, y, x] + theirs[z, y, x]
        for copy in self.first_turn(k):
            copy.start()

    def in_pairs(self, k):
        for copy in self.first_turn(k):
            copy.wait()
        mine, theirs, here = self.buffers[k][0], self.buffers[k][2], self.here
        left, right = self.halves(k)
        for z in range(4):
            for i in range(2):
                mine[z, i, here.x, :, left] = mine[z, i, here.x, :, left] + theirs[0, z, i]
                mine[z, here.y, i, :, right] = mine[z, here.y, i, :, right] + theirs[1, z, i]
        for copy in self.second_turn(k):
            copy.start()

    def in_plane(self, k):
        for copy in self.second_turn(k):
            copy.wait()
        mine, theirs, here = self.buffers[k][0], self.buffers[k][3], self.here
        for z in range(4):
            for i, cols in enumerate(self.halves(k)):
                mine[z, here.y, here.x, :, cols] = mine[z, here.y, here.x, :, cols] + theirs[i, z]
        self.line(k).start()

    def turn0(self, k):
        self.line(k).turn(0)

    def turn1(self, k):
        self.line(k).turn(1)

    def turn2(self, k):
        self.line(k).turn(2)

    def in_line(self, k):
        self.line(k).turn(3)
        mine, done, here = self.buffers[k][0], self.buffers[k][5], self.here
        done[here.r] = mine[here.z, here.y, here.x]
        for copy in self.finished(k):
            copy.start()

    def end(self, k):
        for copy in self.arriving(k):
            copy.wait_recv()
        for copy in (*self.to_core(k), *self.finished(k)):
            copy.wait_send()
        self.line(k).finish()
        self.outs[k][...] = self.buffers[k][5][...]


    def gain_copy(self, stage, i):
        mine, core, plane, line = self.gain_buffers
        if stage == 0:
            return send(mine, core, self.gain_sems[0], 0, self.here.to_core)
        if stage == 1:
            return send(mine, plane.at[self.here.r], self.gain_sems[1], i, self.here.plane[i])
        return send(mine, line.at[i], self.gain_sems[2], i, self.here.line[i])

    def gain_plane_recv(self, i):
        mine, _, plane, _ = self.gain_buffers
        return send(mine, plane.at[self.here.quarters[i]], self.gain_sems[1], i, self.here.plane[i])

    def gain_step(self, stage):
        mine, core, plane, line = self.gain_buffers
        if stage == 0:
            self.gain_copy(0, 0).start()
        elif stage == 1:
            self.gain_copy(0, 0).wait()
            mine[...] += core[...]
            plane[self.here.r] = mine[...]
            for i in range(3):
                self.gain_copy(1, i).start()
        elif stage == 2:
            for i in range(3):
                self.gain_copy(1, i).wait_send()
                self.gain_plane_recv(i).wait_recv()
            mine[...] = (plane[0] + plane[1]) + (plane[2] + plane[3])
            for i in range(3):
                self.gain_copy(2, i).start()
        else:
            for i in range(3):
                self.gain_copy(2, i).wait()
            self.outs[len(self.chunks)][...] = (mine[...] + line[0]) + (line[1] + line[2])


    def token_core(self):
        mine = self.token_window.at[self.here.c]
        return send(mine, mine, self.token_sems, 0, self.here.to_core)

    def token_core_recv(self):
        theirs = self.token_window.at[1 - self.here.c]
        return send(theirs, theirs, self.token_sems, 0, self.here.to_core)

    def token_place(self, start):
        self.token_core().wait_send()
        self.token_core_recv().wait_recv()
        count, rows = 2 * self.token_window.shape[1], self.token_mine.shape[1]
        window = self.token_window[...].reshape(count, D)
        for z in range(4):
            slot = lax.broadcasted_iota(jnp.int32, (rows, count), 0) + (2 * z + self.here.c) * rows
            row = lax.broadcasted_iota(jnp.int32, (rows, count), 1) + start
            self.token_mine[z] = low(dot(low(jnp.where(slot == row, 1.0, 0.0)), window))
        self.token_line.start()

    def token_end(self):
        self.token_line.turn(3)
        self.outs[-1][...] = self.token_mine[self.here.z]
        self.token_line.finish()


def tail_kernel(
    comm, lat_ref, do_ref, p_ref, q_ref, kv_ref, gain_ref, wq_ref, wkv_ref, win_ref, start_ref,
    dm1_ref, ds_ref, dm2_ref, *refs,
):
    n_in, n_out = len(comm.inputs), len(comm.out_shapes)
    ins, lg_ref = refs[:n_in], refs[n_in]
    outs, scratch = refs[n_in + 1 : n_in + 1 + n_out], refs[n_in + 1 + n_out :]
    kv_sum, dkv_ref, more_ref, kv_sems = scratch[0], scratch[1], scratch[2], scratch[3:5]
    comm.bind(ins, outs, scratch[5:])
    here = comm.here
    mixed = len(comm.chunks) - 2
    early, last = range(mixed), mixed + 1
    rows, span = p_ref.shape
    gains = comm.gain_buffers[0]

    here.greet()
    for k in early:
        comm.start(k)
    block = rows // 2
    dwq = None
    gains[...] = jnp.zeros_like(gains)
    for i in range(2):
        at = slice(i * block, (i + 1) * block)
        p, do, q = p_ref[at], do_ref[at], q_ref[at]
        dp = dot_nt(do, kv_ref[:, D:])
        wide_p = p.astype(F32)
        ds = low(wide_p * (dp - jnp.sum(wide_p * dp, axis=1, keepdims=True)))
        dq = low(dot(ds, kv_ref[:, :D]) * CROSS_SCALE)
        dk, dv = dot_tn(ds, q), dot_tn(p, do)
        if i == 0:
            kv_sum[:, :D], kv_sum[:, D:] = dk, dv
        else:
            dkv_ref[:, :D] = low((kv_sum[:, :D] + dk) * CROSS_SCALE)
            dkv_ref[:, D:] = low(kv_sum[:, D:] + dv)
        unit, factor = normed(lat_ref[at].astype(F32))
        gain = gain_ref[0:1, :]
        term = dot_tn(low(unit * gain), dq)
        dwq = term if dwq is None else dwq + term
        back, dgain = norm_back(dot_nt(dq, wq_ref[...]), unit, factor, gain)
        lg_ref[at] = low(back)
        gains[0:1] += dgain
        if i < mixed:
            comm.in_chip(i)
    for k in range(2, mixed):
        comm.in_chip(k)
    half = span // 2
    to_core = send(
        dkv_ref.at[pl.ds(half * (1 - here.c), half)], more_ref, kv_sems, 0, here.to_core)
    to_core.start()
    comm.stages[0][...] = low(dwq).reshape(comm.stages[0].shape)
    comm.start(mixed)
    gains[2:3], gains[3:4], gains[4:5] = dm1_ref[0:1], ds_ref[0:1], dm2_ref[0:1]
    unit, factor = normed(win_ref[pl.ds(half * here.c, half)].astype(F32))
    gain = gain_ref[1:2, :]
    to_core.wait()
    dkv = low(dkv_ref[pl.ds(half * here.c, half)].astype(F32) + more_ref[...].astype(F32))
    back, dgain = norm_back(dot_nt(dkv, wkv_ref[...]), unit, factor, gain)
    comm.token_window[here.c] = low(back)
    comm.token_core().start()
    gains[1:2] = dgain
    comm.gain_step(0)
    comm.stages[1][...] = low(dot_tn(low(unit * gain), dkv)).reshape(comm.stages[1].shape)
    comm.start(last)
    comm.token_place(start_ref[0:1, 0:1])
    comm.in_chip(mixed)
    comm.in_pairs(0)
    comm.in_pairs(1)
    comm.gain_step(1)
    comm.in_chip(last)
    comm.token_line.turn(0)
    comm.in_pairs(2)
    comm.in_plane(0)
    comm.in_pairs(mixed)
    comm.in_plane(1)
    comm.token_line.turn(1)
    comm.in_pairs(last)
    for k in (0, 1):
        comm.turn0(k)
    comm.in_plane(2)
    comm.gain_step(2)
    for k in (0, 1):
        comm.turn1(k)
    comm.in_plane(mixed)
    comm.token_line.turn(2)
    comm.in_plane(last)
    for k in (0, 1):
        comm.turn2(k)
    for k in (2, mixed):
        comm.turn0(k)
    for k in (0, 1):
        comm.in_line(k)
    for k in (2, mixed):
        comm.turn1(k)
    comm.gain_step(3)
    for k in (2, mixed):
        comm.turn2(k)
    comm.in_line(last)
    comm.token_end()
    for k in (2, mixed):
        comm.in_line(k)
    for k in range(last + 1):
        comm.end(k)


def tail(comm, latents, do, p, q, kv, gains, mix, window, start, dgains):
    rows, span = p.shape
    r = (rows, D)
    return call(
        functools.partial(tail_kernel, comm),
        (1,),
        [
            (latents, r, flat),
            (do, r, flat),
            (p, p.shape, flat),
            (q, r, flat),
            (kv, kv.shape, flat),
            (gains, (8, D), flat),
            (mix, (D, D), column(2)),
            (mix, (D, 2 * D), column(0)),
            (window, (span, D), flat),
            (start, start.shape, flat),
        ]
        + [(g, (8, D), flat) for g in dgains],
        [(r, BF16, r, flat)],
        [
            pltpu.VMEM((span, 2 * D), F32),
            pltpu.VMEM((span, 2 * D), BF16),
            pltpu.VMEM((span // 2, 2 * D), BF16),
        ]
        + sem_pair(1),
        comm=comm,
        collective_id=2,
    )


def widen_kernel(cuts, base_ref, term_ref, *refs):
    sources, (sum_ref, *targets) = refs[: len(cuts)], refs[len(cuts) :]
    sum_ref[...] = base_ref[...] + term_ref[...].astype(F32)
    for source, widths in zip(sources, cuts):
        first = 0
        for width in widths:
            targets.pop(0)[...] = source[:, first : first + width].astype(F32)
            first += width


def widen(base, term, arrays, cuts):
    steps = 4
    rows = lambda array: array.shape[0] // steps
    return call(
        functools.partial(widen_kernel, cuts),
        (steps,),
        [(a, (rows(a), a.shape[1]), rows_of) for a in (base, term, *arrays)],
        [(base.shape, F32, (rows(base), base.shape[1]), rows_of)]
        + [
            ((a.shape[0], width), F32, (rows(a), width), rows_of)
            for a, widths in zip(arrays, cuts)
            for width in widths
        ],
    )


def from_partner(shard, bit):
    return lax.ppermute(shard, "lat", [(i, i ^ 1 << bit) for i in range(lax.axis_size("lat"))])


def gather_lat(shard):
    return lax.all_gather(shard, "lat", axis=0, tiled=True)


def halve(value, place, bits):
    kept, more = value, jnp.zeros_like(value)
    for bit in reversed(range(bits)):
        value = low(kept.astype(F32) + more.astype(F32))
        half = value.shape[0] // 2
        upper = place // 2**bit % 2
        kept = lax.dynamic_slice_in_dim(value, upper * half, half)
        more = from_partner(lax.dynamic_slice_in_dim(value, (1 - upper) * half, half), bit)
    return kept, more


def reduce_weights(grad):
    share = lax.psum_scatter(grad, "lat", scatter_dimension=0, tiled=True)
    return lax.psum(share, "row").astype(F32)


def local(
    tokens, latents, segment_ids, pad_mask, block_scene, out_grad,
    gain_cross_q, gain_cross_kv, w_cross_q, w_cross_kv, w_cross_out,
    gain_mlp1, w_up1, w_down1, gain_self, w_self_qkv, w_self_out, gain_mlp2, w_up2, w_down2,
):
    tokens, latents, og = tokens[0], latents[0], out_grad[0]
    rows, slots = latents.shape[0], tokens.shape[0] * lax.axis_size("lat")
    scenes = block_scene.shape[1]
    span = slots // scenes
    place = lax.axis_index("lat")
    group = LAT_SCENE // rows
    bits = group.bit_length() - 1

    gains = [gain_cross_q, gain_cross_kv, gain_mlp1, gain_self, gain_mlp2]
    first_weights = [[w_cross_kv, w_cross_q, w_cross_out], [w_up1], [w_down1], [w_self_qkv]]
    later_weights = [[w_up2], [w_down2], [w_self_out]]
    planes = lax.axis_size("row") == 4 and lax.axis_size("lat") == 8 and group == 2
    join = lambda gathered: [w.reshape(-1, w.shape[-1]) for w in gathered]
    if planes:
        notes = [segment_ids, pad_mask] + [g.reshape(1, -1) for g in gains]
        *weights, all_tokens, tags, gains = gather_now(Gather(first_weights, tokens, notes))
        mix, up1, down1, qkv, all_tokens = join([*weights, all_tokens])
    else:
        tag = jnp.where(pad_mask == 1, segment_ids, -1)
        tags = gather_lat(low(tag))
        all_tokens = gather_lat(tokens)
        gains = lax.all_gather(jnp.stack(gains), "lat", axis=1, tiled=True)
        gains = jnp.pad(gains.astype(F32), ((0, 3), (0, 0)))
        mix, up1, down1, qkv, up2, down2, so = (
            gather_lat(jnp.concatenate(shards, axis=1)) for shards in first_weights + later_weights
        )

    x1, x2, q, p, o, kv, q2, k2, v2, window, start = front(
        latents, all_tokens, tags, block_scene, span, gains, mix, up1, down1, qkv
    )
    if planes:
        o2, p2, scale2, k2_more, v2_more, *weights = self_forward(q2, (k2,), (v2,), Gather(later_weights))
        up2, down2, so = join(weights)
        keys, values = (k2, k2_more), (v2, v2_more)
    else:
        for bit in range(bits):
            upper = place // 2**bit % 2 == 1
            more = from_partner((k2, v2), bit)
            k2, v2 = (
                jnp.where(upper, jnp.concatenate([b, a]), jnp.concatenate([a, b]))
                for a, b in zip((k2, v2), more)
            )
        keys, values = (k2,), (v2,)
        o2, p2, scale2 = self_forward(q2, keys, values)
    out, g3, do2, dwup2, dwdown2, dwso, dgain_m2 = second(x2, o2, og, gains, so, up2, down2)
    comm = WeightSum([[dwup2], [dwdown2], [dwso]], direct=(0, 1, 2)) if planes else None
    dq2, dkv2, early = self_backward(q2, do2, o2, scale2, p2, keys, values, comm)
    if planes:
        dk, dv, dk_more, dv_more = dkv2
    else:
        dk, dk_more = halve(dkv2[0], place, bits)
        dv, dv_more = halve(dkv2[1], place, bits)
    g1, do, dwqkv, dwup1, dwdown1, dwout, dgain_s, dgain_m1 = middle_back(
        x2, g3, dq2, dk, dk_more, dv, dv_more, x1, o, gains, qkv, mix, up1, down1
    )
    if planes:
        comm = WeightSum(
            [[dwqkv], [dwup1], [dwdown1], [Staged(D, D), dwout], [Staged(D, 2 * D)]], gains=(8, D), tokens=slots,
            direct=(4,),
        )
        term, *late, dgains, token_grad = tail(
            comm, latents, do, p, q, kv, gains, mix, window, start, (dgain_m1, dgain_s, dgain_m2)
        )
        dgains = lax.dynamic_slice_in_dim(dgains, place * (D // 8), D // 8, axis=1)
        up2, down2, so, qkv, up1, down1, mixed, dwkv = join([*early, *late])
        latent_grad, token_grad, dwq, dwout, dwkv, *others = widen(
            g1, term, [token_grad, mixed, dwkv, up1, down1, qkv, so, up2, down2],
            ((D,), (D, D), (2 * D,), (FF,), (D,), (3 * D,), (D,), (FF,), (D,)),
        )
        sums = dwq, dwkv, dwout, *others
    else:
        latent_grad, dwq, dkv, dgain_q = cross_back(latents, g1, do, p, q, kv, gains, mix)
        mine, more = halve(dkv, place, bits)
        first = place % group * (span // group)
        token_rows = lax.dynamic_slice_in_dim(window, first, span // group)
        token_part, dwkv, dgain_kv = token_back(token_rows, mine, more, gains, mix)
        token_part = lax.dynamic_update_slice_in_dim(
            jnp.zeros((slots, D), BF16), token_part, start[0, 0] + first, 0
        )
        token_grad = lax.psum_scatter(token_part, "lat", scatter_dimension=0, tiled=True).astype(F32)
        dgains = jnp.stack([g[0] for g in (dgain_q, dgain_kv, dgain_m1, dgain_s, dgain_m2)])
        dgains = lax.psum_scatter(low(dgains), "lat", scatter_dimension=1, tiled=True)
        dgains = lax.psum(dgains, "row").astype(F32)
        sums = [
            reduce_weights(g) for g in (dwq, dwkv, dwout, dwup1, dwdown1, dwqkv, dwso, dwup2, dwdown2)
        ]
    dwq, dwkv, dwout, dwup1, dwdown1, dwqkv, dwso, dwup2, dwdown2 = sums
    return (
        out[None],
        latent_grad[None],
        token_grad[None],
        dgains[0],
        dgains[1],
        dwq,
        dwkv,
        dwout,
        dgains[2],
        dwup1,
        dwdown1,
        dgains[3],
        dwqkv,
        dwso,
        dgains[4],
        dwup2,
        dwdown2,
    )


def solution(mesh):
    by_row = P("row", "lat", None)
    weight = P("lat", None)
    gain = P("lat")
    parameters = (
        gain, gain, weight, weight, weight, gain, weight, weight, gain, weight, weight, gain,
        weight, weight,
    )
    return jax.shard_map(
        local,
        mesh=mesh,
        in_specs=(by_row, by_row, P("row", "lat"), P("row", "lat"), P("row", None), by_row)
        + parameters,
        out_specs=(by_row, by_row, by_row) + parameters,
        check_vma=False,
    )
```

```python
import functools

import jax
import jax.numpy as jnp
from jax import lax
from jax.experimental import pallas as pl
from jax.experimental.pallas import tpu as pltpu
from jax.sharding import PartitionSpec as P

D = 512
FF = 2048
HEADS = 8
LAT_SCENE = 2048
HEAD = D // HEADS
PAIRS = HEADS // 2
LANES = 128
FF_STEP = 512
EPS = 1e-05
NEG = -1e30
CROSS_SCALE = D ** (-0.5)
SELF_SCALE = HEAD ** (-0.5)
GELU_C = 0.7978845608028654
GELU_K = 0.044715
VMEM_LIMIT = 60 * 1024 * 1024
F32 = jnp.float32
BF16 = jnp.bfloat16


def low(value):
    return value.astype(BF16)


def dot(left, right):
    return jnp.dot(left, right, preferred_element_type=F32)


def dot_nt(left, right):
    return lax.dot_general(left, right, (((1,), (1,)), ((), ())), preferred_element_type=F32)


def dot_tn(left, right):
    return lax.dot_general(left, right, (((0,), (0,)), ((), ())), preferred_element_type=F32)


def normed(value):
    centered = value - jnp.mean(value, axis=-1, keepdims=True)
    factor = lax.rsqrt(jnp.mean(centered * centered, axis=-1, keepdims=True) + EPS)
    return centered * factor, factor


def norm_back(grad, unit, factor, gain):
    scaled = grad * gain
    inner = (
        scaled
        - jnp.mean(scaled, axis=-1, keepdims=True)
        - unit * jnp.mean(scaled * unit, axis=-1, keepdims=True)
    )
    return factor * inner, jnp.sum(grad * unit, axis=0, keepdims=True)


def gelu(u):
    return 0.5 * u * (1.0 + jnp.tanh(GELU_C * (u + GELU_K * u * u * u)))


def gelu_both(u):
    square = u * u
    t = jnp.tanh(GELU_C * u * (1.0 + GELU_K * square))
    half = 0.5 * (1.0 + t)
    slope = half + 0.5 * u * (1.0 - t * t) * (GELU_C * (1.0 + 3.0 * GELU_K * square))
    return u * half, slope


def call(kernel, grid, ins, outs, scratch=(), comm=None, collective_id=None):
    in_specs = [ANYWHERE if block is None else pl.BlockSpec(block, index) for _, block, index in ins]
    out_specs = [ANYWHERE if block is None else pl.BlockSpec(block, index) for _, _, block, index in outs]
    out_shape = [jax.ShapeDtypeStruct(shape, kind) for shape, kind, _, _ in outs]
    arrays, scratch = [array for array, _, _ in ins], list(scratch)
    if comm is not None:
        arrays += comm.inputs
        in_specs += comm.in_specs
        out_shape += comm.out_shapes
        out_specs += comm.out_specs
        scratch += comm.scratch
    return pl.pallas_call(
        kernel,
        grid=grid,
        in_specs=in_specs,
        out_specs=out_specs,
        out_shape=out_shape,
        scratch_shapes=scratch,
        compiler_params=pltpu.CompilerParams(
            vmem_limit_bytes=VMEM_LIMIT,
            collective_id=None if comm is None else collective_id,
            has_side_effects=comm is not None,
        ),
    )(*arrays)


def inside(shape):
    return pl.BlockSpec(shape, lambda *_: (0,) * len(shape))


ANYWHERE = pl.BlockSpec(memory_space=pl.ANY)


def flat(*_):
    return (0, 0)


def column(c):
    return lambda *_: (0, c)


def rows_of(i, *_):
    return (i, 0)


def front_kernel(
    lat_rows, lat_ref, tok_ref, tags_ref, scene_ref, gain_ref, wq_ref, wkv_ref, wout_ref, wup_ref, wdown_ref, wqkv_ref,
    x1_ref, x2_ref, q_ref, p_ref, o_ref, kv_ref, q2_ref, k2_ref, v2_ref, win_ref, start_ref,
    bias_ref, sem,
):
    @pl.when(pl.program_id(0) == 0)
    def _():
        span, slots = win_ref.shape[0], tok_ref.shape[0]
        tags, scenes = tags_ref[...].astype(F32), scene_ref[...]
        own = lax.axis_index("lat") * lat_rows // LAT_SCENE
        own = lax.broadcasted_iota(jnp.int32, scenes.shape, 1) == own
        scene = jnp.sum(jnp.where(own, scenes, 0).astype(F32))
        count = lambda chosen: jnp.sum(jnp.where(chosen, 1.0, 0.0)).astype(jnp.int32)
        before = count((tags >= 0.0) & (tags < scene))
        length = count(tags == scene)
        start = pl.multiple_of(jnp.minimum(before // 16 * 16, slots - span), 16)
        copy = pltpu.make_async_copy(tok_ref.at[pl.ds(start, span)], win_ref, sem)
        copy.start()
        start_ref[...] = jnp.full(start_ref.shape, start, jnp.int32)
        slot = lax.broadcasted_iota(jnp.int32, bias_ref.shape, 1) + start
        bias_ref[...] = jnp.where((slot >= before) & (slot < before + length), 0.0, NEG)
        copy.wait()
        unit, _ = normed(win_ref[...].astype(F32))
        kv_ref[...] = low(dot(low(unit * gain_ref[1:2, :]), wkv_ref[...]))

    x = lat_ref[...].astype(F32)
    unit, _ = normed(x)
    q = low(dot(low(unit * gain_ref[0:1, :]), wq_ref[...]))
    q_ref[...] = q
    s = dot_nt(q, kv_ref[:, :D]) * CROSS_SCALE + bias_ref[0:1, :]
    e = jnp.exp(s - jnp.max(s, axis=1, keepdims=True))
    p = low(e / jnp.sum(e, axis=1, keepdims=True))
    p_ref[...] = p
    o = low(dot(p, kv_ref[:, D:]))
    o_ref[...] = o
    x1 = x + dot(o, wout_ref[...])
    x1_ref[...] = x1
    unit, _ = normed(x1)
    m1 = low(unit * gain_ref[2:3, :])
    total = x1
    for c in range(FF // FF_STEP):
        cols = slice(c * FF_STEP, (c + 1) * FF_STEP)
        h = low(gelu(dot(m1, wup_ref[:, cols])))
        total = total + dot(h, wdown_ref[cols, :])
    x2_ref[...] = total
    unit, _ = normed(total)
    bn = low(unit * gain_ref[3:4, :])
    q2_ref[...] = low(dot(bn, wqkv_ref[:, :D])) * SELF_SCALE
    k2_ref[...] = low(dot(bn, wqkv_ref[:, D : 2 * D]))
    v2_ref[...] = low(dot(bn, wqkv_ref[:, 2 * D :]))


def front(latents, tokens, tags, scene, span, gains, mix, up1, down1, qkv):
    rows = latents.shape[0]
    block = min(rows, 512)
    r = (block, D)
    return call(
        functools.partial(front_kernel, rows),
        (rows // block,),
        [
            (latents, r, rows_of),
            (tokens, None, None),
            (tags, tags.shape, flat),
            (scene, scene.shape, flat),
            (gains, (8, D), flat),
            (mix, (D, D), column(2)),
            (mix, (D, 2 * D), column(0)),
            (mix, (D, D), column(3)),
            (up1, (D, FF), flat),
            (down1, (FF, D), flat),
            (qkv, (D, 3 * D), flat),
        ],
        [
            ((rows, D), F32, r, rows_of),
            ((rows, D), F32, r, rows_of),
            ((rows, D), BF16, r, rows_of),
            ((rows, span), BF16, (block, span), rows_of),
            ((rows, D), BF16, r, rows_of),
            ((span, 2 * D), BF16, (span, 2 * D), flat),
            ((rows, D), BF16, r, rows_of),
            ((rows, D), BF16, r, rows_of),
            ((rows, D), BF16, r, rows_of),
            ((span, D), BF16, (span, D), flat),
            ((8, LANES), jnp.int32, (8, LANES), flat),
        ],
        [pltpu.VMEM((8, span), F32), pltpu.SemaphoreType.DMA],
    )


def lane_is(shape, head):
    lane = lax.broadcasted_iota(jnp.int32, shape, 1)
    return (lane < HEAD) if head == 0 else (lane >= HEAD)


def only(value, head):
    return jnp.where(lane_is(value.shape, head), value, jnp.zeros_like(value))


def self_forward_kernel(parts, steps, comm, q_ref, *refs):
    refs = list(refs)
    take = lambda n: [refs.pop(0) for _ in range(n)]
    pair, step = pl.program_id(0), pl.program_id(1)
    point = pair * steps + step
    if comm is None:
        k_refs, v_refs = take(parts), take(parts)
        o_ref, p_ref, scale_ref = take(3)
        ones_refs = refs
    else:
        (k_ref,), (v_ref,) = take(1), take(1)
        both = take(2)
        ins = take(len(comm.inputs))
        o_ref, p_ref, scale_ref, k_more, v_more = take(5)
        outs = take(len(comm.out_shapes))
        ones_refs, (landed,), sems = take(2), take(1), take(2)
        comm.bind(ins, outs, refs)
        k_refs, v_refs = (k_ref, k_more), (v_ref, v_more)

        def to_core(i, p):
            cols = pl.ds(p * LANES, LANES)
            return send(both[i].at[:, cols], landed.at[i, p], sems, (i, p), comm.here.to_core)

        @pl.when(point == 0)
        def _():
            comm.here.greet()
            for p in range(PAIRS):
                for i in range(2):
                    to_core(i, p).start()
            comm.begin()

        pl.when(point == 1)(comm.begin_sends)
        for i in range(comm.steps):
            pl.when(point == SHIFT + i)(functools.partial(comm.step, i))

        @pl.when(step == 0)
        def _():
            for i, ref in enumerate((k_more, v_more)):
                arrived = landed.at[i, pair]
                send(arrived, arrived, sems, (i, pair), comm.here.to_core).wait_recv()
                ref[...] = arrived[...]

    @pl.when(step == 0)
    def _():
        for v_ref, ones_ref in zip(v_refs, ones_refs):
            v = v_ref[...]
            for head in range(2):
                ones_ref[head] = jnp.where(lane_is(v.shape, head), v, jnp.ones_like(v))

    q = q_ref[...]
    outs, scales = [], []
    for head in range(2):
        scores = [dot_nt(only(q, head), k_ref[...]) for k_ref in k_refs]
        top = functools.reduce(jnp.maximum, [jnp.max(s, axis=1, keepdims=True) for s in scores])
        mixed, first = None, 0
        for s, ones_ref in zip(scores, ones_refs):
            p = low(jnp.exp(s - top))
            p_ref[head, :, first : first + p.shape[1]] = p
            first += p.shape[1]
            term = dot(p, ones_ref[head])
            mixed = term if mixed is None else mixed + term
        scales.append(1.0 / pltpu.roll(mixed, HEAD, 1))
        outs.append(mixed * scales[-1])
    left = lane_is(outs[0].shape, 0)
    o_ref[...] = low(jnp.where(left, outs[0], outs[1]))
    scale_ref[...] = jnp.where(left, scales[0], scales[1])

    if comm is not None:
        @pl.when(point == PAIRS * steps - 1)
        def _():
            for p in range(PAIRS):
                for i in range(2):
                    to_core(i, p).wait_send()
            comm.finish()


def self_forward(q2, keys, values, comm=None):
    rows = q2.shape[0]
    block = min(rows, 256)
    parts = len(keys)
    total = sum(k.shape[0] for k in keys) * (1 if comm is None else 2)
    whole = lambda array: (array, (array.shape[0], LANES), lambda p, i: (0, p))
    more = ((rows, D), BF16, (rows, LANES), lambda p, i: (0, p))
    beside = comm is not None
    return call(
        functools.partial(self_forward_kernel, parts, rows // block, comm),
        (PAIRS, rows // block),
        [(q2, (block, LANES), lambda p, i: (i, p))]
        + [whole(k) for k in keys]
        + [whole(v) for v in values]
        + ([(keys[0], None, None), (values[0], None, None)] if beside else []),
        [
            ((rows, D), BF16, (block, LANES), lambda p, i: (i, p)),
            ((HEADS, rows, total), BF16, (2, block, total), lambda p, i: (p, i, 0)),
            ((rows, D), F32, (block, LANES), lambda p, i: (i, p)),
        ]
        + ([more, more] if beside else []),
        [pltpu.VMEM((2, k.shape[0], LANES), BF16) for k in keys * (2 if beside else 1)]
        + ([pltpu.VMEM((2, PAIRS, rows, LANES), BF16)] + sem_pair(2, PAIRS) if beside else []),
        comm=comm,
        collective_id=3,
    )


def run_beside(comm, point, plan, odd):
    for when, work in plan.items():
        if when % 2 != odd:
            continue
        def run(when=when, work=work):
            if when == 0:
                comm.here.greet()
            for name, k in work:
                getattr(comm, name)(k)
        pl.when(point == when)(run)


SELF_PLAN = {
    0: (("start", 0), ("start", 1), ("start", 2)),
    4: (("in_chip", 0),),
    6: (("in_chip", 1),),
    7: (("in_chip", 2),),
    10: (("in_pairs", 0),),
    14: (("in_pairs", 1),),
    16: (("in_pairs", 2),),
    17: (("in_plane", 0),),
    20: (("in_plane", 1),),
    21: (("in_plane", 2),),
    23: (("in_line", 0),),
    27: (("in_line", 1),),
    29: (("in_line", 2),),
    31: (("end", 0), ("end", 1), ("end", 2)),
}


def self_backward_kernel(parts, steps, comm, q_ref, do_ref, o_ref, scale_ref, p_ref, *refs):
    refs = list(refs)
    take = lambda n: [refs.pop(0) for _ in range(n)]
    pair, step = pl.program_id(0), pl.program_id(1)
    point = 2 * (pair * steps + step)
    k_refs, v_refs = take(parts), take(parts)
    if comm is None:
        (dq_ref,), dk_refs, dv_refs = take(1), take(parts), take(parts)
        dk_sums, dv_sums = take(parts), take(parts)
    else:
        ins = take(len(comm.inputs))
        dq_ref, dk_ref, dv_ref, *landed = take(5)
        outs = take(len(comm.out_shapes))
        dk_sums, dv_sums, (stage,), sems = take(parts), take(parts), take(1), take(2)
        comm.bind(ins, outs, refs)
        dk_refs, dv_refs = (dk_ref, stage.at[0, pair]), (dv_ref, stage.at[1, pair])

        def to_core(i, p):
            cols = pl.ds(pl.multiple_of(p * LANES, LANES), LANES)
            return send(stage.at[i, p], landed[i].at[:, cols], sems, (i, p), comm.here.to_core)

        run_beside(comm, point, SELF_PLAN, 0)

    @pl.when(step == 0)
    def _():
        for ref in (*dk_sums, *dv_sums):
            ref[...] = jnp.zeros_like(ref)

    q = q_ref[...]
    do = low(do_ref[...].astype(F32) * scale_ref[...])
    product = do.astype(F32) * o_ref[...].astype(F32)
    q_turned, do_turned = jnp.transpose(q), jnp.transpose(do)
    dqs = []
    for head in range(2):
        rows = slice(head * HEAD, (head + 1) * HEAD)
        doz = only(do, head)
        delta = jnp.sum(only(product, head), axis=1, keepdims=True)
        dq, first = None, 0
        for k_ref, v_ref, dk_sum, dv_sum in zip(k_refs, v_refs, dk_sums, dv_sums):
            count = k_ref.shape[0]
            p = p_ref[head, :, first : first + count]
            first += count
            ds = low(p.astype(F32) * (dot_nt(doz, v_ref[...]) - delta))
            dv_sum[rows, :] += dot(do_turned[rows], p)
            dk_sum[rows, :] += dot(q_turned[rows], ds)
            term = dot(ds, k_ref[...])
            dq = term if dq is None else dq + term
        dqs.append(dq)
    dq_ref[...] = low(jnp.where(lane_is(dqs[0].shape, 0), dqs[0], dqs[1]) * SELF_SCALE)

    @pl.when(step == steps - 1)
    def _():
        for ref, total in zip((*dk_refs, *dv_refs), (*dk_sums, *dv_sums)):
            ref[...] = jnp.transpose(low(total[...]))
        if comm is not None:
            for i in range(2):
                to_core(i, pair).start()

    if comm is not None:
        run_beside(comm, point + 1, SELF_PLAN, 1)

        @pl.when(point == 2 * (PAIRS * steps - 1))
        def _():
            for p in range(PAIRS):
                for i in range(2):
                    to_core(i, p).wait()


def self_backward(q2, do2, o2, scale2, p2, keys, values, comm=None):
    rows = q2.shape[0]
    block = min(rows, 256)
    parts = len(keys)
    whole = lambda array: (array, (array.shape[0], LANES), lambda p, i: (0, p))
    made = lambda array: (array.shape, BF16, (array.shape[0], LANES), lambda p, i: (0, p))
    if comm is None:
        outs, extra = [made(k) for k in keys] + [made(v) for v in values], []
    else:
        outs = [made(keys[0]), made(values[0])] + [((rows, D), BF16, None, None)] * 2
        extra = [pltpu.VMEM((2, PAIRS, rows, LANES), BF16)] + sem_pair(2, PAIRS)
    out = call(
        functools.partial(self_backward_kernel, parts, rows // block, comm),
        (PAIRS, rows // block),
        [
            (q2, (block, LANES), lambda p, i: (i, p)),
            (do2, (block, LANES), lambda p, i: (i, p)),
            (o2, (block, LANES), lambda p, i: (i, p)),
            (scale2, (block, LANES), lambda p, i: (i, p)),
            (p2, (2, block, p2.shape[2]), lambda p, i: (p, i, 0)),
        ]
        + [whole(k) for k in keys]
        + [whole(v) for v in values],
        [((rows, D), BF16, (block, LANES), lambda p, i: (i, p))] + outs,
        [pltpu.VMEM((LANES, k.shape[0]), F32) for k in (*keys, *values)] + extra,
        comm=comm,
        collective_id=1,
    )
    return out[0], out[1 : 1 + len(outs)], out[1 + len(outs) :]


def second_kernel(
    steps, x2_ref, o2_ref, og_ref, gain_ref, wso_ref, wup_ref, wdown_ref,
    out_ref, g3_ref, do_ref, dwup_ref, dwdown_ref, dwso_ref, dgain_ref,
    m_ref, f_ref, dm_ref,
):
    c = pl.program_id(0)

    @pl.when(c == 0)
    def _():
        x3 = x2_ref[...] + dot(o2_ref[...], wso_ref[...])
        unit, _ = normed(x3)
        m_ref[...] = low(unit * gain_ref[4:5, :])
        out_ref[...] = x3
        f_ref[...] = jnp.zeros_like(f_ref)
        dm_ref[...] = jnp.zeros_like(dm_ref)

    m, og = m_ref[...], og_ref[...]
    h, slope = gelu_both(dot(m, wup_ref[...]))
    h = low(h)
    f_ref[...] += dot(h, wdown_ref[...])
    dwdown_ref[...] = low(dot_tn(h, og))
    du = low(slope * dot_nt(og, wdown_ref[...]))
    dwup_ref[...] = low(dot_tn(m, du))
    dm_ref[...] += dot_nt(du, wup_ref[...])

    @pl.when(c == steps - 1)
    def _():
        x3 = out_ref[...]
        unit, factor = normed(x3)
        out_ref[...] = x3 + f_ref[...]
        back, dgain = norm_back(dm_ref[...], unit, factor, gain_ref[4:5, :])
        g3 = og_ref[...].astype(F32) + back
        g3_ref[...] = g3
        dgain_ref[...] = jnp.broadcast_to(dgain, dgain_ref.shape)
        b3 = low(g3)
        o2 = o2_ref[...]
        dwso_ref[...] = low(dot_tn(o2, b3))
        do_ref[...] = low(dot_nt(b3, wso_ref[...]))


def second(x2, o2, og, gains, so, up2, down2):
    rows = x2.shape[0]
    steps = FF // FF_STEP
    r = (rows, D)
    return call(
        functools.partial(second_kernel, steps),
        (steps,),
        [
            (x2, r, flat),
            (o2, r, flat),
            (og, r, flat),
            (gains, (8, D), flat),
            (so, (D, D), flat),
            (up2, (D, FF_STEP), lambda c: (0, c)),
            (down2, (FF_STEP, D), lambda c: (c, 0)),
        ],
        [
            (r, F32, r, flat),
            (r, F32, r, flat),
            (r, BF16, r, flat),
            ((D, FF), BF16, (D, FF_STEP), lambda c: (0, c)),
            ((FF, D), BF16, (FF_STEP, D), lambda c: (c, 0)),
            ((D, D), BF16, (D, D), flat),
            ((8, D), F32, (8, D), flat),
        ],
        [pltpu.VMEM(r, BF16), pltpu.VMEM(r, F32), pltpu.VMEM(r, F32)],
    )


def middle_back_kernel(
    blocks, steps,
    x2_ref, g3_ref, dq_ref, dk_ref, dk_more_ref, dv_ref, dv_more_ref, x1_ref,
    o_ref, gain_ref, wqkv_ref, wout_ref, wup_ref, wdown_ref,
    g1_ref, do_ref, dwqkv_ref, dwup_ref, dwdown_ref, dwout_ref, dgain_s_ref, dgain_m_ref,
    dw_sum, g2_ref, unit_ref, factor_ref, m_ref, b_ref, dm_ref,
):
    step = pl.program_id(0)

    @pl.when(step == 0)
    def _():
        dw_sum[...] = jnp.zeros_like(dw_sum)
        dm_ref[...] = jnp.zeros_like(dm_ref)
        dgain_s_ref[...] = jnp.zeros_like(dgain_s_ref)

    @pl.when(step < blocks)
    def _():
        count = x2_ref.shape[0]
        at = pl.ds(pl.multiple_of(step * count, count), count)
        unit, factor = normed(x2_ref[...])
        gain = gain_ref[3:4, :]
        bn = low(unit * gain)
        dk = low(dk_ref[...].astype(F32) + dk_more_ref[...].astype(F32))
        dv = low(dv_ref[...].astype(F32) + dv_more_ref[...].astype(F32))
        dbn = None
        for i, part in enumerate((dq_ref[...], dk, dv)):
            cols = slice(i * D, (i + 1) * D)
            dw_sum[:, cols] += dot_tn(bn, part)
            term = dot_nt(part, wqkv_ref[:, cols])
            dbn = term if dbn is None else dbn + term
        back, dgain = norm_back(dbn, unit, factor, gain)
        g2 = g3_ref[...] + back
        g2_ref[at] = g2
        b_ref[at] = low(g2)
        dgain_s_ref[...] += jnp.broadcast_to(dgain, dgain_s_ref.shape)
        unit, factor = normed(x1_ref[...])
        unit_ref[at] = unit
        factor_ref[at] = jnp.broadcast_to(factor, (count, LANES))
        m_ref[at] = low(unit * gain_ref[2:3, :])

    @pl.when(step >= blocks)
    def _():
        m, b = m_ref[...], b_ref[...]
        h, slope = gelu_both(dot(m, wup_ref[...]))
        dwdown_ref[...] = low(dot_tn(low(h), b))
        du = low(slope * dot_nt(b, wdown_ref[...]))
        dwup_ref[...] = low(dot_tn(m, du))
        dm_ref[...] += dot_nt(du, wup_ref[...])

    @pl.when(step == blocks + steps - 1)
    def _():
        dwqkv_ref[...] = low(dw_sum[...])
        back, dgain = norm_back(dm_ref[...], unit_ref[...], factor_ref[:, 0:1], gain_ref[2:3, :])
        g1 = g2_ref[...] + back
        g1_ref[...] = g1
        dgain_m_ref[...] = jnp.broadcast_to(dgain, dgain_m_ref.shape)
        b1 = low(g1)
        dwout_ref[...] = low(dot_tn(o_ref[...], b1))
        do_ref[...] = low(dot_nt(b1, wout_ref[...]))


def middle_back(x2, g3, dq, dk, dk_more, dv, dv_more, x1, o, gains, qkv, mix, up1, down1):
    rows = x1.shape[0]
    block = min(rows, 512)
    blocks, steps = rows // block, FF // FF_STEP
    r = (rows, D)
    row_block = lambda s: (jnp.minimum(s, blocks - 1), 0)
    part = lambda s: jnp.maximum(s - blocks, 0)
    return call(
        functools.partial(middle_back_kernel, blocks, steps),
        (blocks + steps,),
        [(a, (block, D), row_block) for a in (x2, g3, dq, dk, dk_more, dv, dv_more, x1)]
        + [
            (o, r, flat),
            (gains, (8, D), flat),
            (qkv, (D, 3 * D), flat),
            (mix, (D, D), column(3)),
            (up1, (D, FF_STEP), lambda s: (0, part(s))),
            (down1, (FF_STEP, D), lambda s: (part(s), 0)),
        ],
        [
            (r, F32, r, flat),
            (r, BF16, r, flat),
            ((D, 3 * D), BF16, (D, 3 * D), flat),
            ((D, FF), BF16, (D, FF_STEP), lambda s: (0, part(s))),
            ((FF, D), BF16, (FF_STEP, D), lambda s: (part(s), 0)),
            ((D, D), BF16, (D, D), flat),
            ((8, D), F32, (8, D), flat),
            ((8, D), F32, (8, D), flat),
        ],
        [
            pltpu.VMEM((D, 3 * D), F32),
            pltpu.VMEM(r, F32),
            pltpu.VMEM(r, F32),
            pltpu.VMEM((rows, LANES), F32),
            pltpu.VMEM(r, BF16),
            pltpu.VMEM(r, BF16),
            pltpu.VMEM(r, F32),
        ],
    )


def cross_back_kernel(
    steps, lat_ref, g1_ref, do_ref, p_ref, q_ref, kv_ref, gain_ref, wq_ref,
    lg_ref, dwq_ref, dkv_ref, dgain_ref, dk_sum, dv_sum, dwq_sum,
):
    i = pl.program_id(0)

    @pl.when(i == 0)
    def _():
        for ref in (dk_sum, dv_sum, dwq_sum, dgain_ref):
            ref[...] = jnp.zeros_like(ref)

    p, do, q = p_ref[...], do_ref[...], q_ref[...]
    dp = dot_nt(do, kv_ref[:, D:])
    wide_p = p.astype(F32)
    ds = low(wide_p * (dp - jnp.sum(wide_p * dp, axis=1, keepdims=True)))
    dq = low(dot(ds, kv_ref[:, :D]) * CROSS_SCALE)
    dk_sum[...] += dot_tn(ds, q)
    dv_sum[...] += dot_tn(p, do)
    unit, factor = normed(lat_ref[...].astype(F32))
    gain = gain_ref[0:1, :]
    dwq_sum[...] += dot_tn(low(unit * gain), dq)
    back, dgain = norm_back(dot_nt(dq, wq_ref[...]), unit, factor, gain)
    lg_ref[...] = g1_ref[...] + back
    dgain_ref[...] += jnp.broadcast_to(dgain, dgain_ref.shape)

    @pl.when(i == steps - 1)
    def _():
        dwq_ref[...] = low(dwq_sum[...])
        dkv_ref[:, :D] = low(dk_sum[...] * CROSS_SCALE)
        dkv_ref[:, D:] = low(dv_sum[...])


def cross_back(latents, g1, do, p, q, kv, gains, mix):
    rows, span = p.shape
    block = min(rows, 512)
    r = (block, D)
    return call(
        functools.partial(cross_back_kernel, rows // block),
        (rows // block,),
        [
            (latents, r, rows_of),
            (g1, r, rows_of),
            (do, r, rows_of),
            (p, (block, span), rows_of),
            (q, r, rows_of),
            (kv, (span, 2 * D), flat),
            (gains, (8, D), flat),
            (mix, (D, D), column(2)),
        ],
        [
            ((rows, D), F32, r, rows_of),
            ((D, D), BF16, (D, D), flat),
            ((span, 2 * D), BF16, (span, 2 * D), flat),
            ((8, D), F32, (8, D), flat),
        ],
        [pltpu.VMEM((span, D), F32), pltpu.VMEM((span, D), F32), pltpu.VMEM((D, D), F32)],
    )


def token_back_kernel(tok_ref, dkv_ref, more_ref, gain_ref, w_ref, tg_ref, dw_ref, dgain_ref):
    unit, factor = normed(tok_ref[...].astype(F32))
    gain = gain_ref[1:2, :]
    dkv = low(dkv_ref[...].astype(F32) + more_ref[...].astype(F32))
    dw_ref[...] = low(dot_tn(low(unit * gain), dkv))
    back, dgain = norm_back(dot_nt(dkv, w_ref[...]), unit, factor, gain)
    tg_ref[...] = low(back)
    dgain_ref[...] = jnp.broadcast_to(dgain, dgain_ref.shape)


def token_back(tokens, dkv, more, gains, mix):
    rows = tokens.shape[0]
    return call(
        token_back_kernel,
        (1,),
        [
            (tokens, (rows, D), flat),
            (dkv, (rows, 2 * D), flat),
            (more, (rows, 2 * D), flat),
            (gains, (8, D), flat),
            (mix, (D, 2 * D), column(0)),
        ],
        [
            ((rows, D), BF16, (rows, D), flat),
            ((D, 2 * D), BF16, (D, 2 * D), flat),
            ((8, D), F32, (8, D), flat),
        ],
    )


MESH = pl.DeviceIdType.MESH
UP, DOWN = 0, 1


class Place:
    def __init__(self):
        row, lat = lax.axis_index("row"), lax.axis_index("lat")
        self.x, self.y, self.z, self.c = row % 2, row // 2, lat // 2, lat % 2
        self.r = row
        self.rx = self.y * 2 + 1 - self.x
        self.ry = (1 - self.y) * 2 + self.x
        self.rd = (1 - self.y) * 2 + 1 - self.x
        self.to_x, self.to_y = (self.rx, lat), (self.ry, lat)
        self.to_core = (row, self.z * 2 + 1 - self.c)
        self.to_z = ((row, lat + 2), (row, lat - 2))
        self.more = (self.z < 3, self.z > 0)

    def greet(self):
        barrier = pltpu.get_barrier_semaphore()
        for device in (self.to_x, self.to_y, self.to_core):
            pl.semaphore_signal(barrier, inc=1, device_id=device, device_id_type=MESH)
        for way in (UP, DOWN):
            @pl.when(self.more[way])
            def _():
                pl.semaphore_signal(barrier, inc=1, device_id=self.to_z[way], device_id_type=MESH)
        pl.semaphore_wait(barrier, 3 + jnp.minimum(self.z, 1) + jnp.minimum(3 - self.z, 1))

    def source(self, way, hop):
        return (self.z - hop, self.z >= hop) if way == UP else (self.z + hop, self.z + hop <= 3)


def send(src, dst, sems, index, device):
    return pltpu.make_async_remote_copy(
        src_ref=src, dst_ref=dst, send_sem=sems[0].at[index], recv_sem=sems[1].at[index],
        device_id=device, device_id_type=MESH,
    )


def sem_pair(*shape):
    return [pltpu.SemaphoreType.DMA(shape), pltpu.SemaphoreType.DMA(shape)]


TOKEN_PARTS = 4
AHEAD = 3
GAP = 2
SHIFT = 3
WEIGHT, TOKENS, NOTES = range(3)


class Gather:
    def __init__(self, weights, tokens=None, notes=()):
        self.inputs, self.out_shapes, self.chunks = [], [], []
        self.shards = []
        for shards in weights:
            shape = (4, shards[0].shape[0] // 4)
            self.shards.append([])
            for shard in shards:
                self.shards[-1].append((len(self.inputs), shard.shape[1]))
                self.inputs.append(shard.reshape(shape + shard.shape[1:]))
            cols = sum(shard.shape[1] for shard in shards)
            self.out_shapes.append(jax.ShapeDtypeStruct((4, 2) + shape + (cols,), BF16))
        self.chunks = [(WEIGHT, k) for k in range(len(weights))]
        self.out_specs = [ANYWHERE] * len(weights)
        self.copies = len(self.inputs)
        self.scratch = []
        self.noted = len(notes)
        if tokens is not None:
            self.inputs += [tokens, *notes]
            self.out_shapes += [
                jax.ShapeDtypeStruct((4, 2) + tokens.shape, BF16),
                jax.ShapeDtypeStruct((8, tokens.shape[0]), BF16),
                jax.ShapeDtypeStruct((8, D), F32),
            ]
            self.out_specs += [ANYWHERE] + [inside(made.shape) for made in self.out_shapes[-2:]]
            self.chunks = [(NOTES, 0)] + self.chunks + [(TOKENS, k) for k in range(TOKEN_PARTS)]
            self.scratch.append(pltpu.VMEM((4, 2, 16, tokens.shape[0]), BF16))
            self.copies += 1
        self.in_specs = [inside(array.shape) for array in self.inputs]
        n = len(self.chunks)
        self.scratch += [pltpu.SemaphoreType.DMA((self.copies,))]
        for shape in ((n, 2, 3), (n, 2, 3, 2), (n, 2, 3, 2), (n, 7)):
            self.scratch += sem_pair(*shape)
        self.steps = n + 4 * GAP + 1

    def bind(self, ins, outs, scratch):
        self.here, self.ins, self.outs = Place(), ins, outs
        scratch = list(scratch)
        take = lambda n: [scratch.pop(0) for _ in range(n)]
        if self.noted:
            self.notes = take(1)[0]
        self.local = take(1)[0]
        self.z_sems, self.p_sems, self.q_sems, self.c_sems = (take(2) for _ in range(4))

    def block(self, k, source, core=None):
        kind, index = self.chunks[k]
        core = self.here.c if core is None else core
        if kind == NOTES:
            return self.notes.at[source, core]
        if kind == TOKENS:
            tokens = self.outs[len(self.shards)]
            rows = tokens.shape[2] // TOKEN_PARTS
            return tokens.at[source, core, pl.ds(index * rows, rows)]
        return self.outs[index].at[source, core]

    def piece(self, k, source, quarter, half=None):
        if not self.shared(k):
            return self.block(k, source)
        ref = self.outs[self.chunks[k][1]]
        if half is None:
            return ref.at[source, self.here.c, quarter]
        width = ref.shape[-1] // 2
        return ref.at[source, self.here.c, quarter, :, pl.ds(half * width, width)]

    def shared(self, k):
        return self.chunks[k][0] == WEIGHT

    def z_send(self, k, way, hop):
        source, _ = self.here.source(way, hop - 1)
        ref = self.piece(k, source, self.here.r)
        return send(ref, ref, self.z_sems, (k, way, hop - 1), self.here.to_z[way])

    def z_recv(self, k, way, hop):
        source, _ = self.here.source(way, hop)
        ref = self.piece(k, source, self.here.r)
        return send(ref, ref, self.z_sems, (k, way, hop - 1), self.here.to_z[way])

    def p_copy(self, k, way, hop, axis, mine):
        here = self.here
        source, _ = here.source(way, hop)
        ref = self.piece(k, source, here.r if mine else (here.rx, here.ry)[axis])
        return send(ref, ref, self.p_sems, (k, way, hop - 1, axis), (here.to_x, here.to_y)[axis])

    def q_copy(self, k, way, hop, half, mine):
        here = self.here
        source, _ = here.source(way, hop)
        ref = self.piece(k, source, (here.rx, here.ry)[half] if mine else here.rd, half)
        return send(ref, ref, self.q_sems, (k, way, hop - 1, half), (here.to_y, here.to_x)[half])

    def c_copy(self, k, source, index, mine):
        ref = self.block(k, source, self.here.c if mine else 1 - self.here.c)
        return send(ref, ref, self.c_sems, (k, index), self.here.to_core)

    def ways(self, hop, fn):
        for way in (UP, DOWN):
            source, valid = self.here.source(way, hop)
            pl.when(valid)(functools.partial(fn, way, hop, source))

    @staticmethod
    def index_of(way, hop):
        return 1 + way * 3 + hop - 1

    def first_sends(self, k):
        for way in (UP, DOWN):
            pl.when(self.here.more[way])(lambda way=way: self.z_send(k, way, 1).start())
        self.c_copy(k, self.here.z, 0, True).start()

    def stage_z(self, k, hop):
        def arrive(way, hop, source):
            self.z_recv(k, way, hop).wait_recv()
            if hop < 3:
                pl.when(self.here.more[way])(lambda: self.z_send(k, way, hop + 1).start())
            if self.shared(k):
                self.p_copy(k, way, hop, 0, True).start()
                self.p_copy(k, way, hop, 1, True).start()
            else:
                self.c_copy(k, source, self.index_of(way, hop), True).start()
        self.ways(hop, arrive)

    def stage_p(self, k, hop):
        def arrive(way, hop, source):
            for axis in (0, 1):
                self.p_copy(k, way, hop, axis, False).wait_recv()
                self.q_copy(k, way, hop, axis, True).start()
        self.ways(hop, arrive)

    def stage_q(self, k, hop):
        def arrive(way, hop, source):
            self.q_copy(k, way, hop, 0, False).wait_recv()
            self.q_copy(k, way, hop, 1, False).wait_recv()
            self.c_copy(k, source, self.index_of(way, hop), True).start()
        self.ways(hop, arrive)

    def local_copies(self):
        z, c = self.here.z, self.here.c
        copies = []
        for k, shards in enumerate(self.shards):
            first = 0
            for index, width in shards:
                copies.append(pltpu.make_async_copy(
                    self.ins[index], self.outs[k].at[z, c, :, :, pl.ds(first, width)],
                    self.local.at[len(copies)]))
                first += width
        if self.noted:
            copies.append(pltpu.make_async_copy(
                self.ins[len(copies)], self.outs[len(self.shards)].at[z, c], self.local.at[len(copies)]))
        return copies

    def begin(self):
        for copy in self.local_copies():
            copy.start()
        if self.noted:
            z, c = self.here.z, self.here.c
            scenes, mask, *gains = self.ins[self.copies :]
            self.notes[z, c] = jnp.zeros(self.notes.shape[2:], BF16)
            self.notes[z, c, 0:1, :] = low(jnp.where(mask[...] == 1, scenes[...], -1).astype(F32))
            for i, gain in enumerate(gains):
                self.notes[z, c, 1 + i : 2 + i, : gain.shape[1]] = gain[...]

    def begin_sends(self):
        for copy in self.local_copies():
            copy.wait()
        for k in range(min(AHEAD, len(self.chunks))):
            self.first_sends(k)

    def step(self, step):
        total = len(self.chunks)
        if step + AHEAD < total:
            self.first_sends(step + AHEAD)
        for lag, stage in ((0, self.stage_z), (GAP, self.stage_p), (2 * GAP, self.stage_q)):
            for hop in (1, 2, 3):
                k = step - lag - GAP * (hop - 1)
                if 0 <= k < total and (lag == 0 or self.shared(k)):
                    stage(k, hop)

    def finish(self):
        here = self.here
        for k in range(len(self.chunks)):
            for way in (UP, DOWN):
                for hop in (1, 2, 3):
                    _, valid = here.source(way, hop - 1)
                    pl.when(valid & here.more[way])(
                        lambda k=k, way=way, hop=hop: self.z_send(k, way, hop).wait_send())
            self.c_copy(k, here.z, 0, True).wait_send()
            self.c_copy(k, here.z, 0, False).wait_recv()

            def settle(way, hop, source):
                self.c_copy(k, source, self.index_of(way, hop), True).wait_send()
                self.c_copy(k, source, self.index_of(way, hop), False).wait_recv()
                if self.shared(k):
                    for axis in (0, 1):
                        self.p_copy(k, way, hop, axis, True).wait_send()
                        self.q_copy(k, way, hop, axis, True).wait_send()
            for hop in (1, 2, 3):
                self.ways(hop, settle)
        if self.noted:
            tags, gains = self.outs[-2:]
            width = D // 8
            gains[...] = jnp.zeros_like(gains)
            for i in range(8):
                tags[i : i + 1, :] = self.notes[i // 2, i % 2, 0:1, :]
                for j in range(5):
                    gains[j : j + 1, i * width : (i + 1) * width] = self.notes[
                        i // 2, i % 2, 1 + j : 2 + j, :width
                    ].astype(F32)


def gather_kernel(comm, *refs):
    n_in, n_out = len(comm.inputs), len(comm.out_shapes)
    comm.bind(refs[:n_in], refs[n_in : n_in + n_out], refs[n_in + n_out :])
    comm.here.greet()
    comm.begin()
    comm.begin_sends()
    for step in range(comm.steps):
        comm.step(step)
    comm.finish()


def gather_now(comm):
    return call(functools.partial(gather_kernel, comm), (1,), [], [], comm=comm, collective_id=0)


class Peers(Place):
    def __init__(self):
        super().__init__()
        lat = lax.axis_index("lat")
        self.plane = (self.to_x, self.to_y, (self.rd, lat))
        self.quarters = (self.rx, self.ry, self.rd)
        self.above = [lax.rem(self.z + 1 + i, 4) for i in range(3)]
        self.line = [(self.r, z * 2 + self.c) for z in self.above]

    def greet(self):
        barrier = pltpu.get_barrier_semaphore()
        others = (self.to_core, *self.plane, *self.line)
        for device in others:
            pl.semaphore_signal(barrier, inc=1, device_id=device, device_id_type=MESH)
        pl.semaphore_wait(barrier, len(others))


LINE = (
    ((1, UP, 3), (2, DOWN, 0)),
    ((1, UP, 2), (2, DOWN, 1), (2, UP, 3), (1, DOWN, 0)),
    ((1, UP, 1), (2, DOWN, 2), (2, UP, 2), (1, DOWN, 1)),
    ((3, UP, 3), (0, DOWN, 0)),
)


class LineSum:
    def __init__(self, here, block, arrived, sems):
        self.here, self.block, self.arrived, self.sems = here, block, arrived, sems

    def copy(self, way, dest):
        index = (way, dest - 1 if way == UP else dest)
        return send(self.block(dest), self.arrived.at[index], self.sems, index, self.here.to_z[way])

    def start(self):
        @pl.when(self.here.z == 0)
        def _():
            for dest in (3, 2, 1):
                self.copy(UP, dest).start()

        @pl.when(self.here.z == 3)
        def _():
            for dest in (0, 1, 2):
                self.copy(DOWN, dest).start()

    def turn(self, group):
        for device, way, dest in LINE[group]:
            @pl.when(self.here.z == device)
            def _(device=device, way=way, dest=dest):
                self.copy(way, dest).wait_recv()
                ref = self.block(dest)
                ref[...] = ref[...] + self.arrived[way, dest - 1 if way == UP else dest]
                if dest != device:
                    self.copy(way, dest).start()

    def finish(self):
        for dest in (1, 2, 3):
            pl.when(self.here.z < dest)(lambda dest=dest: self.copy(UP, dest).wait_send())
        for dest in (0, 1, 2):
            pl.when(self.here.z > dest)(lambda dest=dest: self.copy(DOWN, dest).wait_send())


class DirectSum(LineSum):
    def copy(self, i):
        return send(self.block(self.here.above[i]), self.arrived.at[0, i], self.sems, (0, i), self.here.line[i])

    def start(self):
        for i in range(3):
            self.copy(i).start()

    def turn(self, group):
        if group == len(LINE) - 1:
            for i in range(3):
                self.copy(i).wait()
            ref, arrived = self.block(self.here.z), self.arrived
            total = ref[...].astype(F32) + arrived[0, 0].astype(F32)
            ref[...] = low(total + arrived[0, 1].astype(F32) + arrived[0, 2].astype(F32))

    def finish(self):
        pass


class Staged:
    def __init__(self, rows, cols):
        self.shape = (rows, cols)


class WeightSum:
    def __init__(self, chunks, gains=None, tokens=None, direct=()):
        self.direct = direct
        self.chunks, self.inputs, self.scratch, self.staged = [], [], [], []
        self.sources = 0
        for chunk in chunks:
            parts = []
            for array in chunk:
                shape = (4, 2, 4, array.shape[0] // 32, array.shape[1])
                if isinstance(array, Staged):
                    parts.append((self.sources, None, len(self.staged), shape[-1]))
                    self.staged.append(pltpu.VMEM(shape, BF16))
                else:
                    parts.append((self.sources, len(self.inputs), None, shape[-1]))
                    self.inputs.append(array.reshape(shape))
                self.sources += 1
            self.chunks.append((parts, shape[3], sum(part[3] for part in parts)))
        self.out_shapes = [
            jax.ShapeDtypeStruct((4, rows, cols), BF16) for _, rows, cols in self.chunks
        ]
        for _, rows, cols in self.chunks:
            half = cols // 2
            self.scratch += [
                pltpu.VMEM((4, 2, 2, rows, cols), BF16),
                pltpu.VMEM((4, 2, 2, rows, cols), BF16),
                pltpu.VMEM((2, 4, 2, rows, half), BF16),
                pltpu.VMEM((2, 4, rows, half), BF16),
                pltpu.VMEM((2, 3, rows, cols), BF16),
                pltpu.VMEM((4, rows, cols), BF16),
            ]
        n = len(self.chunks)
        self.scratch += self.staged
        self.scratch += [pltpu.SemaphoreType.DMA((self.sources, 2))]
        for shape in ((self.sources, 2), (n, 2), (n, 2), (n, 2, 3), (n, 3)):
            self.scratch += sem_pair(*shape)
        self.gains, self.tokens = gains, tokens
        if gains is not None:
            self.out_shapes.append(jax.ShapeDtypeStruct(gains, F32))
            self.scratch += [pltpu.VMEM(shape + gains, F32) for shape in ((), (), (4,), (3,))]
            self.scratch += sem_pair(1) + sem_pair(3) + sem_pair(3)
        if tokens is not None:
            self.out_shapes.append(jax.ShapeDtypeStruct((tokens // 8, D), BF16))
            self.scratch += [pltpu.VMEM((4, tokens // 8, D), BF16)]
            self.scratch += [pltpu.VMEM((2, tokens // 8, D), BF16)]
            self.scratch += [pltpu.VMEM((2, 3, tokens // 8, D), BF16)]
            self.scratch += sem_pair(1) + sem_pair(2, 3)
        self.in_specs = [ANYWHERE] * len(self.inputs)
        self.out_specs = [inside(made.shape) for made in self.out_shapes]

    def bind(self, ins, outs, scratch):
        self.here = Peers()
        self.ins, self.outs = ins, outs
        scratch = list(scratch)
        take = lambda n: [scratch.pop(0) for _ in range(n)]
        self.buffers = [take(6) for _ in self.chunks]
        self.stages = take(len(self.staged))
        self.local = take(1)[0]
        self.c_sems, self.x_sems, self.y_sems, self.z_sems, self.g_sems = (take(2) for _ in range(5))
        if self.gains is not None:
            self.gain_buffers = take(4)
            self.gain_sems = [take(2) for _ in range(3)]
        if self.tokens is not None:
            self.token_mine, self.token_window, arrived = take(3)
            self.token_sems = take(2)
            self.token_line = LineSum(self.here, lambda z: self.token_mine.at[z], arrived, take(2))


    def parts(self, k):
        first = 0
        for source, given, staged, width in self.chunks[k][0]:
            ref = self.stages[staged] if given is None else self.ins[given]
            yield source, ref, pl.ds(first, width)
            first += width

    def halves(self, k):
        half = self.chunks[k][2] // 2
        return pl.ds(0, half), pl.ds(half, half)

    def own(self, k):
        for source, ref, cols in self.parts(k):
            for y in range(2):
                yield pltpu.make_async_copy(
                    ref.at[:, self.here.c, pl.ds(2 * y, 2)],
                    self.buffers[k][0].at[:, y, :, :, cols],
                    self.local.at[source, y],
                )

    def to_core(self, k):
        for source, ref, cols in self.parts(k):
            for y in range(2):
                yield send(
                    ref.at[:, 1 - self.here.c, pl.ds(2 * y, 2)],
                    self.buffers[k][1].at[:, y, :, :, cols],
                    self.c_sems, (source, y), self.here.to_core,
                )

    def first_turn(self, k):
        mine, theirs, here = self.buffers[k][0], self.buffers[k][2], self.here
        left, right = self.halves(k)
        yield send(mine.at[:, :, 1 - here.x, :, left], theirs.at[0], self.x_sems, (k, 0), here.to_x)
        yield send(mine.at[:, 1 - here.y, :, :, right], theirs.at[1], self.x_sems, (k, 1), here.to_y)

    def second_turn(self, k):
        mine, theirs, here = self.buffers[k][0], self.buffers[k][3], self.here
        left, right = self.halves(k)
        yield send(mine.at[:, 1 - here.y, here.x, :, left], theirs.at[0], self.y_sems, (k, 0), here.to_y)
        yield send(mine.at[:, here.y, 1 - here.x, :, right], theirs.at[1], self.y_sems, (k, 1), here.to_x)

    def line(self, k):
        here, buffers = self.here, self.buffers[k]
        sems = [sem.at[k] for sem in self.z_sems]
        kind = DirectSum if k in self.direct else LineSum
        return kind(here, lambda z: buffers[0].at[z, here.y, here.x], buffers[4], sems)

    def finished(self, k):
        for i in range(3):
            mine = self.buffers[k][5].at[self.here.r]
            yield send(mine, mine, self.g_sems, (k, i), self.here.plane[i])

    def arriving(self, k):
        for i in range(3):
            theirs = self.buffers[k][5].at[self.here.quarters[i]]
            yield send(theirs, theirs, self.g_sems, (k, i), self.here.plane[i])


    def start(self, k):
        for copy in (*self.own(k), *self.to_core(k)):
            copy.start()

    def in_chip(self, k):
        for copy in self.own(k):
            copy.wait()
        for copy in self.to_core(k):
            copy.wait_recv()
        mine, theirs = self.buffers[k][:2]
        for z in range(4):
            for y in range(2):
                for x in range(2):
                    mine[z, y, x] = mine[z, y, x] + theirs[z, y, x]
        for copy in self.first_turn(k):
            copy.start()

    def in_pairs(self, k):
        for copy in self.first_turn(k):
            copy.wait()
        mine, theirs, here = self.buffers[k][0], self.buffers[k][2], self.here
        left, right = self.halves(k)
        for z in range(4):
            for i in range(2):
                mine[z, i, here.x, :, left] = mine[z, i, here.x, :, left] + theirs[0, z, i]
                mine[z, here.y, i, :, right] = mine[z, here.y, i, :, right] + theirs[1, z, i]
        for copy in self.second_turn(k):
            copy.start()

    def in_plane(self, k):
        for copy in self.second_turn(k):
            copy.wait()
        mine, theirs, here = self.buffers[k][0], self.buffers[k][3], self.here
        for z in range(4):
            for i, cols in enumerate(self.halves(k)):
                mine[z, here.y, here.x, :, cols] = mine[z, here.y, here.x, :, cols] + theirs[i, z]
        self.line(k).start()

    def turn0(self, k):
        self.line(k).turn(0)

    def turn1(self, k):
        self.line(k).turn(1)

    def turn2(self, k):
        self.line(k).turn(2)

    def in_line(self, k):
        self.line(k).turn(3)
        mine, done, here = self.buffers[k][0], self.buffers[k][5], self.here
        done[here.r] = mine[here.z, here.y, here.x]
        for copy in self.finished(k):
            copy.start()

    def end(self, k):
        for copy in self.arriving(k):
            copy.wait_recv()
        for copy in (*self.to_core(k), *self.finished(k)):
            copy.wait_send()
        self.line(k).finish()
        self.outs[k][...] = self.buffers[k][5][...]


    def gain_copy(self, stage, i):
        mine, core, plane, line = self.gain_buffers
        if stage == 0:
            return send(mine, core, self.gain_sems[0], 0, self.here.to_core)
        if stage == 1:
            return send(mine, plane.at[self.here.r], self.gain_sems[1], i, self.here.plane[i])
        return send(mine, line.at[i], self.gain_sems[2], i, self.here.line[i])

    def gain_plane_recv(self, i):
        mine, _, plane, _ = self.gain_buffers
        return send(mine, plane.at[self.here.quarters[i]], self.gain_sems[1], i, self.here.plane[i])

    def gain_step(self, stage):
        mine, core, plane, line = self.gain_buffers
        if stage == 0:
            self.gain_copy(0, 0).start()
        elif stage == 1:
            self.gain_copy(0, 0).wait()
            mine[...] += core[...]
            plane[self.here.r] = mine[...]
            for i in range(3):
                self.gain_copy(1, i).start()
        elif stage == 2:
            for i in range(3):
                self.gain_copy(1, i).wait_send()
                self.gain_plane_recv(i).wait_recv()
            mine[...] = (plane[0] + plane[1]) + (plane[2] + plane[3])
            for i in range(3):
                self.gain_copy(2, i).start()
        else:
            for i in range(3):
                self.gain_copy(2, i).wait()
            self.outs[len(self.chunks)][...] = (mine[...] + line[0]) + (line[1] + line[2])


    def token_core(self):
        mine = self.token_window.at[self.here.c]
        return send(mine, mine, self.token_sems, 0, self.here.to_core)

    def token_core_recv(self):
        theirs = self.token_window.at[1 - self.here.c]
        return send(theirs, theirs, self.token_sems, 0, self.here.to_core)

    def token_place(self, start):
        self.token_core().wait_send()
        self.token_core_recv().wait_recv()
        count, rows = 2 * self.token_window.shape[1], self.token_mine.shape[1]
        window = self.token_window[...].reshape(count, D)
        for z in range(4):
            slot = lax.broadcasted_iota(jnp.int32, (rows, count), 0) + (2 * z + self.here.c) * rows
            row = lax.broadcasted_iota(jnp.int32, (rows, count), 1) + start
            self.token_mine[z] = low(dot(low(jnp.where(slot == row, 1.0, 0.0)), window))
        self.token_line.start()

    def token_end(self):
        self.token_line.turn(3)
        self.outs[-1][...] = self.token_mine[self.here.z]
        self.token_line.finish()


def tail_kernel(
    comm, lat_ref, do_ref, p_ref, q_ref, kv_ref, gain_ref, wq_ref, wkv_ref, win_ref, start_ref,
    dm1_ref, ds_ref, dm2_ref, *refs,
):
    n_in, n_out = len(comm.inputs), len(comm.out_shapes)
    ins, lg_ref = refs[:n_in], refs[n_in]
    outs, scratch = refs[n_in + 1 : n_in + 1 + n_out], refs[n_in + 1 + n_out :]
    kv_sum, dkv_ref, more_ref, kv_sems = scratch[0], scratch[1], scratch[2], scratch[3:5]
    comm.bind(ins, outs, scratch[5:])
    here = comm.here
    mixed = len(comm.chunks) - 2
    early, last = range(mixed), mixed + 1
    rows, span = p_ref.shape
    gains = comm.gain_buffers[0]

    here.greet()
    for k in early:
        comm.start(k)
    block = rows // 2
    dwq = None
    gains[...] = jnp.zeros_like(gains)
    for i in range(2):
        at = slice(i * block, (i + 1) * block)
        p, do, q = p_ref[at], do_ref[at], q_ref[at]
        dp = dot_nt(do, kv_ref[:, D:])
        wide_p = p.astype(F32)
        ds = low(wide_p * (dp - jnp.sum(wide_p * dp, axis=1, keepdims=True)))
        dq = low(dot(ds, kv_ref[:, :D]) * CROSS_SCALE)
        dk, dv = dot_tn(ds, q), dot_tn(p, do)
        if i == 0:
            kv_sum[:, :D], kv_sum[:, D:] = dk, dv
        else:
            dkv_ref[:, :D] = low((kv_sum[:, :D] + dk) * CROSS_SCALE)
            dkv_ref[:, D:] = low(kv_sum[:, D:] + dv)
        unit, factor = normed(lat_ref[at].astype(F32))
        gain = gain_ref[0:1, :]
        term = dot_tn(low(unit * gain), dq)
        dwq = term if dwq is None else dwq + term
        back, dgain = norm_back(dot_nt(dq, wq_ref[...]), unit, factor, gain)
        lg_ref[at] = low(back)
        gains[0:1] += dgain
        if i < mixed:
            comm.in_chip(i)
    for k in range(2, mixed):
        comm.in_chip(k)
    half = span // 2
    to_core = send(
        dkv_ref.at[pl.ds(half * (1 - here.c), half)], more_ref, kv_sems, 0, here.to_core)
    to_core.start()
    comm.stages[0][...] = low(dwq).reshape(comm.stages[0].shape)
    comm.start(mixed)
    gains[2:3], gains[3:4], gains[4:5] = dm1_ref[0:1], ds_ref[0:1], dm2_ref[0:1]
    unit, factor = normed(win_ref[pl.ds(half * here.c, half)].astype(F32))
    gain = gain_ref[1:2, :]
    to_core.wait()
    dkv = low(dkv_ref[pl.ds(half * here.c, half)].astype(F32) + more_ref[...].astype(F32))
    back, dgain = norm_back(dot_nt(dkv, wkv_ref[...]), unit, factor, gain)
    comm.token_window[here.c] = low(back)
    comm.token_core().start()
    gains[1:2] = dgain
    comm.gain_step(0)
    comm.stages[1][...] = low(dot_tn(low(unit * gain), dkv)).reshape(comm.stages[1].shape)
    comm.start(last)
    comm.token_place(start_ref[0:1, 0:1])
    comm.in_chip(mixed)
    comm.in_pairs(0)
    comm.in_pairs(1)
    comm.gain_step(1)
    comm.in_chip(last)
    comm.token_line.turn(0)
    comm.in_pairs(2)
    comm.in_plane(0)
    comm.in_pairs(mixed)
    comm.in_plane(1)
    comm.token_line.turn(1)
    comm.in_pairs(last)
    for k in (0, 1):
        comm.turn0(k)
    comm.in_plane(2)
    comm.gain_step(2)
    for k in (0, 1):
        comm.turn1(k)
    comm.in_plane(mixed)
    comm.token_line.turn(2)
    comm.in_plane(last)
    for k in (0, 1):
        comm.turn2(k)
    for k in (2, mixed):
        comm.turn0(k)
    for k in (0, 1):
        comm.in_line(k)
    for k in (2, mixed):
        comm.turn1(k)
    comm.gain_step(3)
    for k in (2, mixed):
        comm.turn2(k)
    comm.in_line(last)
    comm.token_end()
    for k in (2, mixed):
        comm.in_line(k)
    for k in range(last + 1):
        comm.end(k)


def tail(comm, latents, do, p, q, kv, gains, mix, window, start, dgains):
    rows, span = p.shape
    r = (rows, D)
    return call(
        functools.partial(tail_kernel, comm),
        (1,),
        [
            (latents, r, flat),
            (do, r, flat),
            (p, p.shape, flat),
            (q, r, flat),
            (kv, kv.shape, flat),
            (gains, (8, D), flat),
            (mix, (D, D), column(2)),
            (mix, (D, 2 * D), column(0)),
            (window, (span, D), flat),
            (start, start.shape, flat),
        ]
        + [(g, (8, D), flat) for g in dgains],
        [(r, BF16, r, flat)],
        [
            pltpu.VMEM((span, 2 * D), F32),
            pltpu.VMEM((span, 2 * D), BF16),
            pltpu.VMEM((span // 2, 2 * D), BF16),
        ]
        + sem_pair(1),
        comm=comm,
        collective_id=2,
    )


def widen_kernel(cuts, base_ref, term_ref, *refs):
    sources, (sum_ref, *targets) = refs[: len(cuts)], refs[len(cuts) :]
    sum_ref[...] = base_ref[...] + term_ref[...].astype(F32)
    for source, widths in zip(sources, cuts):
        first = 0
        for width in widths:
            targets.pop(0)[...] = source[:, first : first + width].astype(F32)
            first += width


def widen(base, term, arrays, cuts):
    steps = 4
    rows = lambda array: array.shape[0] // steps
    return call(
        functools.partial(widen_kernel, cuts),
        (steps,),
        [(a, (rows(a), a.shape[1]), rows_of) for a in (base, term, *arrays)],
        [(base.shape, F32, (rows(base), base.shape[1]), rows_of)]
        + [
            ((a.shape[0], width), F32, (rows(a), width), rows_of)
            for a, widths in zip(arrays, cuts)
            for width in widths
        ],
    )


def from_partner(shard, bit):
    return lax.ppermute(shard, "lat", [(i, i ^ 1 << bit) for i in range(lax.axis_size("lat"))])


def gather_lat(shard):
    return lax.all_gather(shard, "lat", axis=0, tiled=True)


def halve(value, place, bits):
    kept, more = value, jnp.zeros_like(value)
    for bit in reversed(range(bits)):
        value = low(kept.astype(F32) + more.astype(F32))
        half = value.shape[0] // 2
        upper = place // 2**bit % 2
        kept = lax.dynamic_slice_in_dim(value, upper * half, half)
        more = from_partner(lax.dynamic_slice_in_dim(value, (1 - upper) * half, half), bit)
    return kept, more


def reduce_weights(grad):
    share = lax.psum_scatter(grad, "lat", scatter_dimension=0, tiled=True)
    return lax.psum(share, "row").astype(F32)


def local(
    tokens, latents, segment_ids, pad_mask, block_scene, out_grad,
    gain_cross_q, gain_cross_kv, w_cross_q, w_cross_kv, w_cross_out,
    gain_mlp1, w_up1, w_down1, gain_self, w_self_qkv, w_self_out, gain_mlp2, w_up2, w_down2,
):
    tokens, latents, og = tokens[0], latents[0], out_grad[0]
    rows, slots = latents.shape[0], tokens.shape[0] * lax.axis_size("lat")
    scenes = block_scene.shape[1]
    span = slots // scenes
    place = lax.axis_index("lat")
    group = LAT_SCENE // rows
    bits = group.bit_length() - 1

    gains = [gain_cross_q, gain_cross_kv, gain_mlp1, gain_self, gain_mlp2]
    first_weights = [[w_cross_kv, w_cross_q, w_cross_out], [w_up1], [w_down1], [w_self_qkv]]
    later_weights = [[w_up2], [w_down2], [w_self_out]]
    planes = lax.axis_size("row") == 4 and lax.axis_size("lat") == 8 and group == 2
    join = lambda gathered: [w.reshape(-1, w.shape[-1]) for w in gathered]
    if planes:
        notes = [segment_ids, pad_mask] + [g.reshape(1, -1) for g in gains]
        *weights, all_tokens, tags, gains = gather_now(Gather(first_weights, tokens, notes))
        mix, up1, down1, qkv, all_tokens = join([*weights, all_tokens])
    else:
        tag = jnp.where(pad_mask == 1, segment_ids, -1)
        tags = gather_lat(low(tag))
        all_tokens = gather_lat(tokens)
        gains = lax.all_gather(jnp.stack(gains), "lat", axis=1, tiled=True)
        gains = jnp.pad(gains.astype(F32), ((0, 3), (0, 0)))
        mix, up1, down1, qkv, up2, down2, so = (
            gather_lat(jnp.concatenate(shards, axis=1)) for shards in first_weights + later_weights
        )

    x1, x2, q, p, o, kv, q2, k2, v2, window, start = front(
        latents, all_tokens, tags, block_scene, span, gains, mix, up1, down1, qkv
    )
    if planes:
        o2, p2, scale2, k2_more, v2_more, *weights = self_forward(q2, (k2,), (v2,), Gather(later_weights))
        up2, down2, so = join(weights)
        keys, values = (k2, k2_more), (v2, v2_more)
    else:
        for bit in range(bits):
            upper = place // 2**bit % 2 == 1
            more = from_partner((k2, v2), bit)
            k2, v2 = (
                jnp.where(upper, jnp.concatenate([b, a]), jnp.concatenate([a, b]))
                for a, b in zip((k2, v2), more)
            )
        keys, values = (k2,), (v2,)
        o2, p2, scale2 = self_forward(q2, keys, values)
    out, g3, do2, dwup2, dwdown2, dwso, dgain_m2 = second(x2, o2, og, gains, so, up2, down2)
    comm = WeightSum([[dwup2], [dwdown2], [dwso]], direct=(0, 1, 2)) if planes else None
    dq2, dkv2, early = self_backward(q2, do2, o2, scale2, p2, keys, values, comm)
    if planes:
        dk, dv, dk_more, dv_more = dkv2
    else:
        dk, dk_more = halve(dkv2[0], place, bits)
        dv, dv_more = halve(dkv2[1], place, bits)
    g1, do, dwqkv, dwup1, dwdown1, dwout, dgain_s, dgain_m1 = middle_back(
        x2, g3, dq2, dk, dk_more, dv, dv_more, x1, o, gains, qkv, mix, up1, down1
    )
    if planes:
        comm = WeightSum(
            [[dwqkv], [dwup1], [dwdown1], [Staged(D, D), dwout], [Staged(D, 2 * D)]], gains=(8, D), tokens=slots,
            direct=(4,),
        )
        term, *late, dgains, token_grad = tail(
            comm, latents, do, p, q, kv, gains, mix, window, start, (dgain_m1, dgain_s, dgain_m2)
        )
        dgains = lax.dynamic_slice_in_dim(dgains, place * (D // 8), D // 8, axis=1)
        up2, down2, so, qkv, up1, down1, mixed, dwkv = join([*early, *late])
        latent_grad, token_grad, dwq, dwout, dwkv, *others = widen(
            g1, term, [token_grad, mixed, dwkv, up1, down1, qkv, so, up2, down2],
            ((D,), (D, D), (2 * D,), (FF,), (D,), (3 * D,), (D,), (FF,), (D,)),
        )
        sums = dwq, dwkv, dwout, *others
    else:
        latent_grad, dwq, dkv, dgain_q = cross_back(latents, g1, do, p, q, kv, gains, mix)
        mine, more = halve(dkv, place, bits)
        first = place % group * (span // group)
        token_rows = lax.dynamic_slice_in_dim(window, first, span // group)
        token_part, dwkv, dgain_kv = token_back(token_rows, mine, more, gains, mix)
        token_part = lax.dynamic_update_slice_in_dim(
            jnp.zeros((slots, D), BF16), token_part, start[0, 0] + first, 0
        )
        token_grad = lax.psum_scatter(token_part, "lat", scatter_dimension=0, tiled=True).astype(F32)
        dgains = jnp.stack([g[0] for g in (dgain_q, dgain_kv, dgain_m1, dgain_s, dgain_m2)])
        dgains = lax.psum_scatter(low(dgains), "lat", scatter_dimension=1, tiled=True)
        dgains = lax.psum(dgains, "row").astype(F32)
        sums = [
            reduce_weights(g) for g in (dwq, dwkv, dwout, dwup1, dwdown1, dwqkv, dwso, dwup2, dwdown2)
        ]
    dwq, dwkv, dwout, dwup1, dwdown1, dwqkv, dwso, dwup2, dwdown2 = sums
    return (
        out[None],
        latent_grad[None],
        token_grad[None],
        dgains[0],
        dgains[1],
        dwq,
        dwkv,
        dwout,
        dgains[2],
        dwup1,
        dwdown1,
        dgains[3],
        dwqkv,
        dwso,
        dgains[4],
        dwup2,
        dwdown2,
    )


def solution(mesh):
    by_row = P("row", "lat", None)
    weight = P("lat", None)
    gain = P("lat")
    parameters = (
        gain, gain, weight, weight, weight, gain, weight, weight, gain, weight, weight, gain,
        weight, weight,
    )
    return jax.shard_map(
        local,
        mesh=mesh,
        in_specs=(by_row, by_row, P("row", "lat"), P("row", "lat"), P("row", None), by_row)
        + parameters,
        out_specs=(by_row, by_row, by_row) + parameters,
        check_vma=False,
    )
```
